128 devices in a mesh: dp: 16 (over z, x), ep: 8 (over y, core).
Axes of the slice: x: 4, y: 4, z: 4, core: 2. Of those that a mesh axis runs over, the one named last changes fastest.
Arguments:
- cache_pool: bfloat16 [16384, 64, 576], P(('dp', 'ep')), may hold values from -6 to 6
- page_table: int32 [128, 64], replicated, may hold values from 0 to 16383, as said below
- page_counts: int32 [128, 4], P(('dp', 'ep')), may hold values from 1 to 32, 64 in all within a row
- queries: bfloat16 [2, 512, 64, 576], P(None, ('dp', 'ep')), may hold values from -60 to 60
- new_latent: bfloat16 [2, 512, 576], P(None, ('dp', 'ep')), may hold values from -6 to 6
- residual: bfloat16 [2, 512, 3584], P(None, ('dp', 'ep')), may hold values from -6 to 6
- w_uv: bfloat16 [64, 512, 128], P('ep'), may hold values from -4 to 4
- w_out: bfloat16 [8192, 3584], P('ep'), may hold values from -0.0625 to 0.0625
- norm_gain: float32 [3584], replicated, may hold values from 0.5 to 1.5
- w_router: float32 [3584, 16], replicated, may hold values from -0.09375 to 0.09375
- w_gate: bfloat16 [16, 3584, 2048], P('dp', None, 'ep'), may hold values from -0.09375 to 0.09375
- w_up: bfloat16 [16, 3584, 2048], P('dp', None, 'ep'), may hold values from -0.09375 to 0.09375
- w_down: bfloat16 [16, 2048, 3584], P('dp', 'ep'), may hold values from -0.125 to 0.125
- routes: int32 [2, 512, 8], P(None, ('dp', 'ep')), may hold values from 0 to 15, all different within a row; in each aligned block of 4 rows (0 to 3, 4 to 7, ..., all dimensions but the last counted through in order) at most 3 rows name the same one
Outputs:
- layer_out: bfloat16 [2, 512, 3584], P(None, ('dp', 'ep'))
The draws below stay inside these ranges and needn't reach their ends.
Inputs may be any that keep to these rules, and one draw needn't show every extreme that they name: `page_table`: row d lists, request after request of device d, the pool pages of its requests' cache; no pool page is listed twice; at most 1 entries of a row lie among one device's 128 pool pages, and every row reaches that. `page_counts`: each device's counts sum to exactly 64, and the largest is 32. `routes`: each row names 8 different experts; at each step, no expert is named by more than 3 of one device's 4 rows, and that is reached.
All inputs are finite; a program needn't handle non-finite values.
Results may differ from the reference program's by a relative error of at most 0.019.
Values may be sent and summed in bfloat16 or wider, within the bound.
A program may use at most 192 MiB of HBM per device.

```python
import math
import jax
import jax.numpy as jnp
import numpy as np
from jax import lax

D = 3584
HEADS = 64
LATENT = 512
ROPE = 64
VHEAD = 128
FF = 2048
TOP = 8
PAGE = 64
STEPS = 2
MAXPAGES = 32
ROWS_DEV = 4
PAGES_DEV = 64
EXPERTS = 16
CAP = 3
CAPP = 1
POOL = 16384
ROWS = 512
N_DP = 16
N_EP = 8
DEVICES = 128


def draw_page_table(key, part):
    key = jax.random.fold_in(key, 11)
    device_count = N_DP * N_EP
    pool_pages = CAPP * device_count
    owner_key, slot_key = jax.random.split(key)
    owner_order = jax.vmap(lambda subkey: jax.random.permutation(subkey, device_count))(jax.random.split(owner_key, device_count))
    slot_order = jax.vmap(lambda subkey: jax.random.permutation(subkey, pool_pages))(jax.random.split(slot_key, device_count))
    page_index = jnp.arange(PAGES_DEV)[None, :]
    destination = jnp.arange(device_count)[:, None]
    owner_of = owner_order[destination, page_index // CAPP]
    local_slot = slot_order[owner_of, destination * CAPP + page_index % CAPP]
    return (owner_of * pool_pages + local_slot).astype(jnp.int32)


def draw_queries(key, part):
    key = jax.random.fold_in(key, 7)
    full_shape = (STEPS, ROWS_DEV * N_DP * N_EP, HEADS, LATENT + ROPE)
    values = jnp.clip(jax.random.normal(key, full_shape, jnp.float32), -6.0, 6.0)
    return values.astype(jnp.bfloat16)


def level_of(own_key, dims, cuts, least, largest):
    factor_of, own = 1.0, jax.random.fold_in(own_key, 6)
    for position, parts in cuts:
        draws = jnp.exp(jax.random.uniform(jax.random.fold_in(own, position), (parts,), jnp.float32, least / len(cuts), largest / len(cuts)))
        factor_of = factor_of * jnp.repeat(draws, dims[position] // parts).reshape([-1 if axis == position else 1 for axis in range(len(dims))])
    return factor_of


def profile(number_of, total, bound, skew):
    weights = [(1 << 20) // math.isqrt(rank ** skew) + 1 for rank in range(2, number_of + 1)]
    rest, given = total - bound - (number_of - 1), [1] * (number_of - 1)
    while rest > 0:
        free = [i for i in range(number_of - 1) if given[i] < bound]
        mass, remaining = sum([weights[i] for i in free]), rest
        for i in free:
            extra = min(bound - given[i], max(1, remaining * weights[i] // mass), rest)
            given[i] = given[i] + extra
            rest = rest - extra
    return np.array([bound] + given)


def ragged(key, number_of, total, limit, lean):
    if number_of == 2:
        one = jax.random.randint(key, (), max(1, total - limit), min(limit, total - 1) + 1)
        return jnp.stack([one, total - one])
    lengths = jnp.asarray(profile(number_of, total, limit, lean), jnp.int32)
    pairs = (number_of - 1) // 2
    donor, taker = lengths[1:1 + 2 * pairs:2], lengths[2:2 + 2 * pairs:2]
    margin = jnp.minimum(donor - 1, limit - taker)
    moved = jax.random.randint(jax.random.fold_in(key, 1), (pairs,), 0, 1 << 20) % (margin + 1)
    lengths = lengths.at[1:1 + 2 * pairs:2].set(donor - moved).at[2:2 + 2 * pairs:2].set(taker + moved)
    return lengths[jax.random.permutation(jax.random.fold_in(key, 2), number_of)]


def deal_out(key, own, number, rows, count, top, limit, slope):
    order = jax.random.permutation(key, count)
    packed, ordinary = load_shares(count, rows * top, limit, slope, True), load_shares(count, rows * top, limit, slope, False)
    places = jnp.arange(count)

    def named(tallies, offset_by):
        used = int((tallies > 0).sum())
        fixed = max(1, used // 4)
        shifted = fixed + (places - fixed + offset_by * (used - fixed)) % max(1, count - fixed)
        return jnp.zeros((count,), jnp.int32).at[order[jnp.where(places < fixed, places, shifted)]].set(jnp.asarray(tallies, jnp.int32))

    tallies = jnp.where(number % 4 == 0, named(packed, number // 4), named(ordinary, number - number // 4 - 1))
    mixed = jax.random.permutation(jax.random.fold_in(own, 3), count)
    giver, receiver = mixed[0:count // 2 * 2:2], mixed[1:count // 2 * 2:2]
    slack = jnp.minimum(tallies[giver] - 1, limit - tallies[receiver]) // 2
    slack = jnp.where((giver == order[0]) | (receiver == order[0]) | (tallies[receiver] == 0), 0, jnp.maximum(slack, 0))
    shifted = jax.random.randint(jax.random.fold_in(own, 4), (count // 2,), 0, 1 << 20) % (slack + 1)
    tallies = tallies.at[giver].add(-shifted).at[receiver].add(shifted)
    labels = jnp.searchsorted(jnp.cumsum(tallies), jnp.arange(rows * top), side="right").astype(jnp.int32)
    table = labels.reshape(top, rows).T
    table = table[jax.random.permutation(jax.random.fold_in(own, 1), rows)]
    offset_by = jax.random.randint(jax.random.fold_in(own, 2), (rows, 1), 0, top)
    return jnp.take_along_axis(table, (jnp.arange(top)[None, :] + offset_by) % top, axis=1)


def load_shares(amount, total, reach, lean, full):
    weights = [(1 << 20) // math.isqrt(standing ** lean) + 1 for standing in range(1, amount + 1)]
    largest = reach if full else min(reach, max(-(-total // amount), total * weights[0] // sum(weights)))
    least = 1 if total - largest >= amount - 1 else 0
    holding, spare = [largest] + [least] * (amount - 1), total - largest - least * (amount - 1)
    while spare > 0:
        free = [i for i in range(1, amount) if holding[i] < largest] or [i for i in range(1, amount) if holding[i] < reach]
        pool, left = sum([weights[i] for i in free]), spare
        for i in free:
            more = min(reach - holding[i], max(1, left * weights[i] // pool), spare)
            holding[i] = holding[i] + more
            spare = spare - more
    return np.array(holding)


def bell_draw(key, dims, deviation, most, pieces=(), kind=jnp.bfloat16):
    values = deviation * jax.random.normal(key, dims, jnp.float32)
    if pieces:
        values = values * level_of(key, dims, pieces, -0.22, 0.18)
    return jnp.clip(values, -most, most).astype(kind)


def setup_inputs(seed: int = 0) -> dict:
    streams_of = jax.random.split(jax.random.key(seed), 15)
    cache_pool = bell_draw(streams_of[0], (POOL, PAGE, LATENT + ROPE), 1.0, 6.0, ((0, 128),))
    page_table = draw_page_table(jax.random.fold_in(streams_of[14], 71), 0)
    page_counts = jax.vmap(lambda own: ragged(own, ROWS_DEV, PAGES_DEV, MAXPAGES, 2))(jax.random.split(streams_of[2], DEVICES)).reshape((DEVICES, ROWS_DEV)).astype(jnp.int32)
    queries = draw_queries(jax.random.fold_in(streams_of[14], 71), 0)
    new_latent = bell_draw(streams_of[4], (STEPS, ROWS, LATENT + ROPE), 1.0, 6.0, ((1, 128),))
    residual = bell_draw(streams_of[5], (STEPS, ROWS, D), 1.0, 6.0, ((1, 128),))
    w_uv = bell_draw(streams_of[6], (HEADS, LATENT, VHEAD), (max(1, LATENT // 256)) ** -0.5, 4.0, ((0, 8),))
    w_out = bell_draw(streams_of[7], (HEADS * VHEAD, D), (HEADS * VHEAD) ** -0.5, 0.0625, ((0, 8),))
    norm_gain = jnp.clip(1.0 + 0.1 * jax.random.normal(streams_of[8], (D,), jnp.float32), 0.5, 1.5)
    w_router = bell_draw(streams_of[9], (D, EXPERTS), D ** -0.5, 0.09375, (), jnp.float32)
    w_gate = bell_draw(streams_of[10], (EXPERTS, D, FF), D ** -0.5, 0.09375, ((0, 16), (2, 8)))
    w_up = bell_draw(streams_of[11], (EXPERTS, D, FF), D ** -0.5, 0.09375, ((0, 16), (2, 8)))
    w_down = bell_draw(streams_of[12], (EXPERTS, FF, D), FF ** -0.5, 0.125, ((0, 16), (1, 8)))
    routes_keys = jax.random.split(jax.random.fold_in(streams_of[13], 1), STEPS * ROWS // ROWS_DEV)
    routes_turns = jax.random.permutation(jax.random.fold_in(streams_of[13], 3), STEPS * ROWS // ROWS_DEV)
    routes = jax.vmap(lambda own, number: deal_out(jax.random.fold_in(streams_of[13], 2), own, number, ROWS_DEV, EXPERTS, TOP, CAP, 2))(routes_keys, routes_turns).reshape((STEPS, ROWS, TOP))
    return {"cache_pool": cache_pool, "page_table": page_table, "page_counts": page_counts, "queries": queries, "new_latent": new_latent, "residual": residual, "w_uv": w_uv, "w_out": w_out, "norm_gain": norm_gain, "w_router": w_router, "w_gate": w_gate, "w_up": w_up, "w_down": w_down, "routes": routes}


score_scale = 192.0 ** (-0.5)
route_scale = 2.5
norm_eps = 1e-06
highest = lax.Precision.HIGHEST

def lower_round(values):
    return lax.optimization_barrier(values.astype(jnp.bfloat16)).astype(jnp.float32)

def attend_device(cache_pool, table_row, counts, query_block, latent_block):
    page_data = cache_pool[table_row].astype(jnp.float32)
    row_ends = jnp.cumsum(counts)
    page_index = jnp.arange(table_row.shape[0])
    row_of = lax.optimization_barrier(jnp.sum(page_index[:, None] >= row_ends[None, :], axis=1))
    member = row_of[None, :] == jnp.arange(counts.shape[0])[:, None]
    member_real = member.astype(jnp.float32)
    outputs = []
    for step_index in range(STEPS):
        queries_now = query_block[step_index].astype(jnp.float32)
        per_page = queries_now[row_of]
        scores = jnp.einsum('jhc,jtc->jht', per_page, page_data) * score_scale
        own_latent = latent_block[:step_index + 1].astype(jnp.float32)
        own_scores = jnp.einsum('rhc,src->rhs', queries_now, own_latent) * score_scale
        page_max = lax.optimization_barrier(jnp.max(scores, axis=2))
        row_max = lax.optimization_barrier(jnp.max(jnp.where(member[:, :, None], page_max[None, :, :], -jnp.inf), axis=1))
        row_max = jnp.maximum(row_max, lax.optimization_barrier(jnp.max(own_scores, axis=2)))
        weights = jnp.exp(scores - row_max[row_of][:, :, None])
        own_weights = jnp.exp(own_scores - row_max[:, :, None])
        total = jnp.dot(member_real, lax.optimization_barrier(jnp.sum(weights, axis=2)), precision=highest) + lax.optimization_barrier(jnp.sum(own_weights, axis=2))
        per_page_out = jnp.einsum('jht,jtc->jhc', lower_round(weights), page_data[:, :, :LATENT])
        gathered = jnp.einsum('rj,jhc->rhc', member_real, per_page_out, precision=highest)
        gathered = gathered + jnp.einsum('rhs,src->rhc', lower_round(own_weights), own_latent[:, :, :LATENT])
        outputs.append((gathered / total[:, :, None]).astype(jnp.bfloat16))
    return jnp.stack(outputs)

def reference(cache_pool, page_table, page_counts, queries, new_latent, residual, w_uv, w_out, norm_gain, w_router, w_gate, w_up, w_down, routes):

    def per_device(device_index):
        rows_start = device_index * ROWS_DEV
        query_block = lax.dynamic_slice_in_dim(queries, rows_start, ROWS_DEV, 1)
        latent_block = lax.dynamic_slice_in_dim(new_latent, rows_start, ROWS_DEV, 1)
        return attend_device(cache_pool, page_table[device_index], page_counts[device_index], query_block, latent_block)
    attended = lax.map(per_device, jnp.arange(N_DP * N_EP, dtype=jnp.int32))
    attended = jnp.transpose(attended, (1, 0, 2, 3, 4)).reshape(STEPS, ROWS, HEADS, LATENT)
    out_groups = w_out.reshape(N_EP, -1, D).astype(jnp.float32)
    outputs = []
    for step_index in range(STEPS):
        head_values = jnp.einsum('rhc,hcv->rhv', attended[step_index].astype(jnp.float32), w_uv.astype(jnp.float32)).astype(jnp.bfloat16)
        grouped = head_values.reshape(ROWS, N_EP, -1).astype(jnp.float32)
        partial_value = jnp.einsum('rgk,gkd->rgd', grouped, out_groups)
        attention_out = lax.optimization_barrier(jnp.sum(lower_round(partial_value), axis=1))
        hidden = residual[step_index].astype(jnp.float32) + attention_out
        normed = (hidden * lax.rsqrt(lax.optimization_barrier(jnp.mean(hidden * hidden, axis=-1, keepdims=True)) + norm_eps) * norm_gain).astype(jnp.bfloat16)
        affinity = jax.nn.sigmoid(jnp.dot(normed.astype(jnp.float32), w_router, precision=highest))
        chosen = jnp.take_along_axis(affinity, routes[step_index], axis=1)
        gate_weights = route_scale * chosen / lax.optimization_barrier(jnp.sum(chosen, axis=1, keepdims=True))
        combine = lax.optimization_barrier(jnp.sum(jnp.where(routes[step_index][:, :, None] == jnp.arange(EXPERTS)[None, None, :], gate_weights[:, :, None], 0.0), axis=1))

        def expert_step(running, expert):
            gate_w, up_w, down_w, column = expert
            gate_out = jnp.dot(normed, gate_w, preferred_element_type=jnp.float32)
            up_out = jnp.dot(normed, up_w, preferred_element_type=jnp.float32)
            inner_act = (jax.nn.silu(gate_out) * up_out).astype(jnp.bfloat16)
            shards = jnp.einsum('rgf,gfd->rgd', inner_act.reshape(ROWS, N_EP, -1).astype(jnp.float32), down_w.reshape(N_EP, -1, D).astype(jnp.float32))
            result = lax.optimization_barrier(jnp.sum(lower_round(shards), axis=1)).astype(jnp.bfloat16)
            return (running + column[:, None] * result.astype(jnp.float32), None)
        expert_mix, unused = lax.scan(expert_step, jnp.zeros((ROWS, D), jnp.float32), (w_gate, w_up, w_down, combine.T))
        outputs.append((hidden + expert_mix).astype(jnp.bfloat16))
    return jnp.stack(outputs)
```

```python
import functools

import jax
import jax.numpy as jnp
from jax import lax
from jax.experimental import pallas as pl
from jax.experimental.pallas import tpu as pltpu
from jax.sharding import PartitionSpec as P

MESH = pl.DeviceIdType.MESH
F32 = jnp.float32
BF16 = jnp.bfloat16

LATENT = 512
PAGE = 64
TILE = 8
score_scale = 192.0 ** (-0.5)
route_scale = 2.5
norm_eps = 1e-06

HALF = 1792
PART = 640
ORDERS = ((0, 1, 2), (1, 2, 0), (2, 0, 1))
WIDTHS = (640, 640, 512)


def attend_kernel(owner, starts, counts, q_ref, own_ref, slots, out_ref, keys, scores, sem):
    rows = 64 * PAGE

    def fetch(j, _):
        at = pl.multiple_of(j * PAGE, PAGE)
        pltpu.make_async_copy(slots.at[owner[j]], keys.at[pl.ds(at, PAGE)], sem).start()
        return 0

    lax.fori_loop(0, 64, fetch, 0)

    def clear(j, _):
        at = pl.multiple_of(rows + j * PAGE, PAGE)
        keys[pl.ds(at, PAGE), :] = jnp.zeros((PAGE, keys.shape[1]), BF16)
        return 0

    lax.fori_loop(0, TILE, clear, 0)
    filled = keys.at[pl.ds(0, rows)]
    pltpu.make_async_copy(filled, filled, sem).wait()
    width = TILE * PAGE
    step_of = lax.broadcasted_iota(jnp.int32, (128, 16), 0) // 64
    token = lax.broadcasted_iota(jnp.int32, (128, 16), 1)

    def request(r, _):
        q = jnp.concatenate([q_ref[0, r], q_ref[1, r]], axis=0)
        own = own_ref[r]
        s_own = lax.dot_general(q, own, (((1,), (1,)), ((), ())), preferred_element_type=F32)
        s_own = jnp.where(token <= step_of, s_own * score_scale, -jnp.inf)
        start = starts[r] * PAGE
        length = counts[r] * PAGE
        tiles = (length + width - 1) // width

        def score(t, top):
            at = pl.multiple_of(start + t * width, PAGE)
            s = lax.dot_general(
                q, keys[pl.ds(at, width), :], (((1,), (1,)), ((), ())), preferred_element_type=F32
            )
            place = t * width + lax.broadcasted_iota(jnp.int32, (128, width), 1)
            s = jnp.where(place < length, s * score_scale, -jnp.inf)
            scores[t] = s
            return jnp.maximum(top, jnp.max(s, axis=1, keepdims=True))

        top = lax.fori_loop(0, tiles, score, jnp.max(s_own, axis=1, keepdims=True))
        p_own = jnp.exp(s_own - top)
        total = jnp.sum(p_own, axis=1, keepdims=True)
        acc = jnp.dot(p_own.astype(BF16), own[:, :LATENT], preferred_element_type=F32)

        def mix(t, carry):
            total, acc = carry
            at = pl.multiple_of(start + t * width, PAGE)
            p = jnp.exp(scores[t] - top)
            total = total + jnp.sum(p, axis=1, keepdims=True)
            acc = acc + jnp.dot(
                p.astype(BF16), keys[pl.ds(at, width), :LATENT], preferred_element_type=F32
            )
            return total, acc

        total, acc = lax.fori_loop(0, tiles, mix, (total, acc))
        res = (acc / total).reshape(2, 8, 8, LATENT)
        at = pl.multiple_of(r * 16, 16)
        for g in range(8):
            block = jnp.concatenate([res[0, g], res[1, g]], axis=0)
            out_ref[g, pl.ds(at, 16), :] = block.astype(BF16)
        return 0

    lax.fori_loop(0, 4, request, 0)


def attend(owner, starts, counts, queries, own, slots):
    smem = pl.BlockSpec(memory_space=pltpu.SMEM)
    vmem = pl.BlockSpec(memory_space=pltpu.VMEM)
    return pl.pallas_call(
        attend_kernel,
        out_shape=jax.ShapeDtypeStruct((8, 64, LATENT), BF16),
        in_specs=[smem, smem, smem, vmem, vmem, pl.BlockSpec(memory_space=pl.ANY)],
        out_specs=vmem,
        scratch_shapes=[
            pltpu.VMEM(((64 + TILE) * PAGE, slots.shape[-1]), BF16),
            pltpu.VMEM((32 // TILE, 128, TILE * PAGE), F32),
            pltpu.SemaphoreType.DMA,
        ],
        compiler_params=pltpu.CompilerParams(vmem_limit_bytes=40 * 2**20),
        name="attend",
    )(owner, starts, counts, queries, own, slots)


def layer_kernel(
    attended, resid, member, gain, router, w_uv, w_out, w_gate, w_up, w_down,
    out_ref,
    heads_in, masked, part_out, part_in, res_all, mem_all, stat_out, stat_in, hidden,
    gath, v_uv, v_out, v_gate, v_up, v_down, inner,
    mix, sib_out, sib_in, t1, ul1, ur1, t2, ul2, ur2, last, fin_out, fin_in,
    wsem, lsem, head_s, head_r, part_s, part_r, pair_s, pair_r,
    ag_s, ag_r, sib_s, sib_r, red_s, red_r, sum_s, sum_r,
):
    dp = lax.axis_index("dp")
    ep = lax.axis_index("ep")
    pos = (dp // 4, dp % 4, ep // 2)
    core = ep % 2
    other = 1 - core

    def device(coords, c):
        return (coords[0] * 4 + coords[1], coords[2] * 2 + c)

    def along(axis, delta):
        coords = [pos[0], pos[1], pos[2]]
        coords[axis] = (coords[axis] + delta) % 4
        return device(coords, core)

    sibling = device(pos, other)
    ep_peers = [(dp, (ep + o) % 8) for o in range(1, 8)]
    ring_peers = [along(a, d) for a in (0, 1) for d in (1, 2, 3)]

    def remote(src, dst, ssem, rsem, peer):
        copy = pltpu.make_async_remote_copy(
            src_ref=src, dst_ref=dst, send_sem=ssem, recv_sem=rsem,
            device_id=peer, device_id_type=MESH,
        )
        copy.start()
        sent.append((src, ssem))

    def landed(ref, rsem):
        pltpu.make_async_copy(ref, ref, rsem).wait()

    sent = []

    loads = [(w_uv, v_uv), (w_out, v_out), (w_gate, v_gate), (w_up, v_up), (w_down, v_down)]
    copies = [pltpu.make_async_copy(a, b, wsem.at[i]) for i, (a, b) in enumerate(loads)]
    for copy in copies:
        copy.start()

    barrier = pltpu.get_barrier_semaphore()
    for peer in ep_peers + ring_peers:
        pl.semaphore_signal(barrier, inc=1, device_id=peer, device_id_type=MESH)
    pl.semaphore_wait(barrier, len(ep_peers) + len(ring_peers))

    for o in range(1, 8):
        to = (ep + o) % 8
        remote(attended.at[to], heads_in.at[ep], head_s.at[o], head_r.at[o], (dp, to))
    own_heads = pltpu.make_async_copy(attended.at[ep], heads_in.at[ep], lsem)
    own_heads.start()
    own_rows = pl.ds(pl.multiple_of(core * 8, 8), 8)
    other_rows = pl.ds(pl.multiple_of(other * 8, 8), 8)
    remote(resid.at[other], res_all.at[own_rows], pair_s.at[0], pair_r.at[0], sibling)
    remote(member, mem_all.at[own_rows], pair_s.at[1], pair_r.at[1], sibling)
    res_all[own_rows, :] = resid[core]
    mem_all[own_rows, :] = member[...]
    own_heads.wait()
    for o in range(1, 8):
        landed(heads_in.at[(ep + 8 - o) % 8], head_r.at[o])

    copies[0].wait()
    x = heads_in[...].reshape(512, LATENT)
    row_head = lax.broadcasted_iota(jnp.int32, (512, 128), 0) % 8
    for h in range(8):
        y = jnp.dot(x, v_uv[h], preferred_element_type=F32)
        masked[:, h * 128 : (h + 1) * 128] = jnp.where(row_head == h, y, 0.0).astype(BF16)
    to_row = lax.broadcasted_iota(jnp.int32, (64, 512), 0)
    from_row = lax.broadcasted_iota(jnp.int32, (64, 512), 1) // 8
    wanted = (to_row // 8) * 8 + (to_row % 4) * 2 + (to_row % 8) // 4
    pick = jnp.where(from_row == wanted, 1.0, 0.0).astype(BF16)
    flat = jnp.dot(pick, masked[...], preferred_element_type=F32).astype(BF16)

    copies[1].wait()
    for h in range(2):
        for t in range(HALF // 256):
            col = h * HALF + t * 256
            y = jnp.dot(flat, v_out[:, col : col + 256], preferred_element_type=F32)
            part_out[h, :, :, t * 256 : (t + 1) * 256] = y.astype(BF16).reshape(4, 16, 256)
    for o in range(1, 8):
        to = (ep + o) % 8
        remote(
            part_out.at[to % 2, to // 2], part_in.at[ep], part_s.at[o], part_r.at[o], (dp, to)
        )
    landed(res_all.at[other_rows], pair_r.at[0])
    landed(mem_all.at[other_rows], pair_r.at[1])
    hid = part_out[core, pos[2]].astype(F32)
    for o in range(1, 8):
        src = (ep + 8 - o) % 8
        landed(part_in.at[src], part_r.at[o])
        hid = hid + part_in[src].astype(F32)
    hid = hid + res_all[...]
    hidden[...] = hid

    half_cols = pl.ds(pl.multiple_of(core * HALF, 128), HALF)
    scaled = hid * gain[:, half_cols]
    stat_out[0] = lax.dot_general(
        scaled, router[:, half_cols], (((1,), (1,)), ((), ())),
        preferred_element_type=F32, precision=lax.Precision.HIGHEST,
    )
    stat_out[1] = jnp.broadcast_to(jnp.sum(hid * hid, axis=1, keepdims=True), (16, 128))
    remote(stat_out, stat_in, pair_s.at[2], pair_r.at[2], sibling)
    landed(stat_in, pair_r.at[2])
    square = stat_out[1] + stat_in[1]
    inv = lax.rsqrt(square / (2 * HALF) + norm_eps)
    affinity = jax.nn.sigmoid((stat_out[0] + stat_in[0]) * inv) * mem_all[...]
    gates = route_scale * affinity / jnp.sum(affinity, axis=1, keepdims=True)
    coarse = gates.astype(BF16)
    fine = (gates - coarse.astype(F32)).astype(BF16)
    normed = (scaled * inv[:, 0:1]).astype(BF16)
    z, xx, yy = pos
    gath[core, 0, z, xx, yy] = normed[:, 0:640]
    gath[core, 1, z, xx, yy] = normed[:, 640:1280]
    gath[core, 2, z, xx, yy, :, 0:512] = normed[:, 1280:1792]
    gath[core, 2, z, xx, yy, :, 512:640] = jnp.where(core == 0, coarse, fine)

    whole = pl.ds(0, 4)
    halves = (pl.ds(0, 2), pl.ds(2, 2))

    def g_at(cls, spec):
        return gath.at[core, cls, spec[0], spec[1], spec[2]]

    def spec_of(order, values):
        spec = [None, None, None]
        for axis, value in zip(order, values):
            spec[axis] = value
        return spec

    for cls, order in enumerate(ORDERS):
        own = g_at(cls, pos)
        for d in (1, 2, 3):
            remote(own, own, ag_s.at[cls, 0, d], ag_r.at[cls, 0, d], along(order[0], d))
    for cls, order in enumerate(ORDERS):
        a1, a2, a3 = order
        for d in (1, 2, 3):
            src = list(pos)
            src[a1] = (pos[a1] + 4 - d) % 4
            landed(g_at(cls, src), ag_r.at[cls, 0, d])
    for phase in (1, 2):

        def block(cls, shift, half):
            a1, a2, a3 = ORDERS[cls]
            if phase == 1:
                return g_at(cls, spec_of((a1, a2, a3), (half, (pos[a2] + shift) % 4, pos[a3])))
            return g_at(cls, spec_of((a1, a2, a3), (half, whole, (pos[a3] + shift) % 4)))

        for cls, order in enumerate(ORDERS):
            if phase == 2:
                plane = g_at(cls, spec_of(order, (whole, whole, pos[order[2]])))
                remote(plane, plane, sib_s.at[cls, 0], sib_r.at[cls, 0], sibling)
            axis = order[phase]
            for half, delta, k in ((0, 1, 0), (1, 3, 1), (1, 1, 2), (0, 3, 3)):
                b = block(cls, 0, halves[half])
                remote(b, b, ag_s.at[cls, phase, k], ag_r.at[cls, phase, k], along(axis, delta))
        for cls, order in enumerate(ORDERS):
            axis = order[phase]
            b = block(cls, 3, halves[0])
            landed(b, ag_r.at[cls, phase, 0])
            remote(b, b, ag_s.at[cls, phase, 4], ag_r.at[cls, phase, 4], along(axis, 1))
            b = block(cls, 1, halves[1])
            landed(b, ag_r.at[cls, phase, 1])
            remote(b, b, ag_s.at[cls, phase, 5], ag_r.at[cls, phase, 5], along(axis, 3))
        for cls, order in enumerate(ORDERS):
            landed(block(cls, 3, halves[1]), ag_r.at[cls, phase, 2])
            landed(block(cls, 1, halves[0]), ag_r.at[cls, phase, 3])
            if phase == 2:
                for k, shift in ((1, 3), (2, 1)):
                    plane = block(cls, shift, whole)
                    remote(plane, plane, sib_s.at[cls, k], sib_r.at[cls, k], sibling)
        for cls, order in enumerate(ORDERS):
            landed(block(cls, 2, halves[0]), ag_r.at[cls, phase, 4])
            landed(block(cls, 2, halves[1]), ag_r.at[cls, phase, 5])
            if phase == 2:
                plane = block(cls, 2, whole)
                remote(plane, plane, sib_s.at[cls, 3], sib_r.at[cls, 3], sibling)
    for cls, order in enumerate(ORDERS):
        a1, a2, a3 = order
        for k, shift in ((0, 0), (1, 3), (2, 1), (3, 2)):
            spec = spec_of(order, (whole, whole, (pos[a3] + shift) % 4))
            landed(gath.at[other, cls, spec[0], spec[1], spec[2]], sib_r.at[cls, k])

    for copy in copies[2:]:
        copy.wait()

    def expert_in(i, _):
        gate = jnp.zeros((256, 256), F32)
        up = jnp.zeros((256, 256), F32)
        for h in range(2):
            for cls in range(3):
                n = WIDTHS[cls]
                k0 = h * HALF + cls * PART
                rows_in = gath[h, cls, i].reshape(256, PART)[:, :n]
                gate = gate + jnp.dot(rows_in, v_gate[0, k0 : k0 + n, :], preferred_element_type=F32)
                up = up + jnp.dot(rows_in, v_up[0, k0 : k0 + n, :], preferred_element_type=F32)
        act = gate / (1.0 + jnp.exp(-gate)) * up
        at = pl.multiple_of(i * 256, 256)
        inner[pl.ds(at, 256), :] = act.astype(BF16)
        return 0

    lax.fori_loop(0, 4, expert_in, 0)
    lane = lax.broadcasted_iota(jnp.int32, (256, 128), 1)

    def expert_out(i, half, dest):
        at = pl.multiple_of(i * 256, 256)
        weights = gath[0, 2, i, :, :, :, 512:640].astype(F32) + gath[1, 2, i, :, :, :, 512:640].astype(F32)
        weight = jnp.sum(
            jnp.where(lane == dp, weights.reshape(256, 128), 0.0), axis=1, keepdims=True
        )
        act = inner[pl.ds(at, 256), :]
        for cls in range(3):
            n = WIDTHS[cls]
            cols = pl.ds(pl.multiple_of(half * HALF + cls * PART, 128), n)
            y = jnp.dot(act, v_down[0, :, cols], preferred_element_type=F32) * weight
            dest[cls, i, :, :, :, 0:n] = y.astype(BF16).reshape(4, 4, 16, n)

    def to_sibling(i, _):
        expert_out(i, other, sib_out)
        return 0

    lax.fori_loop(0, 4, to_sibling, 0)
    remote(sib_out, sib_in, red_s.at[0], red_r.at[0], sibling)

    def to_self(i, _):
        expert_out(i, core, mix)
        return 0

    lax.fori_loop(0, 4, to_self, 0)
    landed(sib_in, red_r.at[0])

    def add_sibling(i, _):
        for cls in range(3):
            n = WIDTHS[cls]
            total = mix[cls, i, :, :, :, 0:n].astype(F32) + sib_in[cls, i, :, :, :, 0:n].astype(F32)
            mix[cls, i, :, :, :, 0:n] = total.astype(BF16)
        return 0

    lax.fori_loop(0, 4, add_sibling, 0)

    def cut(ref, n):
        return ref.at[..., pl.ds(0, n)]

    for phase in (2, 1):
        bt, bl, br = (t1, ul1, ur1) if phase == 2 else (t2, ul2, ur2)
        red = 0 if phase == 2 else 1

        def block(cls, shift, half):
            a1, a2, a3 = ORDERS[cls]
            if phase == 1:
                spec = spec_of((a1, a2, a3), (half, (pos[a2] + shift) % 4, pos[a3]))
            else:
                spec = spec_of((a1, a2, a3), (half, whole, (pos[a3] + shift) % 4))
            return (cls, spec[0], spec[1], spec[2], slice(None), pl.ds(0, WIDTHS[cls]))

        def temp(cls, half):
            a1, a2, a3 = ORDERS[cls]
            if phase == 1:
                return (cls, half, slice(None), pl.ds(0, WIDTHS[cls]))
            if a1 < a2:
                return (cls, half, whole, slice(None), pl.ds(0, WIDTHS[cls]))
            return (cls, whole, half, slice(None), pl.ds(0, WIDTHS[cls]))

        def send(cls, shift, half, buf, k, delta):
            remote(
                mix.at[block(cls, shift, halves[half])], buf.at[temp(cls, halves[half])],
                sum_s.at[cls, red, k], sum_r.at[cls, red, k], along(ORDERS[cls][phase], delta),
            )

        for cls in range(3):
            send(cls, 2, 0, bt, 0, 1)
            send(cls, 2, 1, bt, 1, 3)
            send(cls, 1, 1, bl, 2, 1)
            send(cls, 3, 0, br, 3, 3)
        for cls in range(3):
            for half, shift, buf, k, delta in ((0, 1, bl, 0, 1), (1, 3, br, 1, 3)):
                at, tmp = block(cls, shift, halves[half]), temp(cls, halves[half])
                landed(bt.at[tmp], sum_r.at[cls, red, k])
                mix[at] = (mix[at].astype(F32) + bt[tmp].astype(F32)).astype(BF16)
                send(cls, shift, half, buf, k + 4, delta)
        for cls in range(3):
            for half, ks in ((0, (4, 3)), (1, (2, 5))):
                at, tmp = block(cls, 0, halves[half]), temp(cls, halves[half])
                landed(bl.at[tmp], sum_r.at[cls, red, ks[0]])
                landed(br.at[tmp], sum_r.at[cls, red, ks[1]])
                total = mix[at].astype(F32) + bl[tmp].astype(F32) + br[tmp].astype(F32)
                mix[at] = total.astype(BF16)

    for cls, order in enumerate(ORDERS):
        a1 = order[0]
        for d in (1, 2, 3):
            coords = list(pos)
            coords[a1] = (pos[a1] + d) % 4
            src = mix.at[cls, coords[0], coords[1], coords[2], :, pl.ds(0, WIDTHS[cls])]
            dst = last.at[cls, d - 1, :, pl.ds(0, WIDTHS[cls])]
            remote(src, dst, sum_s.at[cls, 2, d], sum_r.at[cls, 2, d], along(a1, d))
    for cls in range(3):
        n = WIDTHS[cls]
        total = mix[cls, pos[0], pos[1], pos[2], :, 0:n].astype(F32)
        for d in (1, 2, 3):
            landed(last.at[cls, d - 1, :, pl.ds(0, n)], sum_r.at[cls, 2, d])
            total = total + last[cls, d - 1, :, 0:n].astype(F32)
        total = total + hidden[:, cls * PART : cls * PART + n]
        fin_out[0, :, cls * PART : cls * PART + n] = total[0:8]
        fin_out[1, :, cls * PART : cls * PART + n] = total[8:16]
    remote(fin_out.at[other], fin_in, pair_s.at[3], pair_r.at[3], sibling)
    out_ref[:, half_cols] = fin_out[core].astype(BF16)
    landed(fin_in, pair_r.at[3])
    out_ref[:, pl.ds(pl.multiple_of(other * HALF, 128), HALF)] = fin_in[...].astype(BF16)
    for src, ssem in sent:
        pltpu.make_async_copy(src, src, ssem).wait()


def layer(attended, resid, member, gain, router, w_uv, w_out, w_gate, w_up, w_down):
    vmem = pl.BlockSpec(memory_space=pltpu.VMEM)
    hbm = pl.BlockSpec(memory_space=pl.ANY)
    dma = pltpu.SemaphoreType.DMA
    grid = (3, 4, 4, 4, 16, PART)
    return pl.pallas_call(
        layer_kernel,
        out_shape=jax.ShapeDtypeStruct((8, 2 * HALF), BF16),
        in_specs=[vmem] * 5 + [hbm] * 5,
        out_specs=vmem,
        scratch_shapes=[
            pltpu.VMEM((8, 64, LATENT), BF16),
            pltpu.VMEM((512, 1024), BF16),
            pltpu.VMEM((2, 4, 16, HALF), BF16),
            pltpu.VMEM((8, 16, HALF), BF16),
            pltpu.VMEM((16, HALF), F32),
            pltpu.VMEM((16, 128), F32),
            pltpu.VMEM((2, 16, 128), F32),
            pltpu.VMEM((2, 16, 128), F32),
            pltpu.VMEM((16, HALF), F32),
            pltpu.VMEM((2,) + grid, BF16),
            pltpu.VMEM(w_uv.shape, BF16),
            pltpu.VMEM(w_out.shape, BF16),
            pltpu.VMEM(w_gate.shape, BF16),
            pltpu.VMEM(w_up.shape, BF16),
            pltpu.VMEM(w_down.shape, BF16),
            pltpu.VMEM((1024, 256), BF16),
            pltpu.VMEM(grid, BF16),
            pltpu.VMEM(grid, BF16),
            pltpu.VMEM(grid, BF16),
            pltpu.VMEM((3, 4, 4, 16, PART), BF16),
            pltpu.VMEM((3, 4, 4, 16, PART), BF16),
            pltpu.VMEM((3, 4, 4, 16, PART), BF16),
            pltpu.VMEM((3, 4, 16, PART), BF16),
            pltpu.VMEM((3, 4, 16, PART), BF16),
            pltpu.VMEM((3, 4, 16, PART), BF16),
            pltpu.VMEM((3, 3, 16, PART), BF16),
            pltpu.VMEM((2, 8, HALF), F32),
            pltpu.VMEM((8, HALF), F32),
            dma((5,)), dma, dma((8,)), dma((8,)), dma((8,)), dma((8,)), dma((4,)), dma((4,)),
            dma((3, 3, 6)), dma((3, 3, 6)), dma((3, 4)), dma((3, 4)), dma((1,)), dma((1,)),
            dma((3, 3, 6)), dma((3, 3, 6)),
        ],
        compiler_params=pltpu.CompilerParams(
            collective_id=1, has_side_effects=True, vmem_limit_bytes=56 * 2**20
        ),
        name="layer",
    )(attended, resid, member, gain, router, w_uv, w_out, w_gate, w_up, w_down)


def shards(
    cache_pool,
    page_table,
    page_counts,
    queries,
    new_latent,
    residual,
    w_uv,
    w_out,
    norm_gain,
    w_router,
    w_gate,
    w_up,
    w_down,
    routes,
):
    ep_size = lax.axis_size("ep")
    my_index = lax.axis_index("dp") * ep_size + lax.axis_index("ep")
    pool_dev = cache_pool.shape[0]
    owner_all = page_table // pool_dev
    local_all = page_table % pool_dev
    source = jnp.sum(jnp.where(owner_all == my_index, local_all, 0), axis=1)
    outgoing = cache_pool[source]
    incoming = lax.all_to_all(outgoing, ("dp", "ep"), split_axis=0, concat_axis=0, tiled=True)
    owner = lax.dynamic_index_in_dim(owner_all, my_index, 0, keepdims=False)
    counts = page_counts[0]
    starts = jnp.cumsum(counts) - counts
    own = jnp.pad(jnp.transpose(new_latent, (1, 0, 2)), ((0, 0), (0, 14), (0, 0)))
    attended = attend(owner, starts, counts, queries, own, incoming)

    d_model = residual.shape[2]
    resid = residual.reshape(8, 2, d_model // 2).transpose(1, 0, 2).astype(F32)
    experts = w_router.shape[1]
    member = jnp.any(routes.reshape(8, -1)[:, :, None] == jnp.arange(128)[None, None, :], axis=1)
    router = jnp.pad(w_router.T, ((0, 128 - experts), (0, 0)))
    out = layer(
        attended, resid, member.astype(F32), norm_gain.reshape(1, -1), router,
        w_uv, w_out, w_gate, w_up, w_down,
    )
    return out.reshape(residual.shape)


def solution(mesh):
    return jax.shard_map(
        shards,
        mesh=mesh,
        in_specs=(
            P(("dp", "ep"), None, None),
            P(),
            P(("dp", "ep"), None),
            P(None, ("dp", "ep"), None, None),
            P(None, ("dp", "ep"), None),
            P(None, ("dp", "ep"), None),
            P("ep", None, None),
            P("ep", None),
            P(),
            P(),
            P("dp", None, "ep"),
            P("dp", None, "ep"),
            P("dp", "ep", None),
            P(None, ("dp", "ep"), None),
        ),
        out_specs=P(None, ("dp", "ep"), None),
        check_vma=False,
    )
```

```python
import functools

import jax
import jax.numpy as jnp
from jax import lax
from jax.experimental import pallas as pl
from jax.experimental.pallas import tpu as pltpu
from jax.sharding import PartitionSpec as P

MESH = pl.DeviceIdType.MESH
F32 = jnp.float32
BF16 = jnp.bfloat16

LATENT = 512
ROPE = 64
PAGE = 64
TILE = 8
score_scale = 192.0 ** (-0.5)
route_scale = 2.5
norm_eps = 1e-06

HALF = 1792
PART = 640
ORDERS = ((0, 1, 2), (1, 2, 0), (2, 0, 1))
WIDTHS = (640, 640, 512)


def exchange_kernel(
    source, pool, out,
    pool_v, slots, held1, held2, stage,
    psem, lsem, csem, send1, recv1, send2, recv2, send3, recv3,
):
    dp = lax.axis_index("dp")
    ep = lax.axis_index("ep")
    pos = (dp // 4, dp % 4, ep // 2)
    core = ep % 2
    other = 1 - core
    whole = pl.ds(0, 4)

    loads = [
        pltpu.make_async_copy(
            pool.at[pl.ds(i * 16, 16)], pool_v.at[pl.ds(i * 16, 16)], psem.at[i]
        )
        for i in range(4)
    ]
    for load in loads:
        load.start()

    def along(axis, delta, c):
        coords = list(pos)
        coords[axis] = (coords[axis] + delta) % 4
        return (coords[0] * 4 + coords[1], coords[2] * 2 + c)

    def spec_of(order, values):
        spec = [None, None, None]
        for axis, value in zip(order, values):
            spec[axis] = value
        return tuple(spec)

    barrier = pltpu.get_barrier_semaphore()
    peers = [along(a, d, c) for a in range(3) for d in (1, 2, 3) for c in (core, other)]
    peers.append(along(0, 0, other))
    for peer in peers:
        pl.semaphore_signal(barrier, inc=1, device_id=peer, device_id_type=MESH)

    lane = lax.broadcasted_iota(jnp.int32, (128, 128), 1)
    onehot = jnp.where(source[...] == lane, 1.0, 0.0).astype(BF16)

    def put(cls, row, pieces):
        for j in range(0, 16, 4):
            x = jnp.concatenate(pieces(j), axis=0)
            y = lax.dot_general(onehot, x, (((1,), (1,)), ((), ())), preferred_element_type=F32)
            for i in range(4):
                stage[:, j + i, :] = y[:, i * 128 : (i + 1) * 128]
        at = pl.multiple_of(row, 16)
        block = stage[...].astype(BF16).reshape(4, 4, 4, 2, 16, 128)
        slots[cls, :, :, :, :, pl.ds(at, 16), :] = block

    def latent_rows(cls, chunk, first, count, row):
        def unit(u, _):
            def pieces(j):
                t = (first + u) * 16 + j
                return [pool_v[pl.ds(t, 4), chunk * 128 : (chunk + 1) * 128, :].reshape(512, 128)]

            put(cls, row + u * 16, pieces)
            return 0

        lax.fori_loop(0, count, unit, 0)

    def rope_rows(cls, row):
        def unit(u, _):
            def pieces(j):
                found = []
                for i in range(4):
                    found.append(pool_v[u * 16 + j + i, 512:576, :])
                    found.append(pool_v[32 + u * 16 + j + i, 512:576, :])
                return found

            put(cls, row + u * 16, pieces)
            return 0

        lax.fori_loop(0, 2, unit, 0)

    sends = []

    def remote(src, dst, ssem, rsem, peer):
        pltpu.make_async_remote_copy(
            src_ref=src, dst_ref=dst, send_sem=ssem, recv_sem=rsem,
            device_id=peer, device_id_type=MESH,
        ).start()
        sends.append((src, ssem))

    def landed(ref, sem):
        pltpu.make_async_copy(ref, ref, sem).wait()

    for load in loads:
        load.wait()
    for cls, order in enumerate(ORDERS):
        a1, a2, a3 = order
        latent_rows(cls, cls, 0, 4, 0)
        if cls < 2:
            latent_rows(cls, 3, 2 * cls, 2, 64)
        else:
            rope_rows(cls, 64)
        if cls == 0:
            pl.semaphore_wait(barrier, len(peers))
        for d in (1, 2, 3):
            src = spec_of(order, ((pos[a1] + d) % 4, whole, whole))
            dst = spec_of(order, (pos[a1], whole, whole))
            remote(
                slots.at[(cls,) + src], held1.at[(cls,) + dst],
                send1.at[cls, d], recv1.at[cls, d], along(a1, d, core),
            )
        own = spec_of(order, (pos[a1], whole, whole))
        pltpu.make_async_copy(slots.at[(cls,) + own], held1.at[(cls,) + own], lsem.at[cls]).start()

    def second(cls, buf, e):
        a1, a2, a3 = order = ORDERS[cls]
        src1 = (pos[a1] + 4 - e) % 4
        for d in (1, 2, 3):
            src = spec_of(order, (src1, (pos[a2] + d) % 4, whole))
            dst = spec_of(order, (src1, pos[a2], whole))
            remote(
                buf.at[(cls,) + src], held2.at[(cls,) + dst],
                send2.at[cls, d, e], recv2.at[cls, d, e], along(a2, d, core),
            )

    def third(cls, buf, f):
        a1, a2, a3 = order = ORDERS[cls]
        src2 = (pos[a2] + 4 - f) % 4
        for d in (1, 2, 3, 0):
            for k, c in ((0, core), (1, other)):
                src = spec_of(order, (whole, src2, (pos[a3] + d) % 4))
                dst = spec_of(order, (whole, src2, pos[a3]))
                a = buf.at[(cls,) + src + (c,)]
                b = out.at[dst + (core, cls)]
                if d == 0 and k == 0:
                    pltpu.make_async_copy(a, b, csem.at[cls, f]).start()
                else:
                    remote(a, b, send3.at[cls, f, d, k], recv3.at[cls, f, d, k], along(a3, d, c))

    for cls in range(3):
        second(cls, slots, 0)
    for e in (1, 3, 2):
        for cls, order in enumerate(ORDERS):
            src1 = (pos[order[0]] + 4 - e) % 4
            at = spec_of(order, (src1, whole, whole))
            landed(held1.at[(cls,) + at], recv1.at[cls, e])
            second(cls, held1, e)
    for cls, order in enumerate(ORDERS):
        own = spec_of(order, (pos[order[0]], whole, whole))
        landed(held1.at[(cls,) + own], lsem.at[cls])
        third(cls, held1, 0)
    for f in (1, 3, 2):
        for cls, order in enumerate(ORDERS):
            a1, a2, a3 = order
            for e in range(4):
                at = spec_of(order, ((pos[a1] + 4 - e) % 4, (pos[a2] + 4 - f) % 4, whole))
                landed(held2.at[(cls,) + at], recv2.at[cls, f, e])
            third(cls, held2, f)
    for cls, order in enumerate(ORDERS):
        a1, a2, a3 = order
        for f in range(4):
            for d in range(4):
                for k, c in ((0, core), (1, other)):
                    at = spec_of(order, (whole, (pos[a2] + 4 - f) % 4, (pos[a3] + 4 - d) % 4))
                    ref = out.at[at + (c, cls)]
                    landed(ref, csem.at[cls, f] if d == 0 and k == 0 else recv3.at[cls, f, d, k])
    for src, ssem in sends:
        landed(src, ssem)


def exchange(source, pool):
    vmem = pl.BlockSpec(memory_space=pltpu.VMEM)
    hbm = pl.BlockSpec(memory_space=pl.ANY)
    dma = pltpu.SemaphoreType.DMA
    held = (3, 4, 4, 4, 2, 96, 128)
    return pl.pallas_call(
        exchange_kernel,
        out_shape=jax.ShapeDtypeStruct((4, 4, 4, 2, 3, 96, 128), BF16),
        in_specs=[vmem, hbm],
        out_specs=hbm,
        scratch_shapes=[
            pltpu.VMEM(pool.shape, BF16),
            pltpu.VMEM(held, BF16),
            pltpu.VMEM(held, BF16),
            pltpu.VMEM(held, BF16),
            pltpu.VMEM((128, 16, 128), F32),
            dma((4,)), dma((3,)), dma((3, 4)), dma((3, 4)), dma((3, 4)), dma((3, 4, 4)),
            dma((3, 4, 4)), dma((3, 4, 4, 2)), dma((3, 4, 4, 2)),
        ],
        compiler_params=pltpu.CompilerParams(
            collective_id=2, has_side_effects=True, vmem_limit_bytes=56 * 2**20
        ),
        name="exchange",
    )(source, pool)


def attend_kernel(
    owner, starts, counts, q_ref, own_ref, slots, out_ref, keys, last, ropes, scores, sem
):
    pages = 64

    def fetch(j, _):
        at = pl.multiple_of(j * PAGE, PAGE)
        slot = slots.at[owner[j]]
        pltpu.make_async_copy(
            slot.at[:, pl.ds(0, 64), :], keys.at[:, pl.ds(at, PAGE), :], sem.at[0]
        ).start()
        pltpu.make_async_copy(
            slot.at[pl.ds(0, 2), pl.ds(64, 32), :], last.at[j], sem.at[1]
        ).start()
        pltpu.make_async_copy(slot.at[2, pl.ds(64, 32), :], ropes.at[j], sem.at[2]).start()
        return 0

    lax.fori_loop(0, pages, fetch, 0)

    def clear(j, _):
        at = pl.multiple_of((pages + j) * PAGE, PAGE)
        keys[:, pl.ds(at, PAGE), :] = jnp.zeros((3, PAGE, 128), BF16)
        last[pages + j] = jnp.zeros((2, 32, 128), BF16)
        ropes[pages + j] = jnp.zeros((32, 128), BF16)
        return 0

    lax.fori_loop(0, TILE, clear, 0)
    for k, ref in enumerate(
        (keys.at[:, pl.ds(0, pages * PAGE), :], last.at[pl.ds(0, pages)], ropes.at[pl.ds(0, pages)])
    ):
        pltpu.make_async_copy(ref, ref, sem.at[k]).wait()
    width = TILE * PAGE
    step_of = lax.broadcasted_iota(jnp.int32, (128, 16), 0) // 64
    token = lax.broadcasted_iota(jnp.int32, (128, 16), 1)
    low = lax.broadcasted_iota(jnp.int32, (TILE, 32, 128), 2) < ROPE

    def values_of(page):
        at = pl.multiple_of(page * PAGE, PAGE)
        parts = [keys[k, pl.ds(at, width), :] for k in range(3)]
        parts.append(last[pl.ds(page, TILE)].reshape(width, 128))
        return jnp.concatenate(parts, axis=1)

    def request(r, _):
        q = jnp.concatenate([q_ref[0, r], q_ref[1, r]], axis=0)
        own = own_ref[r]
        s_own = lax.dot_general(q, own, (((1,), (1,)), ((), ())), preferred_element_type=F32)
        s_own = jnp.where(token <= step_of, s_own * score_scale, -jnp.inf)
        q_rope = q[:, LATENT:]
        q_wide = jnp.concatenate([q[:, :LATENT], q_rope, q_rope], axis=1)
        start = starts[r]
        length = counts[r] * PAGE
        tiles = (length + width - 1) // width

        def score(t, top):
            page = start + t * TILE
            rope = ropes[pl.ds(page, TILE)]
            zero = jnp.zeros_like(rope)
            pair = jnp.concatenate([jnp.where(low, rope, zero), jnp.where(low, zero, rope)], axis=1)
            key = jnp.concatenate([values_of(page), pair.reshape(width, 128)], axis=1)
            s = lax.dot_general(q_wide, key, (((1,), (1,)), ((), ())), preferred_element_type=F32)
            place = t * width + lax.broadcasted_iota(jnp.int32, (128, width), 1)
            s = jnp.where(place < length, s * score_scale, -jnp.inf)
            scores[t] = s
            return jnp.maximum(top, jnp.max(s, axis=1, keepdims=True))

        top = lax.fori_loop(0, tiles, score, jnp.max(s_own, axis=1, keepdims=True))
        p_own = jnp.exp(s_own - top)
        total = jnp.sum(p_own, axis=1, keepdims=True)
        acc = jnp.dot(p_own.astype(BF16), own[:, :LATENT], preferred_element_type=F32)

        def mix(t, carry):
            total, acc = carry
            p = jnp.exp(scores[t] - top)
            total = total + jnp.sum(p, axis=1, keepdims=True)
            acc = acc + jnp.dot(
                p.astype(BF16), values_of(start + t * TILE), preferred_element_type=F32
            )
            return total, acc

        total, acc = lax.fori_loop(0, tiles, mix, (total, acc))
        res = (acc / total).reshape(2, 8, 8, LATENT)
        at = pl.multiple_of(r * 16, 16)
        for g in range(8):
            block = jnp.concatenate([res[0, g], res[1, g]], axis=0)
            out_ref[g, pl.ds(at, 16), :] = block.astype(BF16)
        return 0

    lax.fori_loop(0, 4, request, 0)


def attend(owner, starts, counts, queries, own, slots):
    smem = pl.BlockSpec(memory_space=pltpu.SMEM)
    vmem = pl.BlockSpec(memory_space=pltpu.VMEM)
    return pl.pallas_call(
        attend_kernel,
        out_shape=jax.ShapeDtypeStruct((8, 64, LATENT), BF16),
        in_specs=[smem, smem, smem, vmem, vmem, pl.BlockSpec(memory_space=pl.ANY)],
        out_specs=vmem,
        scratch_shapes=[
            pltpu.VMEM((3, (64 + TILE) * PAGE, 128), BF16),
            pltpu.VMEM((64 + TILE, 2, 32, 128), BF16),
            pltpu.VMEM((64 + TILE, 32, 128), BF16),
            pltpu.VMEM((32 // TILE, 128, TILE * PAGE), F32),
            pltpu.SemaphoreType.DMA((3,)),
        ],
        compiler_params=pltpu.CompilerParams(vmem_limit_bytes=40 * 2**20),
        name="attend",
    )(owner, starts, counts, queries, own, slots)


def layer_kernel(
    attended, resid, member, gain, router, w_uv, w_out, w_gate, w_up, w_down,
    out_ref,
    heads_in, masked, part_out, part_in, res_all, mem_all, stat_out, stat_in, hidden,
    gath, v_uv, v_out, v_gate, v_up, v_down, inner,
    mix, sib_out, sib_in, t1, ul1, ur1, t2, ul2, ur2, last, fin_out, fin_in,
    wsem, lsem, head_s, head_r, part_s, part_r, pair_s, pair_r,
    ag_s, ag_r, sib_s, sib_r, red_s, red_r, sum_s, sum_r,
):
    dp = lax.axis_index("dp")
    ep = lax.axis_index("ep")
    pos = (dp // 4, dp % 4, ep // 2)
    core = ep % 2
    other = 1 - core

    def device(coords, c):
        return (coords[0] * 4 + coords[1], coords[2] * 2 + c)

    def along(axis, delta):
        coords = [pos[0], pos[1], pos[2]]
        coords[axis] = (coords[axis] + delta) % 4
        return device(coords, core)

    sibling = device(pos, other)
    ep_peers = [(dp, (ep + o) % 8) for o in range(1, 8)]
    ring_peers = [along(a, d) for a in (0, 1) for d in (1, 2, 3)]

    def remote(src, dst, ssem, rsem, peer):
        copy = pltpu.make_async_remote_copy(
            src_ref=src, dst_ref=dst, send_sem=ssem, recv_sem=rsem,
            device_id=peer, device_id_type=MESH,
        )
        copy.start()
        sent.append((src, ssem))

    def landed(ref, rsem):
        pltpu.make_async_copy(ref, ref, rsem).wait()

    sent = []

    loads = [(w_uv, v_uv), (w_out, v_out), (w_gate, v_gate), (w_up, v_up), (w_down, v_down)]
    copies = [pltpu.make_async_copy(a, b, wsem.at[i]) for i, (a, b) in enumerate(loads)]
    for copy in copies:
        copy.start()

    barrier = pltpu.get_barrier_semaphore()
    for peer in ep_peers + ring_peers:
        pl.semaphore_signal(barrier, inc=1, device_id=peer, device_id_type=MESH)
    pl.semaphore_wait(barrier, len(ep_peers) + len(ring_peers))

    for o in range(1, 8):
        to = (ep + o) % 8
        remote(attended.at[to], heads_in.at[ep], head_s.at[o], head_r.at[o], (dp, to))
    own_heads = pltpu.make_async_copy(attended.at[ep], heads_in.at[ep], lsem)
    own_heads.start()
    own_rows = pl.ds(pl.multiple_of(core * 8, 8), 8)
    other_rows = pl.ds(pl.multiple_of(other * 8, 8), 8)
    remote(resid.at[other], res_all.at[own_rows], pair_s.at[0], pair_r.at[0], sibling)
    remote(member, mem_all.at[own_rows], pair_s.at[1], pair_r.at[1], sibling)
    res_all[own_rows, :] = resid[core]
    mem_all[own_rows, :] = member[...]
    own_heads.wait()
    for o in range(1, 8):
        landed(heads_in.at[(ep + 8 - o) % 8], head_r.at[o])

    copies[0].wait()
    x = heads_in[...].reshape(512, LATENT)
    row_head = lax.broadcasted_iota(jnp.int32, (512, 128), 0) % 8
    for h in range(8):
        y = jnp.dot(x, v_uv[h], preferred_element_type=F32)
        masked[:, h * 128 : (h + 1) * 128] = jnp.where(row_head == h, y, 0.0).astype(BF16)
    to_row = lax.broadcasted_iota(jnp.int32, (64, 512), 0)
    from_row = lax.broadcasted_iota(jnp.int32, (64, 512), 1) // 8
    wanted = (to_row // 8) * 8 + (to_row % 4) * 2 + (to_row % 8) // 4
    pick = jnp.where(from_row == wanted, 1.0, 0.0).astype(BF16)
    flat = jnp.dot(pick, masked[...], preferred_element_type=F32).astype(BF16)

    copies[1].wait()
    for h in range(2):
        for t in range(HALF // 256):
            col = h * HALF + t * 256
            y = jnp.dot(flat, v_out[:, col : col + 256], preferred_element_type=F32)
            part_out[h, :, :, t * 256 : (t + 1) * 256] = y.astype(BF16).reshape(4, 16, 256)
    for o in range(1, 8):
        to = (ep + o) % 8
        remote(
            part_out.at[to % 2, to // 2], part_in.at[ep], part_s.at[o], part_r.at[o], (dp, to)
        )
    landed(res_all.at[other_rows], pair_r.at[0])
    landed(mem_all.at[other_rows], pair_r.at[1])
    hid = part_out[core, pos[2]].astype(F32)
    for o in range(1, 8):
        src = (ep + 8 - o) % 8
        landed(part_in.at[src], part_r.at[o])
        hid = hid + part_in[src].astype(F32)
    hid = hid + res_all[...]
    hidden[...] = hid

    half_cols = pl.ds(pl.multiple_of(core * HALF, 128), HALF)
    scaled = hid * gain[:, half_cols]
    stat_out[0] = lax.dot_general(
        scaled, router[:, half_cols], (((1,), (1,)), ((), ())),
        preferred_element_type=F32, precision=lax.Precision.HIGHEST,
    )
    stat_out[1] = jnp.broadcast_to(jnp.sum(hid * hid, axis=1, keepdims=True), (16, 128))
    remote(stat_out, stat_in, pair_s.at[2], pair_r.at[2], sibling)
    landed(stat_in, pair_r.at[2])
    square = stat_out[1] + stat_in[1]
    inv = lax.rsqrt(square / (2 * HALF) + norm_eps)
    affinity = jax.nn.sigmoid((stat_out[0] + stat_in[0]) * inv) * mem_all[...]
    gates = route_scale * affinity / jnp.sum(affinity, axis=1, keepdims=True)
    coarse = gates.astype(BF16)
    fine = (gates - coarse.astype(F32)).astype(BF16)
    normed = (scaled * inv[:, 0:1]).astype(BF16)
    z, xx, yy = pos
    gath[core, 0, z, xx, yy] = normed[:, 0:640]
    gath[core, 1, z, xx, yy] = normed[:, 640:1280]
    gath[core, 2, z, xx, yy, :, 0:512] = normed[:, 1280:1792]
    gath[core, 2, z, xx, yy, :, 512:640] = jnp.where(core == 0, coarse, fine)

    whole = pl.ds(0, 4)
    halves = (pl.ds(0, 2), pl.ds(2, 2))

    def g_at(cls, spec):
        return gath.at[core, cls, spec[0], spec[1], spec[2]]

    def spec_of(order, values):
        spec = [None, None, None]
        for axis, value in zip(order, values):
            spec[axis] = value
        return spec

    for cls, order in enumerate(ORDERS):
        own = g_at(cls, pos)
        for d in (1, 2, 3):
            remote(own, own, ag_s.at[cls, 0, d], ag_r.at[cls, 0, d], along(order[0], d))
    for cls, order in enumerate(ORDERS):
        a1, a2, a3 = order
        for d in (1, 2, 3):
            src = list(pos)
            src[a1] = (pos[a1] + 4 - d) % 4
            landed(g_at(cls, src), ag_r.at[cls, 0, d])
    for phase in (1, 2):

        def block(cls, shift, half):
            a1, a2, a3 = ORDERS[cls]
            if phase == 1:
                return g_at(cls, spec_of((a1, a2, a3), (half, (pos[a2] + shift) % 4, pos[a3])))
            return g_at(cls, spec_of((a1, a2, a3), (half, whole, (pos[a3] + shift) % 4)))

        for cls, order in enumerate(ORDERS):
            if phase == 2:
                plane = g_at(cls, spec_of(order, (whole, whole, pos[order[2]])))
                remote(plane, plane, sib_s.at[cls, 0], sib_r.at[cls, 0], sibling)
            axis = order[phase]
            for half, delta, k in ((0, 1, 0), (1, 3, 1), (1, 1, 2), (0, 3, 3)):
                b = block(cls, 0, halves[half])
                remote(b, b, ag_s.at[cls, phase, k], ag_r.at[cls, phase, k], along(axis, delta))
        for cls, order in enumerate(ORDERS):
            axis = order[phase]
            b = block(cls, 3, halves[0])
            landed(b, ag_r.at[cls, phase, 0])
            remote(b, b, ag_s.at[cls, phase, 4], ag_r.at[cls, phase, 4], along(axis, 1))
            b = block(cls, 1, halves[1])
            landed(b, ag_r.at[cls, phase, 1])
            remote(b, b, ag_s.at[cls, phase, 5], ag_r.at[cls, phase, 5], along(axis, 3))
        for cls, order in enumerate(ORDERS):
            landed(block(cls, 3, halves[1]), ag_r.at[cls, phase, 2])
            landed(block(cls, 1, halves[0]), ag_r.at[cls, phase, 3])
            if phase == 2:
                for k, shift in ((1, 3), (2, 1)):
                    plane = block(cls, shift, whole)
                    remote(plane, plane, sib_s.at[cls, k], sib_r.at[cls, k], sibling)
        for cls, order in enumerate(ORDERS):
            landed(block(cls, 2, halves[0]), ag_r.at[cls, phase, 4])
            landed(block(cls, 2, halves[1]), ag_r.at[cls, phase, 5])
            if phase == 2:
                plane = block(cls, 2, whole)
                remote(plane, plane, sib_s.at[cls, 3], sib_r.at[cls, 3], sibling)
    for cls, order in enumerate(ORDERS):
        a1, a2, a3 = order
        for k, shift in ((0, 0), (1, 3), (2, 1), (3, 2)):
            spec = spec_of(order, (whole, whole, (pos[a3] + shift) % 4))
            landed(gath.at[other, cls, spec[0], spec[1], spec[2]], sib_r.at[cls, k])

    for copy in copies[2:]:
        copy.wait()

    def expert_in(i, _):
        gate = jnp.zeros((256, 256), F32)
        up = jnp.zeros((256, 256), F32)
        for h in range(2):
            for cls in range(3):
                n = WIDTHS[cls]
                k0 = h * HALF + cls * PART
                rows_in = gath[h, cls, i].reshape(256, PART)[:, :n]
                gate = gate + jnp.dot(rows_in, v_gate[0, k0 : k0 + n, :], preferred_element_type=F32)
                up = up + jnp.dot(rows_in, v_up[0, k0 : k0 + n, :], preferred_element_type=F32)
        act = gate / (1.0 + jnp.exp(-gate)) * up
        at = pl.multiple_of(i * 256, 256)
        inner[pl.ds(at, 256), :] = act.astype(BF16)
        return 0

    lax.fori_loop(0, 4, expert_in, 0)
    lane = lax.broadcasted_iota(jnp.int32, (256, 128), 1)

    def expert_out(i, half, dest):
        at = pl.multiple_of(i * 256, 256)
        weights = gath[0, 2, i, :, :, :, 512:640].astype(F32) + gath[1, 2, i, :, :, :, 512:640].astype(F32)
        weight = jnp.sum(
            jnp.where(lane == dp, weights.reshape(256, 128), 0.0), axis=1, keepdims=True
        )
        act = inner[pl.ds(at, 256), :]
        for cls in range(3):
            n = WIDTHS[cls]
            cols = pl.ds(pl.multiple_of(half * HALF + cls * PART, 128), n)
            y = jnp.dot(act, v_down[0, :, cols], preferred_element_type=F32) * weight
            dest[cls, i, :, :, :, 0:n] = y.astype(BF16).reshape(4, 4, 16, n)

    def to_sibling(i, _):
        expert_out(i, other, sib_out)
        return 0

    lax.fori_loop(0, 4, to_sibling, 0)
    remote(sib_out, sib_in, red_s.at[0], red_r.at[0], sibling)

    def to_self(i, _):
        expert_out(i, core, mix)
        return 0

    lax.fori_loop(0, 4, to_self, 0)
    landed(sib_in, red_r.at[0])

    def add_sibling(i, _):
        for cls in range(3):
            n = WIDTHS[cls]
            total = mix[cls, i, :, :, :, 0:n].astype(F32) + sib_in[cls, i, :, :, :, 0:n].astype(F32)
            mix[cls, i, :, :, :, 0:n] = total.astype(BF16)
        return 0

    lax.fori_loop(0, 4, add_sibling, 0)

    def cut(ref, n):
        return ref.at[..., pl.ds(0, n)]

    for phase in (2, 1):
        bt, bl, br = (t1, ul1, ur1) if phase == 2 else (t2, ul2, ur2)
        red = 0 if phase == 2 else 1

        def block(cls, shift, half):
            a1, a2, a3 = ORDERS[cls]
            if phase == 1:
                spec = spec_of((a1, a2, a3), (half, (pos[a2] + shift) % 4, pos[a3]))
            else:
                spec = spec_of((a1, a2, a3), (half, whole, (pos[a3] + shift) % 4))
            return (cls, spec[0], spec[1], spec[2], slice(None), pl.ds(0, WIDTHS[cls]))

        def temp(cls, half):
            a1, a2, a3 = ORDERS[cls]
            if phase == 1:
                return (cls, half, slice(None), pl.ds(0, WIDTHS[cls]))
            if a1 < a2:
                return (cls, half, whole, slice(None), pl.ds(0, WIDTHS[cls]))
            return (cls, whole, half, slice(None), pl.ds(0, WIDTHS[cls]))

        def send(cls, shift, half, buf, k, delta):
            remote(
                mix.at[block(cls, shift, halves[half])], buf.at[temp(cls, halves[half])],
                sum_s.at[cls, red, k], sum_r.at[cls, red, k], along(ORDERS[cls][phase], delta),
            )

        for cls in range(3):
            send(cls, 2, 0, bt, 0, 1)
            send(cls, 2, 1, bt, 1, 3)
            send(cls, 1, 1, bl, 2, 1)
            send(cls, 3, 0, br, 3, 3)
        for cls in range(3):
            for half, shift, buf, k, delta in ((0, 1, bl, 0, 1), (1, 3, br, 1, 3)):
                at, tmp = block(cls, shift, halves[half]), temp(cls, halves[half])
                landed(bt.at[tmp], sum_r.at[cls, red, k])
                mix[at] = (mix[at].astype(F32) + bt[tmp].astype(F32)).astype(BF16)
                send(cls, shift, half, buf, k + 4, delta)
        for cls in range(3):
            for half, ks in ((0, (4, 3)), (1, (2, 5))):
                at, tmp = block(cls, 0, halves[half]), temp(cls, halves[half])
                landed(bl.at[tmp], sum_r.at[cls, red, ks[0]])
                landed(br.at[tmp], sum_r.at[cls, red, ks[1]])
                total = mix[at].astype(F32) + bl[tmp].astype(F32) + br[tmp].astype(F32)
                mix[at] = total.astype(BF16)

    for cls, order in enumerate(ORDERS):
        a1 = order[0]
        for d in (1, 2, 3):
            coords = list(pos)
            coords[a1] = (pos[a1] + d) % 4
            src = mix.at[cls, coords[0], coords[1], coords[2], :, pl.ds(0, WIDTHS[cls])]
            dst = last.at[cls, d - 1, :, pl.ds(0, WIDTHS[cls])]
            remote(src, dst, sum_s.at[cls, 2, d], sum_r.at[cls, 2, d], along(a1, d))
    for cls in range(3):
        n = WIDTHS[cls]
        total = mix[cls, pos[0], pos[1], pos[2], :, 0:n].astype(F32)
        for d in (1, 2, 3):
            landed(last.at[cls, d - 1, :, pl.ds(0, n)], sum_r.at[cls, 2, d])
            total = total + last[cls, d - 1, :, 0:n].astype(F32)
        total = total + hidden[:, cls * PART : cls * PART + n]
        fin_out[0, :, cls * PART : cls * PART + n] = total[0:8]
        fin_out[1, :, cls * PART : cls * PART + n] = total[8:16]
    remote(fin_out.at[other], fin_in, pair_s.at[3], pair_r.at[3], sibling)
    out_ref[:, half_cols] = fin_out[core].astype(BF16)
    landed(fin_in, pair_r.at[3])
    out_ref[:, pl.ds(pl.multiple_of(other * HALF, 128), HALF)] = fin_in[...].astype(BF16)
    for src, ssem in sent:
        pltpu.make_async_copy(src, src, ssem).wait()


def layer(attended, resid, member, gain, router, w_uv, w_out, w_gate, w_up, w_down):
    vmem = pl.BlockSpec(memory_space=pltpu.VMEM)
    hbm = pl.BlockSpec(memory_space=pl.ANY)
    dma = pltpu.SemaphoreType.DMA
    grid = (3, 4, 4, 4, 16, PART)
    return pl.pallas_call(
        layer_kernel,
        out_shape=jax.ShapeDtypeStruct((8, 2 * HALF), BF16),
        in_specs=[vmem] * 5 + [hbm] * 5,
        out_specs=vmem,
        scratch_shapes=[
            pltpu.VMEM((8, 64, LATENT), BF16),
            pltpu.VMEM((512, 1024), BF16),
            pltpu.VMEM((2, 4, 16, HALF), BF16),
            pltpu.VMEM((8, 16, HALF), BF16),
            pltpu.VMEM((16, HALF), F32),
            pltpu.VMEM((16, 128), F32),
            pltpu.VMEM((2, 16, 128), F32),
            pltpu.VMEM((2, 16, 128), F32),
            pltpu.VMEM((16, HALF), F32),
            pltpu.VMEM((2,) + grid, BF16),
            pltpu.VMEM(w_uv.shape, BF16),
            pltpu.VMEM(w_out.shape, BF16),
            pltpu.VMEM(w_gate.shape, BF16),
            pltpu.VMEM(w_up.shape, BF16),
            pltpu.VMEM(w_down.shape, BF16),
            pltpu.VMEM((1024, 256), BF16),
            pltpu.VMEM(grid, BF16),
            pltpu.VMEM(grid, BF16),
            pltpu.VMEM(grid, BF16),
            pltpu.VMEM((3, 4, 4, 16, PART), BF16),
            pltpu.VMEM((3, 4, 4, 16, PART), BF16),
            pltpu.VMEM((3, 4, 4, 16, PART), BF16),
            pltpu.VMEM((3, 4, 16, PART), BF16),
            pltpu.VMEM((3, 4, 16, PART), BF16),
            pltpu.VMEM((3, 4, 16, PART), BF16),
            pltpu.VMEM((3, 3, 16, PART), BF16),
            pltpu.VMEM((2, 8, HALF), F32),
            pltpu.VMEM((8, HALF), F32),
            dma((5,)), dma, dma((8,)), dma((8,)), dma((8,)), dma((8,)), dma((4,)), dma((4,)),
            dma((3, 3, 6)), dma((3, 3, 6)), dma((3, 4)), dma((3, 4)), dma((1,)), dma((1,)),
            dma((3, 3, 6)), dma((3, 3, 6)),
        ],
        compiler_params=pltpu.CompilerParams(
            collective_id=1, has_side_effects=True, vmem_limit_bytes=56 * 2**20
        ),
        name="layer",
    )(attended, resid, member, gain, router, w_uv, w_out, w_gate, w_up, w_down)


def shards(
    cache_pool,
    page_table,
    page_counts,
    queries,
    new_latent,
    residual,
    w_uv,
    w_out,
    norm_gain,
    w_router,
    w_gate,
    w_up,
    w_down,
    routes,
):
    ep_size = lax.axis_size("ep")
    my_index = lax.axis_index("dp") * ep_size + lax.axis_index("ep")
    pool_dev = cache_pool.shape[0]
    owner_all = page_table // pool_dev
    local_all = page_table % pool_dev
    source = jnp.sum(jnp.where(owner_all == my_index, local_all, 0), axis=1)
    incoming = exchange(source.reshape(-1, 1), jnp.transpose(cache_pool, (1, 2, 0)))
    incoming = incoming.reshape(-1, 3, 96, 128)
    owner = lax.dynamic_index_in_dim(owner_all, my_index, 0, keepdims=False)
    counts = page_counts[0]
    starts = jnp.cumsum(counts) - counts
    own = jnp.pad(jnp.transpose(new_latent, (1, 0, 2)), ((0, 0), (0, 14), (0, 0)))
    attended = attend(owner, starts, counts, queries, own, incoming)

    d_model = residual.shape[2]
    resid = residual.reshape(8, 2, d_model // 2).transpose(1, 0, 2).astype(F32)
    experts = w_router.shape[1]
    member = jnp.any(routes.reshape(8, -1)[:, :, None] == jnp.arange(128)[None, None, :], axis=1)
    router = jnp.pad(w_router.T, ((0, 128 - experts), (0, 0)))
    out = layer(
        attended, resid, member.astype(F32), norm_gain.reshape(1, -1), router,
        w_uv, w_out, w_gate, w_up, w_down,
    )
    return out.reshape(residual.shape)


def solution(mesh):
    return jax.shard_map(
        shards,
        mesh=mesh,
        in_specs=(
            P(("dp", "ep"), None, None),
            P(),
            P(("dp", "ep"), None),
            P(None, ("dp", "ep"), None, None),
            P(None, ("dp", "ep"), None),
            P(None, ("dp", "ep"), None),
            P("ep", None, None),
            P("ep", None),
            P(),
            P(),
            P("dp", None, "ep"),
            P("dp", None, "ep"),
            P("dp", "ep", None),
            P(None, ("dp", "ep"), None),
        ),
        out_specs=P(None, ("dp", "ep"), None),
        check_vma=False,
    )
```

```python
import functools

import jax
import jax.numpy as jnp
from jax import lax
from jax.experimental import pallas as pl
from jax.experimental.pallas import tpu as pltpu
from jax.sharding import PartitionSpec as P

MESH = pl.DeviceIdType.MESH
F32 = jnp.float32
BF16 = jnp.bfloat16

LATENT = 512
ROPE = 64
PAGE = 64
TILE = 8
score_scale = 192.0 ** (-0.5)
route_scale = 2.5
norm_eps = 1e-06

HALF = 1792
PART = 640
ORDERS = ((0, 1, 2), (1, 2, 0), (2, 0, 1))
WIDTHS = (640, 640, 512)


def exchange_kernel(
    table, pool, out,
    pool_v, slots, held1, held2, stage,
    psem, lsem, csem, send1, recv1, send2, recv2, send3, recv3,
):
    dp = lax.axis_index("dp")
    ep = lax.axis_index("ep")
    pos = (dp // 4, dp % 4, ep // 2)
    core = ep % 2
    other = 1 - core
    whole = pl.ds(0, 4)

    loads = [
        pltpu.make_async_copy(
            pool.at[pl.ds(i * 16, 16)], pool_v.at[pl.ds(i * 16, 16)], psem.at[i]
        )
        for i in range(4)
    ]
    for load in loads:
        load.start()

    def along(axis, delta, c):
        coords = list(pos)
        coords[axis] = (coords[axis] + delta) % 4
        return (coords[0] * 4 + coords[1], coords[2] * 2 + c)

    def spec_of(order, values):
        spec = [None, None, None]
        for axis, value in zip(order, values):
            spec[axis] = value
        return tuple(spec)

    barrier = pltpu.get_barrier_semaphore()
    peers = [along(a, d, c) for a in range(3) for d in (1, 2, 3) for c in (core, other)]
    peers.append(along(0, 0, other))
    for peer in peers:
        pl.semaphore_signal(barrier, inc=1, device_id=peer, device_id_type=MESH)

    pages = table[...]
    wanted = jnp.where(pages // 128 == dp * 8 + ep, pages % 128, 0)
    wanted = jnp.sum(wanted, axis=0, keepdims=True)
    page = lax.broadcasted_iota(jnp.int32, (128, 128), 0)
    onehot = jnp.transpose(jnp.where(wanted == page, 1.0, 0.0)).astype(BF16)

    def put(cls, row, pieces):
        for j in range(0, 16, 4):
            x = jnp.concatenate(pieces(j), axis=0)
            y = lax.dot_general(onehot, x, (((1,), (1,)), ((), ())), preferred_element_type=F32)
            for i in range(4):
                stage[:, j + i, :] = y[:, i * 128 : (i + 1) * 128]
        at = pl.multiple_of(row, 16)
        block = stage[...].astype(BF16).reshape(4, 4, 4, 2, 16, 128)
        slots[cls, :, :, :, :, pl.ds(at, 16), :] = block

    def latent_rows(cls, chunk, first, count, row):
        def unit(u, _):
            def pieces(j):
                t = (first + u) * 16 + j
                return [pool_v[pl.ds(t, 4), chunk * 128 : (chunk + 1) * 128, :].reshape(512, 128)]

            put(cls, row + u * 16, pieces)
            return 0

        lax.fori_loop(0, count, unit, 0)

    def rope_rows(cls, row):
        def unit(u, _):
            def pieces(j):
                found = []
                for i in range(4):
                    found.append(pool_v[u * 16 + j + i, 512:576, :])
                    found.append(pool_v[32 + u * 16 + j + i, 512:576, :])
                return found

            put(cls, row + u * 16, pieces)
            return 0

        lax.fori_loop(0, 2, unit, 0)

    sends = []

    def remote(src, dst, ssem, rsem, peer):
        pltpu.make_async_remote_copy(
            src_ref=src, dst_ref=dst, send_sem=ssem, recv_sem=rsem,
            device_id=peer, device_id_type=MESH,
        ).start()
        sends.append((src, ssem))

    def landed(ref, sem):
        pltpu.make_async_copy(ref, ref, sem).wait()

    for part in range(3):
        rows = pl.ds(part * 32, 32)
        for load in loads[2 * part : 2 * part + 2]:
            load.wait()
        for cls, order in enumerate(ORDERS):
            a1, a2, a3 = order
            if part < 2:
                latent_rows(cls, cls, 2 * part, 2, 32 * part)
            elif cls < 2:
                latent_rows(cls, 3, 2 * cls, 2, 64)
            else:
                rope_rows(cls, 64)
            if part == 0 and cls == 0:
                pl.semaphore_wait(barrier, len(peers))
            for d in (1, 2, 3):
                src = spec_of(order, ((pos[a1] + d) % 4, whole, whole))
                dst = spec_of(order, (pos[a1], whole, whole))
                remote(
                    slots.at[(cls,) + src + (pl.ds(0, 2), rows)],
                    held1.at[(cls,) + dst + (pl.ds(0, 2), rows)],
                    send1.at[cls, d, part], recv1.at[cls, d, part], along(a1, d, core),
                )
            if part == 2:
                own = (cls,) + spec_of(order, (pos[a1], whole, whole))
                pltpu.make_async_copy(slots.at[own], held1.at[own], lsem.at[cls]).start()

    def second(cls, buf, e):
        a1, a2, a3 = order = ORDERS[cls]
        src1 = (pos[a1] + 4 - e) % 4
        for d in (1, 2, 3):
            src = spec_of(order, (src1, (pos[a2] + d) % 4, whole))
            dst = spec_of(order, (src1, pos[a2], whole))
            remote(
                buf.at[(cls,) + src], held2.at[(cls,) + dst],
                send2.at[cls, d, e], recv2.at[cls, d, e], along(a2, d, core),
            )

    def third(cls, buf, f):
        a1, a2, a3 = order = ORDERS[cls]
        src2 = (pos[a2] + 4 - f) % 4
        for d in (1, 2, 3, 0):
            for k, c in ((0, core), (1, other)):
                src = spec_of(order, (whole, src2, (pos[a3] + d) % 4))
                dst = spec_of(order, (whole, src2, pos[a3]))
                a = buf.at[(cls,) + src + (c,)]
                b = out.at[dst + (core, cls)]
                if d == 0 and k == 0:
                    pltpu.make_async_copy(a, b, csem.at[cls, f]).start()
                else:
                    remote(a, b, send3.at[cls, f, d, k], recv3.at[cls, f, d, k], along(a3, d, c))

    for cls in range(3):
        second(cls, slots, 0)
    for e in (1, 3, 2):
        for cls, order in enumerate(ORDERS):
            src1 = (pos[order[0]] + 4 - e) % 4
            at = spec_of(order, (src1, whole, whole))
            for part in range(3):
                rows = pl.ds(part * 32, 32)
                landed(held1.at[(cls,) + at + (pl.ds(0, 2), rows)], recv1.at[cls, e, part])
            second(cls, held1, e)
    for cls, order in enumerate(ORDERS):
        own = spec_of(order, (pos[order[0]], whole, whole))
        landed(held1.at[(cls,) + own], lsem.at[cls])
        third(cls, held1, 0)
    for f in (1, 3, 2):
        for cls, order in enumerate(ORDERS):
            a1, a2, a3 = order
            for e in range(4):
                at = spec_of(order, ((pos[a1] + 4 - e) % 4, (pos[a2] + 4 - f) % 4, whole))
                landed(held2.at[(cls,) + at], recv2.at[cls, f, e])
            third(cls, held2, f)
    for cls, order in enumerate(ORDERS):
        a1, a2, a3 = order
        for f in range(4):
            for d in range(4):
                for k, c in ((0, core), (1, other)):
                    at = spec_of(order, (whole, (pos[a2] + 4 - f) % 4, (pos[a3] + 4 - d) % 4))
                    ref = out.at[at + (c, cls)]
                    landed(ref, csem.at[cls, f] if d == 0 and k == 0 else recv3.at[cls, f, d, k])
    for src, ssem in sends:
        landed(src, ssem)


def exchange(table, pool):
    vmem = pl.BlockSpec(memory_space=pltpu.VMEM)
    hbm = pl.BlockSpec(memory_space=pl.ANY)
    dma = pltpu.SemaphoreType.DMA
    held = (3, 4, 4, 4, 2, 96, 128)
    return pl.pallas_call(
        exchange_kernel,
        out_shape=jax.ShapeDtypeStruct((4, 4, 4, 2, 3, 96, 128), BF16),
        in_specs=[vmem, hbm],
        out_specs=hbm,
        scratch_shapes=[
            pltpu.VMEM(pool.shape, BF16),
            pltpu.VMEM(held, BF16),
            pltpu.VMEM(held, BF16),
            pltpu.VMEM(held, BF16),
            pltpu.VMEM((128, 16, 128), F32),
            dma((4,)), dma((3,)), dma((3, 4)), dma((3, 4, 3)), dma((3, 4, 3)), dma((3, 4, 4)),
            dma((3, 4, 4)), dma((3, 4, 4, 2)), dma((3, 4, 4, 2)),
        ],
        compiler_params=pltpu.CompilerParams(
            collective_id=2, has_side_effects=True, vmem_limit_bytes=56 * 2**20
        ),
        name="exchange",
    )(table, pool)


def attend_kernel(
    owner, starts, counts, q_ref, own_ref, slots, out_ref, keys, last, ropes, scores, sem
):
    pages = 64

    def fetch(j, _):
        at = pl.multiple_of(j * PAGE, PAGE)
        slot = slots.at[owner[j]]
        pltpu.make_async_copy(
            slot.at[:, pl.ds(0, 64), :], keys.at[:, pl.ds(at, PAGE), :], sem.at[0]
        ).start()
        pltpu.make_async_copy(
            slot.at[pl.ds(0, 2), pl.ds(64, 32), :], last.at[j], sem.at[1]
        ).start()
        pltpu.make_async_copy(slot.at[2, pl.ds(64, 32), :], ropes.at[j], sem.at[2]).start()
        return 0

    lax.fori_loop(0, pages, fetch, 0)

    def clear(j, _):
        at = pl.multiple_of((pages + j) * PAGE, PAGE)
        keys[:, pl.ds(at, PAGE), :] = jnp.zeros((3, PAGE, 128), BF16)
        last[pages + j] = jnp.zeros((2, 32, 128), BF16)
        ropes[pages + j] = jnp.zeros((32, 128), BF16)
        return 0

    lax.fori_loop(0, TILE, clear, 0)
    for k, ref in enumerate(
        (keys.at[:, pl.ds(0, pages * PAGE), :], last.at[pl.ds(0, pages)], ropes.at[pl.ds(0, pages)])
    ):
        pltpu.make_async_copy(ref, ref, sem.at[k]).wait()
    width = TILE * PAGE
    step_of = lax.broadcasted_iota(jnp.int32, (128, 16), 0) // 64
    token = lax.broadcasted_iota(jnp.int32, (128, 16), 1)
    low = lax.broadcasted_iota(jnp.int32, (TILE, 32, 128), 2) < ROPE

    def values_of(page):
        at = pl.multiple_of(page * PAGE, PAGE)
        parts = [keys[k, pl.ds(at, width), :] for k in range(3)]
        parts.append(last[pl.ds(page, TILE)].reshape(width, 128))
        return jnp.concatenate(parts, axis=1)

    def request(r, _):
        q = jnp.concatenate([q_ref[0, r], q_ref[1, r]], axis=0)
        own = own_ref[r]
        s_own = lax.dot_general(q, own, (((1,), (1,)), ((), ())), preferred_element_type=F32)
        s_own = jnp.where(token <= step_of, s_own * score_scale, -jnp.inf)
        q_rope = q[:, LATENT:]
        q_wide = jnp.concatenate([q[:, :LATENT], q_rope, q_rope], axis=1)
        start = starts[r]
        length = counts[r] * PAGE
        tiles = (length + width - 1) // width

        def score(t, top):
            page = start + t * TILE
            rope = ropes[pl.ds(page, TILE)]
            zero = jnp.zeros_like(rope)
            pair = jnp.concatenate([jnp.where(low, rope, zero), jnp.where(low, zero, rope)], axis=1)
            key = jnp.concatenate([values_of(page), pair.reshape(width, 128)], axis=1)
            s = lax.dot_general(q_wide, key, (((1,), (1,)), ((), ())), preferred_element_type=F32)
            place = t * width + lax.broadcasted_iota(jnp.int32, (128, width), 1)
            s = jnp.where(place < length, s * score_scale, -jnp.inf)
            scores[t] = s
            return jnp.maximum(top, jnp.max(s, axis=1, keepdims=True))

        top = lax.fori_loop(0, tiles, score, jnp.max(s_own, axis=1, keepdims=True))
        p_own = jnp.exp(s_own - top)
        total = jnp.sum(p_own, axis=1, keepdims=True)
        acc = jnp.dot(p_own.astype(BF16), own[:, :LATENT], preferred_element_type=F32)

        def mix(t, carry):
            total, acc = carry
            p = jnp.exp(scores[t] - top)
            total = total + jnp.sum(p, axis=1, keepdims=True)
            acc = acc + jnp.dot(
                p.astype(BF16), values_of(start + t * TILE), preferred_element_type=F32
            )
            return total, acc

        total, acc = lax.fori_loop(0, tiles, mix, (total, acc))
        res = (acc / total).reshape(2, 8, 8, LATENT)
        at = pl.multiple_of(r * 16, 16)
        for g in range(8):
            block = jnp.concatenate([res[0, g], res[1, g]], axis=0)
            out_ref[g, pl.ds(at, 16), :] = block.astype(BF16)
        return 0

    lax.fori_loop(0, 4, request, 0)


def attend(owner, starts, counts, queries, own, slots):
    smem = pl.BlockSpec(memory_space=pltpu.SMEM)
    vmem = pl.BlockSpec(memory_space=pltpu.VMEM)
    return pl.pallas_call(
        attend_kernel,
        out_shape=jax.ShapeDtypeStruct((8, 64, LATENT), BF16),
        in_specs=[smem, smem, smem, vmem, vmem, pl.BlockSpec(memory_space=pl.ANY)],
        out_specs=vmem,
        scratch_shapes=[
            pltpu.VMEM((3, (64 + TILE) * PAGE, 128), BF16),
            pltpu.VMEM((64 + TILE, 2, 32, 128), BF16),
            pltpu.VMEM((64 + TILE, 32, 128), BF16),
            pltpu.VMEM((32 // TILE, 128, TILE * PAGE), F32),
            pltpu.SemaphoreType.DMA((3,)),
        ],
        compiler_params=pltpu.CompilerParams(vmem_limit_bytes=60 * 2**20),
        name="attend",
    )(owner, starts, counts, queries, own, slots)


def layer_kernel(
    attended, residual, routes, gain, router, w_uv, w_out, w_gate, w_up, w_down,
    out_ref,
    resid, member, heads_in, masked, part_out, part_in, res_all, mem_all, stat_out, stat_in, hidden,
    gath, v_uv, v_out, v_gate, v_up, v_down, inner,
    mix, sib_out, sib_in, t1, ul1, ur1, t2, ul2, ur2, last, fin_out, fin_in,
    wsem, lsem, head_s, head_r, part_s, part_r, pair_s, pair_r,
    ag_s, ag_r, sib_s, sib_r, red_s, red_r, sum_s, sum_r,
):
    dp = lax.axis_index("dp")
    ep = lax.axis_index("ep")
    pos = (dp // 4, dp % 4, ep // 2)
    core = ep % 2
    other = 1 - core

    def device(coords, c):
        return (coords[0] * 4 + coords[1], coords[2] * 2 + c)

    def along(axis, delta):
        coords = [pos[0], pos[1], pos[2]]
        coords[axis] = (coords[axis] + delta) % 4
        return device(coords, core)

    sibling = device(pos, other)
    ep_peers = [(dp, (ep + o) % 8) for o in range(1, 8)]
    ring_peers = [along(a, d) for a in (0, 1) for d in (1, 2, 3)]

    def remote(src, dst, ssem, rsem, peer):
        copy = pltpu.make_async_remote_copy(
            src_ref=src, dst_ref=dst, send_sem=ssem, recv_sem=rsem,
            device_id=peer, device_id_type=MESH,
        )
        copy.start()
        sent.append((src, ssem))

    def landed(ref, rsem):
        pltpu.make_async_copy(ref, ref, rsem).wait()

    sent = []

    loads = [(w_uv, v_uv), (w_out, v_out), (w_gate, v_gate), (w_up, v_up), (w_down, v_down)]
    copies = [pltpu.make_async_copy(a, b, wsem.at[i]) for i, (a, b) in enumerate(loads)]
    for copy in copies:
        copy.start()

    barrier = pltpu.get_barrier_semaphore()
    for peer in ep_peers + ring_peers:
        pl.semaphore_signal(barrier, inc=1, device_id=peer, device_id_type=MESH)
    for h in range(2):
        cols = slice(h * HALF, (h + 1) * HALF)
        both = [residual[s, :, cols].astype(F32) for s in range(2)]
        resid[h] = jnp.concatenate(both, axis=0)
    route = jnp.concatenate([routes[0], routes[1]], axis=0)
    lanes = lax.broadcasted_iota(jnp.int32, (8, 128), 1)
    named = jnp.zeros((8, 128), F32)
    for k in range(8):
        named = jnp.where(route[:, k : k + 1] == lanes, 1.0, named)
    member[...] = named
    pl.semaphore_wait(barrier, len(ep_peers) + len(ring_peers))

    for o in range(1, 8):
        to = (ep + o) % 8
        remote(attended.at[to], heads_in.at[ep], head_s.at[o], head_r.at[o], (dp, to))
    own_heads = pltpu.make_async_copy(attended.at[ep], heads_in.at[ep], lsem)
    own_heads.start()
    own_rows = pl.ds(pl.multiple_of(core * 8, 8), 8)
    other_rows = pl.ds(pl.multiple_of(other * 8, 8), 8)
    remote(resid.at[other], res_all.at[own_rows], pair_s.at[0], pair_r.at[0], sibling)
    remote(member, mem_all.at[own_rows], pair_s.at[1], pair_r.at[1], sibling)
    res_all[own_rows, :] = resid[core]
    mem_all[own_rows, :] = member[...]
    own_heads.wait()
    for o in range(1, 8):
        landed(heads_in.at[(ep + 8 - o) % 8], head_r.at[o])

    copies[0].wait()
    x = heads_in[...].reshape(512, LATENT)
    row_head = lax.broadcasted_iota(jnp.int32, (512, 128), 0) % 8
    for h in range(8):
        y = jnp.dot(x, v_uv[h], preferred_element_type=F32)
        masked[:, h * 128 : (h + 1) * 128] = jnp.where(row_head == h, y, 0.0).astype(BF16)
    to_row = lax.broadcasted_iota(jnp.int32, (64, 512), 0)
    from_row = lax.broadcasted_iota(jnp.int32, (64, 512), 1) // 8
    wanted = (to_row // 8) * 8 + (to_row % 4) * 2 + (to_row % 8) // 4
    pick = jnp.where(from_row == wanted, 1.0, 0.0).astype(BF16)
    flat = jnp.dot(pick, masked[...], preferred_element_type=F32).astype(BF16)

    copies[1].wait()
    for h in range(2):
        for t in range(HALF // 256):
            col = h * HALF + t * 256
            y = jnp.dot(flat, v_out[:, col : col + 256], preferred_element_type=F32)
            part_out[h, :, :, t * 256 : (t + 1) * 256] = y.astype(BF16).reshape(4, 16, 256)
    for o in range(1, 8):
        to = (ep + o) % 8
        remote(
            part_out.at[to % 2, to // 2], part_in.at[ep], part_s.at[o], part_r.at[o], (dp, to)
        )
    landed(res_all.at[other_rows], pair_r.at[0])
    landed(mem_all.at[other_rows], pair_r.at[1])
    hid = part_out[core, pos[2]].astype(F32)
    for o in range(1, 8):
        src = (ep + 8 - o) % 8
        landed(part_in.at[src], part_r.at[o])
        hid = hid + part_in[src].astype(F32)
    hid = hid + res_all[...]
    hidden[...] = hid

    half_cols = pl.ds(pl.multiple_of(core * HALF, 128), HALF)
    scaled = hid * gain[half_cols].reshape(1, HALF)
    stat_out[0] = jnp.zeros((16, 128), F32)
    stat_out[0, :, 0:16] = lax.dot_general(
        scaled, router[:, half_cols], (((1,), (1,)), ((), ())),
        preferred_element_type=F32, precision=lax.Precision.HIGHEST,
    )
    stat_out[1] = jnp.broadcast_to(jnp.sum(hid * hid, axis=1, keepdims=True), (16, 128))
    remote(stat_out, stat_in, pair_s.at[2], pair_r.at[2], sibling)
    landed(stat_in, pair_r.at[2])
    square = stat_out[1] + stat_in[1]
    inv = lax.rsqrt(square / (2 * HALF) + norm_eps)
    affinity = jax.nn.sigmoid((stat_out[0] + stat_in[0]) * inv) * mem_all[...]
    gates = route_scale * affinity / jnp.sum(affinity, axis=1, keepdims=True)
    coarse = gates.astype(BF16)
    fine = (gates - coarse.astype(F32)).astype(BF16)
    normed = (scaled * inv[:, 0:1]).astype(BF16)
    z, xx, yy = pos
    gath[core, 0, z, xx, yy] = normed[:, 0:640]
    gath[core, 1, z, xx, yy] = normed[:, 640:1280]
    gath[core, 2, z, xx, yy, :, 0:512] = normed[:, 1280:1792]
    gath[core, 2, z, xx, yy, :, 512:640] = jnp.where(core == 0, coarse, fine)

    whole = pl.ds(0, 4)
    halves = (pl.ds(0, 2), pl.ds(2, 2))

    def g_at(cls, spec):
        return gath.at[core, cls, spec[0], spec[1], spec[2]]

    def spec_of(order, values):
        spec = [None, None, None]
        for axis, value in zip(order, values):
            spec[axis] = value
        return spec

    for cls, order in enumerate(ORDERS):
        own = g_at(cls, pos)
        for d in (1, 2, 3):
            remote(own, own, ag_s.at[cls, 0, d], ag_r.at[cls, 0, d], along(order[0], d))
    for cls, order in enumerate(ORDERS):
        a1, a2, a3 = order
        for d in (1, 2, 3):
            src = list(pos)
            src[a1] = (pos[a1] + 4 - d) % 4
            landed(g_at(cls, src), ag_r.at[cls, 0, d])
    for phase in (1, 2):

        def block(cls, shift, half):
            a1, a2, a3 = ORDERS[cls]
            if phase == 1:
                return g_at(cls, spec_of((a1, a2, a3), (half, (pos[a2] + shift) % 4, pos[a3])))
            return g_at(cls, spec_of((a1, a2, a3), (half, whole, (pos[a3] + shift) % 4)))

        for cls, order in enumerate(ORDERS):
            if phase == 2:
                plane = g_at(cls, spec_of(order, (whole, whole, pos[order[2]])))
                remote(plane, plane, sib_s.at[cls, 0], sib_r.at[cls, 0], sibling)
            axis = order[phase]
            for half, delta, k in ((0, 1, 0), (1, 3, 1), (1, 1, 2), (0, 3, 3)):
                b = block(cls, 0, halves[half])
                remote(b, b, ag_s.at[cls, phase, k], ag_r.at[cls, phase, k], along(axis, delta))
        for cls, order in enumerate(ORDERS):
            axis = order[phase]
            b = block(cls, 3, halves[0])
            landed(b, ag_r.at[cls, phase, 0])
            remote(b, b, ag_s.at[cls, phase, 4], ag_r.at[cls, phase, 4], along(axis, 1))
            b = block(cls, 1, halves[1])
            landed(b, ag_r.at[cls, phase, 1])
            remote(b, b, ag_s.at[cls, phase, 5], ag_r.at[cls, phase, 5], along(axis, 3))
        for cls, order in enumerate(ORDERS):
            landed(block(cls, 3, halves[1]), ag_r.at[cls, phase, 2])
            landed(block(cls, 1, halves[0]), ag_r.at[cls, phase, 3])
            if phase == 2:
                for k, shift in ((1, 3), (2, 1)):
                    plane = block(cls, shift, whole)
                    remote(plane, plane, sib_s.at[cls, k], sib_r.at[cls, k], sibling)
        for cls, order in enumerate(ORDERS):
            landed(block(cls, 2, halves[0]), ag_r.at[cls, phase, 4])
            landed(block(cls, 2, halves[1]), ag_r.at[cls, phase, 5])
            if phase == 2:
                plane = block(cls, 2, whole)
                remote(plane, plane, sib_s.at[cls, 3], sib_r.at[cls, 3], sibling)
    for cls, order in enumerate(ORDERS):
        a1, a2, a3 = order
        for k, shift in ((0, 0), (1, 3), (2, 1), (3, 2)):
            spec = spec_of(order, (whole, whole, (pos[a3] + shift) % 4))
            landed(gath.at[other, cls, spec[0], spec[1], spec[2]], sib_r.at[cls, k])

    for copy in copies[2:]:
        copy.wait()

    def expert_in(i, _):
        gate = jnp.zeros((256, 256), F32)
        up = jnp.zeros((256, 256), F32)
        for h in range(2):
            for cls in range(3):
                n = WIDTHS[cls]
                k0 = h * HALF + cls * PART
                rows_in = gath[h, cls, i].reshape(256, PART)[:, :n]
                gate = gate + jnp.dot(rows_in, v_gate[0, k0 : k0 + n, :], preferred_element_type=F32)
                up = up + jnp.dot(rows_in, v_up[0, k0 : k0 + n, :], preferred_element_type=F32)
        act = gate / (1.0 + jnp.exp(-gate)) * up
        at = pl.multiple_of(i * 256, 256)
        inner[pl.ds(at, 256), :] = act.astype(BF16)
        return 0

    lax.fori_loop(0, 4, expert_in, 0)
    lane = lax.broadcasted_iota(jnp.int32, (256, 128), 1)

    def expert_out(i, half, dest):
        at = pl.multiple_of(i * 256, 256)
        weights = gath[0, 2, i, :, :, :, 512:640].astype(F32) + gath[1, 2, i, :, :, :, 512:640].astype(F32)
        weight = jnp.sum(
            jnp.where(lane == dp, weights.reshape(256, 128), 0.0), axis=1, keepdims=True
        )
        act = inner[pl.ds(at, 256), :]
        for cls in range(3):
            n = WIDTHS[cls]
            cols = pl.ds(pl.multiple_of(half * HALF + cls * PART, 128), n)
            y = jnp.dot(act, v_down[0, :, cols], preferred_element_type=F32) * weight
            dest[cls, i, :, :, :, 0:n] = y.astype(BF16).reshape(4, 4, 16, n)

    def to_sibling(i, _):
        expert_out(i, other, sib_out)
        return 0

    lax.fori_loop(0, 4, to_sibling, 0)
    remote(sib_out, sib_in, red_s.at[0], red_r.at[0], sibling)

    def to_self(i, _):
        expert_out(i, core, mix)
        return 0

    lax.fori_loop(0, 4, to_self, 0)
    landed(sib_in, red_r.at[0])

    def add_sibling(i, _):
        for cls in range(3):
            n = WIDTHS[cls]
            total = mix[cls, i, :, :, :, 0:n].astype(F32) + sib_in[cls, i, :, :, :, 0:n].astype(F32)
            mix[cls, i, :, :, :, 0:n] = total.astype(BF16)
        return 0

    lax.fori_loop(0, 4, add_sibling, 0)

    def cut(ref, n):
        return ref.at[..., pl.ds(0, n)]

    for phase in (2, 1):
        bt, bl, br = (t1, ul1, ur1) if phase == 2 else (t2, ul2, ur2)
        red = 0 if phase == 2 else 1

        def block(cls, shift, half):
            a1, a2, a3 = ORDERS[cls]
            if phase == 1:
                spec = spec_of((a1, a2, a3), (half, (pos[a2] + shift) % 4, pos[a3]))
            else:
                spec = spec_of((a1, a2, a3), (half, whole, (pos[a3] + shift) % 4))
            return (cls, spec[0], spec[1], spec[2], slice(None), pl.ds(0, WIDTHS[cls]))

        def temp(cls, half):
            a1, a2, a3 = ORDERS[cls]
            if phase == 1:
                return (cls, half, slice(None), pl.ds(0, WIDTHS[cls]))
            if a1 < a2:
                return (cls, half, whole, slice(None), pl.ds(0, WIDTHS[cls]))
            return (cls, whole, half, slice(None), pl.ds(0, WIDTHS[cls]))

        def send(cls, shift, half, buf, k, delta):
            remote(
                mix.at[block(cls, shift, halves[half])], buf.at[temp(cls, halves[half])],
                sum_s.at[cls, red, k], sum_r.at[cls, red, k], along(ORDERS[cls][phase], delta),
            )

        for cls in range(3):
            send(cls, 2, 0, bt, 0, 1)
            send(cls, 2, 1, bt, 1, 3)
            send(cls, 1, 1, bl, 2, 1)
            send(cls, 3, 0, br, 3, 3)
        for cls in range(3):
            for half, shift, buf, k, delta in ((0, 1, bl, 0, 1), (1, 3, br, 1, 3)):
                at, tmp = block(cls, shift, halves[half]), temp(cls, halves[half])
                landed(bt.at[tmp], sum_r.at[cls, red, k])
                mix[at] = (mix[at].astype(F32) + bt[tmp].astype(F32)).astype(BF16)
                send(cls, shift, half, buf, k + 4, delta)
        for cls in range(3):
            for half, ks in ((0, (4, 3)), (1, (2, 5))):
                at, tmp = block(cls, 0, halves[half]), temp(cls, halves[half])
                landed(bl.at[tmp], sum_r.at[cls, red, ks[0]])
                landed(br.at[tmp], sum_r.at[cls, red, ks[1]])
                total = mix[at].astype(F32) + bl[tmp].astype(F32) + br[tmp].astype(F32)
                mix[at] = total.astype(BF16)

    for cls, order in enumerate(ORDERS):
        a1 = order[0]
        for d in (1, 2, 3):
            coords = list(pos)
            coords[a1] = (pos[a1] + d) % 4
            src = mix.at[cls, coords[0], coords[1], coords[2], :, pl.ds(0, WIDTHS[cls])]
            dst = last.at[cls, d - 1, :, pl.ds(0, WIDTHS[cls])]
            remote(src, dst, sum_s.at[cls, 2, d], sum_r.at[cls, 2, d], along(a1, d))
    for cls in range(3):
        n = WIDTHS[cls]
        total = mix[cls, pos[0], pos[1], pos[2], :, 0:n].astype(F32)
        for d in (1, 2, 3):
            landed(last.at[cls, d - 1, :, pl.ds(0, n)], sum_r.at[cls, 2, d])
            total = total + last[cls, d - 1, :, 0:n].astype(F32)
        total = total + hidden[:, cls * PART : cls * PART + n]
        fin_out[0, :, cls * PART : cls * PART + n] = total[0:8]
        fin_out[1, :, cls * PART : cls * PART + n] = total[8:16]
    remote(fin_out.at[other], fin_in, pair_s.at[3], pair_r.at[3], sibling)
    for s in range(2):
        out_ref[s, :, half_cols] = fin_out[core, s * 4 : s * 4 + 4].astype(BF16)
    landed(fin_in, pair_r.at[3])
    for s in range(2):
        cols = pl.ds(pl.multiple_of(other * HALF, 128), HALF)
        out_ref[s, :, cols] = fin_in[s * 4 : s * 4 + 4].astype(BF16)
    for src, ssem in sent:
        pltpu.make_async_copy(src, src, ssem).wait()


def layer(attended, residual, routes, gain, router, w_uv, w_out, w_gate, w_up, w_down):
    vmem = pl.BlockSpec(memory_space=pltpu.VMEM)
    hbm = pl.BlockSpec(memory_space=pl.ANY)
    dma = pltpu.SemaphoreType.DMA
    grid = (3, 4, 4, 4, 16, PART)
    return pl.pallas_call(
        layer_kernel,
        out_shape=jax.ShapeDtypeStruct((2, 4, 2 * HALF), BF16),
        in_specs=[vmem] * 5 + [hbm] * 5,
        out_specs=vmem,
        scratch_shapes=[
            pltpu.VMEM((2, 8, HALF), F32),
            pltpu.VMEM((8, 128), F32),
            pltpu.VMEM((8, 64, LATENT), BF16),
            pltpu.VMEM((512, 1024), BF16),
            pltpu.VMEM((2, 4, 16, HALF), BF16),
            pltpu.VMEM((8, 16, HALF), BF16),
            pltpu.VMEM((16, HALF), F32),
            pltpu.VMEM((16, 128), F32),
            pltpu.VMEM((2, 16, 128), F32),
            pltpu.VMEM((2, 16, 128), F32),
            pltpu.VMEM((16, HALF), F32),
            pltpu.VMEM((2,) + grid, BF16),
            pltpu.VMEM(w_uv.shape, BF16),
            pltpu.VMEM(w_out.shape, BF16),
            pltpu.VMEM(w_gate.shape, BF16),
            pltpu.VMEM(w_up.shape, BF16),
            pltpu.VMEM(w_down.shape, BF16),
            pltpu.VMEM((1024, 256), BF16),
            pltpu.VMEM(grid, BF16),
            pltpu.VMEM(grid, BF16),
            pltpu.VMEM(grid, BF16),
            pltpu.VMEM((3, 4, 4, 16, PART), BF16),
            pltpu.VMEM((3, 4, 4, 16, PART), BF16),
            pltpu.VMEM((3, 4, 4, 16, PART), BF16),
            pltpu.VMEM((3, 4, 16, PART), BF16),
            pltpu.VMEM((3, 4, 16, PART), BF16),
            pltpu.VMEM((3, 4, 16, PART), BF16),
            pltpu.VMEM((3, 3, 16, PART), BF16),
            pltpu.VMEM((2, 8, HALF), F32),
            pltpu.VMEM((8, HALF), F32),
            dma((5,)), dma, dma((8,)), dma((8,)), dma((8,)), dma((8,)), dma((4,)), dma((4,)),
            dma((3, 3, 6)), dma((3, 3, 6)), dma((3, 4)), dma((3, 4)), dma((1,)), dma((1,)),
            dma((3, 3, 6)), dma((3, 3, 6)),
        ],
        compiler_params=pltpu.CompilerParams(
            collective_id=1, has_side_effects=True, vmem_limit_bytes=56 * 2**20
        ),
        name="layer",
    )(attended, residual, routes, gain, router, w_uv, w_out, w_gate, w_up, w_down)


def shards(
    cache_pool,
    page_table,
    page_counts,
    queries,
    new_latent,
    residual,
    w_uv,
    w_out,
    norm_gain,
    w_router,
    w_gate,
    w_up,
    w_down,
    routes,
):
    ep_size = lax.axis_size("ep")
    my_index = lax.axis_index("dp") * ep_size + lax.axis_index("ep")
    pool_dev = cache_pool.shape[0]
    owner_all = page_table // pool_dev
    incoming = exchange(page_table.T, jnp.transpose(cache_pool, (1, 2, 0)))
    incoming = incoming.reshape(-1, 3, 96, 128)
    owner = lax.dynamic_index_in_dim(owner_all, my_index, 0, keepdims=False)
    counts = page_counts[0]
    starts = jnp.cumsum(counts) - counts
    own = jnp.pad(jnp.transpose(new_latent, (1, 0, 2)), ((0, 0), (0, 14), (0, 0)))
    attended = attend(owner, starts, counts, queries, own, incoming)

    return layer(
        attended, residual, routes, norm_gain, w_router.T, w_uv, w_out, w_gate, w_up, w_down
    )


def solution(mesh):
    return jax.shard_map(
        shards,
        mesh=mesh,
        in_specs=(
            P(("dp", "ep"), None, None),
            P(),
            P(("dp", "ep"), None),
            P(None, ("dp", "ep"), None, None),
            P(None, ("dp", "ep"), None),
            P(None, ("dp", "ep"), None),
            P("ep", None, None),
            P("ep", None),
            P(),
            P(),
            P("dp", None, "ep"),
            P("dp", None, "ep"),
            P("dp", "ep", None),
            P(None, ("dp", "ep"), None),
        ),
        out_specs=P(None, ("dp", "ep"), None),
        check_vma=False,
    )
```

```python
import functools

import jax
import jax.numpy as jnp
from jax import lax
from jax.experimental import pallas as pl
from jax.experimental.pallas import tpu as pltpu
from jax.sharding import PartitionSpec as P

MESH = pl.DeviceIdType.MESH
F32 = jnp.float32
BF16 = jnp.bfloat16

LATENT = 512
ROPE = 64
PAGE = 64
TILE = 16
score_scale = 192.0 ** (-0.5)
route_scale = 2.5
norm_eps = 1e-06

HALF = 1792
PART = 640
ORDERS = ((0, 1, 2), (1, 2, 0), (2, 0, 1))
WIDTHS = (640, 640, 512)


def exchange_kernel(
    table, pool, out,
    pool_v, slots, held1, held2, stage,
    psem, lsem, csem, send1, recv1, send2, recv2, send3, recv3,
):
    dp = lax.axis_index("dp")
    ep = lax.axis_index("ep")
    pos = (dp // 4, dp % 4, ep // 2)
    core = ep % 2
    other = 1 - core
    whole = pl.ds(0, 4)

    loads = [
        pltpu.make_async_copy(
            pool.at[pl.ds(i * 16, 16)], pool_v.at[pl.ds(i * 16, 16)], psem.at[i]
        )
        for i in range(4)
    ]
    for load in loads:
        load.start()

    def along(axis, delta, c):
        coords = list(pos)
        coords[axis] = (coords[axis] + delta) % 4
        return (coords[0] * 4 + coords[1], coords[2] * 2 + c)

    def spec_of(order, values):
        spec = [None, None, None]
        for axis, value in zip(order, values):
            spec[axis] = value
        return tuple(spec)

    barrier = pltpu.get_barrier_semaphore()
    peers = [along(a, d, c) for a in range(3) for d in (1, 2, 3) for c in (core, other)]
    peers.append(along(0, 0, other))
    for peer in peers:
        pl.semaphore_signal(barrier, inc=1, device_id=peer, device_id_type=MESH)

    pages = table[...]
    wanted = jnp.where(pages // 128 == dp * 8 + ep, pages % 128, 0)
    wanted = jnp.sum(wanted, axis=0, keepdims=True)
    page = lax.broadcasted_iota(jnp.int32, (128, 128), 0)
    onehot = jnp.transpose(jnp.where(wanted == page, 1.0, 0.0)).astype(BF16)

    def put(cls, row, pieces):
        for j in range(0, 16, 4):
            x = jnp.concatenate(pieces(j), axis=0)
            y = lax.dot_general(onehot, x, (((1,), (1,)), ((), ())), preferred_element_type=F32)
            for i in range(4):
                stage[:, j + i, :] = y[:, i * 128 : (i + 1) * 128]
        at = pl.multiple_of(row, 16)
        block = stage[...].astype(BF16).reshape(4, 4, 4, 2, 16, 128)
        slots[cls, :, :, :, :, pl.ds(at, 16), :] = block

    def latent_rows(cls, chunk, first, count, row):
        def unit(u, _):
            def pieces(j):
                t = (first + u) * 16 + j
                return [pool_v[pl.ds(t, 4), chunk * 128 : (chunk + 1) * 128, :].reshape(512, 128)]

            put(cls, row + u * 16, pieces)
            return 0

        lax.fori_loop(0, count, unit, 0)

    def rope_rows(cls, row):
        def unit(u, _):
            def pieces(j):
                found = []
                for i in range(4):
                    found.append(pool_v[u * 16 + j + i, 512:576, :])
                    found.append(pool_v[32 + u * 16 + j + i, 512:576, :])
                return found

            put(cls, row + u * 16, pieces)
            return 0

        lax.fori_loop(0, 2, unit, 0)

    sends = []

    def remote(src, dst, ssem, rsem, peer):
        pltpu.make_async_remote_copy(
            src_ref=src, dst_ref=dst, send_sem=ssem, recv_sem=rsem,
            device_id=peer, device_id_type=MESH,
        ).start()
        sends.append((src, ssem))

    def landed(ref, sem):
        pltpu.make_async_copy(ref, ref, sem).wait()

    for part in range(3):
        rows = pl.ds(part * 32, 32)
        for load in loads[2 * part : 2 * part + 2]:
            load.wait()
        for cls, order in enumerate(ORDERS):
            a1, a2, a3 = order
            if part < 2:
                latent_rows(cls, cls, 2 * part, 2, 32 * part)
            elif cls < 2:
                latent_rows(cls, 3, 2 * cls, 2, 64)
            else:
                rope_rows(cls, 64)
            if part == 0 and cls == 0:
                pl.semaphore_wait(barrier, len(peers))
            for d in (1, 2, 3):
                src = spec_of(order, ((pos[a1] + d) % 4, whole, whole))
                dst = spec_of(order, (pos[a1], whole, whole))
                remote(
                    slots.at[(cls,) + src + (pl.ds(0, 2), rows)],
                    held1.at[(cls,) + dst + (pl.ds(0, 2), rows)],
                    send1.at[cls, d, part], recv1.at[cls, d, part], along(a1, d, core),
                )
            if part == 2:
                own = (cls,) + spec_of(order, (pos[a1], whole, whole))
                pltpu.make_async_copy(slots.at[own], held1.at[own], lsem.at[cls]).start()

    def second(cls, buf, e):
        a1, a2, a3 = order = ORDERS[cls]
        src1 = (pos[a1] + 4 - e) % 4
        for d in (1, 2, 3):
            src = spec_of(order, (src1, (pos[a2] + d) % 4, whole))
            dst = spec_of(order, (src1, pos[a2], whole))
            remote(
                buf.at[(cls,) + src], held2.at[(cls,) + dst],
                send2.at[cls, d, e], recv2.at[cls, d, e], along(a2, d, core),
            )

    def third(cls, buf, f):
        a1, a2, a3 = order = ORDERS[cls]
        src2 = (pos[a2] + 4 - f) % 4
        for d in (1, 2, 3, 0):
            for k, c in ((0, core), (1, other)):
                src = spec_of(order, (whole, src2, (pos[a3] + d) % 4))
                dst = spec_of(order, (whole, src2, pos[a3]))
                a = buf.at[(cls,) + src + (c,)]
                b = out.at[dst + (core, cls)]
                if d == 0 and k == 0:
                    pltpu.make_async_copy(a, b, csem.at[cls, f]).start()
                else:
                    remote(a, b, send3.at[cls, f, d, k], recv3.at[cls, f, d, k], along(a3, d, c))

    for cls in range(3):
        second(cls, slots, 0)
    for e in (1, 3, 2):
        for cls, order in enumerate(ORDERS):
            src1 = (pos[order[0]] + 4 - e) % 4
            at = spec_of(order, (src1, whole, whole))
            for part in range(3):
                rows = pl.ds(part * 32, 32)
                landed(held1.at[(cls,) + at + (pl.ds(0, 2), rows)], recv1.at[cls, e, part])
            second(cls, held1, e)
    for cls, order in enumerate(ORDERS):
        own = spec_of(order, (pos[order[0]], whole, whole))
        landed(held1.at[(cls,) + own], lsem.at[cls])
        third(cls, held1, 0)
    for f in (1, 3, 2):
        for cls, order in enumerate(ORDERS):
            a1, a2, a3 = order
            for e in range(4):
                at = spec_of(order, ((pos[a1] + 4 - e) % 4, (pos[a2] + 4 - f) % 4, whole))
                landed(held2.at[(cls,) + at], recv2.at[cls, f, e])
            third(cls, held2, f)
    for cls, order in enumerate(ORDERS):
        a1, a2, a3 = order
        for f in range(4):
            for d in range(4):
                for k, c in ((0, core), (1, other)):
                    at = spec_of(order, (whole, (pos[a2] + 4 - f) % 4, (pos[a3] + 4 - d) % 4))
                    ref = out.at[at + (c, cls)]
                    landed(ref, csem.at[cls, f] if d == 0 and k == 0 else recv3.at[cls, f, d, k])
    for src, ssem in sends:
        landed(src, ssem)


def exchange(table, pool):
    vmem = pl.BlockSpec(memory_space=pltpu.VMEM)
    hbm = pl.BlockSpec(memory_space=pl.ANY)
    dma = pltpu.SemaphoreType.DMA
    held = (3, 4, 4, 4, 2, 96, 128)
    return pl.pallas_call(
        exchange_kernel,
        out_shape=jax.ShapeDtypeStruct((4, 4, 4, 2, 3, 96, 128), BF16),
        in_specs=[vmem, hbm],
        out_specs=hbm,
        scratch_shapes=[
            pltpu.VMEM(pool.shape, BF16),
            pltpu.VMEM(held, BF16),
            pltpu.VMEM(held, BF16),
            pltpu.VMEM(held, BF16),
            pltpu.VMEM((128, 16, 128), F32),
            dma((4,)), dma((3,)), dma((3, 4)), dma((3, 4, 3)), dma((3, 4, 3)), dma((3, 4, 4)),
            dma((3, 4, 4)), dma((3, 4, 4, 2)), dma((3, 4, 4, 2)),
        ],
        compiler_params=pltpu.CompilerParams(
            collective_id=2, has_side_effects=True, vmem_limit_bytes=56 * 2**20
        ),
        name="exchange",
    )(table, pool)


def attend_kernel(
    table, counts, q_ref, new_ref, slots, out_ref, own_ref, keys, last, ropes, scores, sem
):
    pages = 64
    me = lax.axis_index("dp") * 8 + lax.axis_index("ep")

    def fetch(j, _):
        at = pl.multiple_of(j * PAGE, PAGE)
        slot = slots.at[table[j, me] // 128]
        pltpu.make_async_copy(
            slot.at[:, pl.ds(0, 64), :], keys.at[:, pl.ds(at, PAGE), :], sem.at[0]
        ).start()
        pltpu.make_async_copy(
            slot.at[pl.ds(0, 2), pl.ds(64, 32), :], last.at[j], sem.at[1]
        ).start()
        pltpu.make_async_copy(slot.at[2, pl.ds(64, 32), :], ropes.at[j], sem.at[2]).start()
        return 0

    lax.fori_loop(0, pages, fetch, 0)

    def clear(j, _):
        at = pl.multiple_of((pages + j) * PAGE, PAGE)
        keys[:, pl.ds(at, PAGE), :] = jnp.zeros((3, PAGE, 128), BF16)
        last[pages + j] = jnp.zeros((2, 32, 128), BF16)
        ropes[pages + j] = jnp.zeros((32, 128), BF16)
        return 0

    lax.fori_loop(0, TILE, clear, 0)
    own_ref[...] = jnp.zeros_like(own_ref)
    for step in range(2):
        fresh = new_ref[step].astype(F32)
        for r in range(4):
            own_ref[r, step : step + 1, :] = fresh[r : r + 1]
    for k, ref in enumerate(
        (keys.at[:, pl.ds(0, pages * PAGE), :], last.at[pl.ds(0, pages)], ropes.at[pl.ds(0, pages)])
    ):
        pltpu.make_async_copy(ref, ref, sem.at[k]).wait()
    width = TILE * PAGE
    step_of = lax.broadcasted_iota(jnp.int32, (128, 16), 0) // 64
    token = lax.broadcasted_iota(jnp.int32, (128, 16), 1)
    low = lax.broadcasted_iota(jnp.int32, (TILE, 32, 128), 2) < ROPE

    def values_of(page):
        at = pl.multiple_of(page * PAGE, PAGE)
        parts = [keys[k, pl.ds(at, width), :] for k in range(3)]
        parts.append(last[pl.ds(page, TILE)].reshape(width, 128))
        return jnp.concatenate(parts, axis=1)

    def request(r, start):
        q = jnp.concatenate([q_ref[0, r], q_ref[1, r]], axis=0)
        own = own_ref[r].astype(BF16)
        s_own = lax.dot_general(q, own, (((1,), (1,)), ((), ())), preferred_element_type=F32)
        s_own = jnp.where(token <= step_of, s_own * score_scale, -jnp.inf)
        q_rope = q[:, LATENT:]
        q_wide = jnp.concatenate([q[:, :LATENT], q_rope, q_rope], axis=1)
        length = counts[0, r] * PAGE
        tiles = (length + width - 1) // width

        def score(t, top):
            page = start + t * TILE
            rope = ropes[pl.ds(page, TILE)]
            zero = jnp.zeros_like(rope)
            pair = jnp.concatenate([jnp.where(low, rope, zero), jnp.where(low, zero, rope)], axis=1)
            key = jnp.concatenate([values_of(page), pair.reshape(width, 128)], axis=1)
            s = lax.dot_general(q_wide, key, (((1,), (1,)), ((), ())), preferred_element_type=F32)
            place = t * width + lax.broadcasted_iota(jnp.int32, (128, width), 1)
            s = jnp.where(place < length, s * score_scale, -jnp.inf)
            scores[t] = s
            return jnp.maximum(top, jnp.max(s, axis=1, keepdims=True))

        top = lax.fori_loop(0, tiles, score, jnp.max(s_own, axis=1, keepdims=True))
        p_own = jnp.exp(s_own - top)
        total = jnp.sum(p_own, axis=1, keepdims=True)
        acc = jnp.dot(p_own.astype(BF16), own[:, :LATENT], preferred_element_type=F32)

        def mix(t, carry):
            total, acc = carry
            p = jnp.exp(scores[t] - top)
            total = total + jnp.sum(p, axis=1, keepdims=True)
            acc = acc + jnp.dot(
                p.astype(BF16), values_of(start + t * TILE), preferred_element_type=F32
            )
            return total, acc

        total, acc = lax.fori_loop(0, tiles, mix, (total, acc))
        res = (acc / total).reshape(2, 8, 8, LATENT)
        at = pl.multiple_of(r * 16, 16)
        for g in range(8):
            block = jnp.concatenate([res[0, g], res[1, g]], axis=0)
            out_ref[g, pl.ds(at, 16), :] = block.astype(BF16)
        return start + counts[0, r]

    lax.fori_loop(0, 4, request, 0)


def attend(table, counts, queries, new_latent, slots):
    smem = pl.BlockSpec(memory_space=pltpu.SMEM)
    vmem = pl.BlockSpec(memory_space=pltpu.VMEM)
    return pl.pallas_call(
        attend_kernel,
        out_shape=jax.ShapeDtypeStruct((8, 64, LATENT), BF16),
        in_specs=[smem, smem, vmem, vmem, pl.BlockSpec(memory_space=pl.ANY)],
        out_specs=vmem,
        scratch_shapes=[
            pltpu.VMEM((4, 16, LATENT + ROPE), F32),
            pltpu.VMEM((3, (64 + TILE) * PAGE, 128), BF16),
            pltpu.VMEM((64 + TILE, 2, 32, 128), BF16),
            pltpu.VMEM((64 + TILE, 32, 128), BF16),
            pltpu.VMEM((32 // TILE, 128, TILE * PAGE), F32),
            pltpu.SemaphoreType.DMA((3,)),
        ],
        compiler_params=pltpu.CompilerParams(vmem_limit_bytes=60 * 2**20),
        name="attend",
    )(table, counts, queries, new_latent, slots)


def layer_kernel(
    attended, residual, routes, gain, router, w_uv, w_out, w_gate, w_up, w_down,
    out_ref,
    resid, member, heads_in, masked, part_out, part_in, res_all, mem_all, stat_out, stat_in, hidden,
    gath, v_uv, v_out, v_gate, v_up, v_down, acc, inner,
    mix, sib_out, sib_in, t1, ul1, ur1, t2, ul2, ur2, last, fin_out, fin_in,
    wsem, lsem, head_s, head_r, part_s, part_r, pair_s, pair_r,
    ag1_s, ag1_r, ag2_s, ag2_r, ag3_s, ag3_r, sib_s, sib_r, red_s, red_r, sum_s, sum_r,
):
    dp = lax.axis_index("dp")
    ep = lax.axis_index("ep")
    pos = (dp // 4, dp % 4, ep // 2)
    core = ep % 2
    other = 1 - core

    def device(coords, c):
        return (coords[0] * 4 + coords[1], coords[2] * 2 + c)

    def along(axis, delta):
        coords = [pos[0], pos[1], pos[2]]
        coords[axis] = (coords[axis] + delta) % 4
        return device(coords, core)

    sibling = device(pos, other)
    ep_peers = [(dp, (ep + o) % 8) for o in range(1, 8)]
    ring_peers = [along(a, d) for a in (0, 1) for d in (1, 2, 3)]

    def remote(src, dst, ssem, rsem, peer):
        copy = pltpu.make_async_remote_copy(
            src_ref=src, dst_ref=dst, send_sem=ssem, recv_sem=rsem,
            device_id=peer, device_id_type=MESH,
        )
        copy.start()
        sent.append((src, ssem))

    def landed(ref, rsem):
        pltpu.make_async_copy(ref, ref, rsem).wait()

    sent = []

    loads = [(w_uv, v_uv), (w_out, v_out), (w_gate, v_gate), (w_up, v_up), (w_down, v_down)]
    copies = [pltpu.make_async_copy(a, b, wsem.at[i]) for i, (a, b) in enumerate(loads)]
    for copy in copies:
        copy.start()

    barrier = pltpu.get_barrier_semaphore()
    for peer in ep_peers + ring_peers:
        pl.semaphore_signal(barrier, inc=1, device_id=peer, device_id_type=MESH)
    for h in range(2):
        cols = slice(h * HALF, (h + 1) * HALF)
        both = [residual[s, :, cols].astype(F32) for s in range(2)]
        resid[h] = jnp.concatenate(both, axis=0)
    route = jnp.concatenate([routes[0], routes[1]], axis=0)
    lanes = lax.broadcasted_iota(jnp.int32, (8, 128), 1)
    named = jnp.zeros((8, 128), F32)
    for k in range(8):
        named = jnp.where(route[:, k : k + 1] == lanes, 1.0, named)
    member[...] = named

    def clear(i, _):
        acc[0, i] = jnp.zeros((4, 4, 16, 256), F32)
        acc[1, i] = jnp.zeros((4, 4, 16, 256), F32)
        return 0

    lax.fori_loop(0, 4, clear, 0)
    pl.semaphore_wait(barrier, len(ep_peers) + len(ring_peers))

    for o in range(1, 8):
        to = (ep + o) % 8
        remote(attended.at[to], heads_in.at[ep], head_s.at[o], head_r.at[o], (dp, to))
    own_heads = pltpu.make_async_copy(attended.at[ep], heads_in.at[ep], lsem)
    own_heads.start()
    own_rows = pl.ds(pl.multiple_of(core * 8, 8), 8)
    other_rows = pl.ds(pl.multiple_of(other * 8, 8), 8)
    remote(resid.at[other], res_all.at[own_rows], pair_s.at[0], pair_r.at[0], sibling)
    remote(member, mem_all.at[own_rows], pair_s.at[1], pair_r.at[1], sibling)
    res_all[own_rows, :] = resid[core]
    mem_all[own_rows, :] = member[...]
    own_heads.wait()
    for o in range(1, 8):
        landed(heads_in.at[(ep + 8 - o) % 8], head_r.at[o])

    copies[0].wait()
    x = heads_in[...].reshape(512, LATENT)
    row_head = lax.broadcasted_iota(jnp.int32, (512, 128), 0) % 8
    for h in range(8):
        y = jnp.dot(x, v_uv[h], preferred_element_type=F32)
        masked[:, h * 128 : (h + 1) * 128] = jnp.where(row_head == h, y, 0.0).astype(BF16)
    to_row = lax.broadcasted_iota(jnp.int32, (64, 512), 0)
    from_row = lax.broadcasted_iota(jnp.int32, (64, 512), 1) // 8
    wanted = (to_row // 8) * 8 + (to_row % 4) * 2 + (to_row % 8) // 4
    pick = jnp.where(from_row == wanted, 1.0, 0.0).astype(BF16)
    flat = jnp.dot(pick, masked[...], preferred_element_type=F32).astype(BF16)

    copies[1].wait()
    for h in range(2):
        for t in range(HALF // 256):
            col = h * HALF + t * 256
            y = jnp.dot(flat, v_out[:, col : col + 256], preferred_element_type=F32)
            part_out[h, :, :, t * 256 : (t + 1) * 256] = y.astype(BF16).reshape(4, 16, 256)
    for o in range(1, 8):
        to = (ep + o) % 8
        remote(
            part_out.at[to % 2, to // 2], part_in.at[ep], part_s.at[o], part_r.at[o], (dp, to)
        )
    landed(res_all.at[other_rows], pair_r.at[0])
    landed(mem_all.at[other_rows], pair_r.at[1])
    hid = part_out[core, pos[2]].astype(F32)
    for o in range(1, 8):
        src = (ep + 8 - o) % 8
        landed(part_in.at[src], part_r.at[o])
        hid = hid + part_in[src].astype(F32)
    hid = hid + res_all[...]
    hidden[...] = hid

    half_cols = pl.ds(pl.multiple_of(core * HALF, 128), HALF)
    scaled = hid * gain[half_cols].reshape(1, HALF)
    stat_out[0] = jnp.zeros((16, 128), F32)
    stat_out[0, :, 0:16] = lax.dot_general(
        scaled, router[:, half_cols], (((1,), (1,)), ((), ())),
        preferred_element_type=F32, precision=lax.Precision.HIGHEST,
    )
    stat_out[1] = jnp.broadcast_to(jnp.sum(hid * hid, axis=1, keepdims=True), (16, 128))
    remote(stat_out, stat_in, pair_s.at[2], pair_r.at[2], sibling)
    landed(stat_in, pair_r.at[2])
    square = stat_out[1] + stat_in[1]
    inv = lax.rsqrt(square / (2 * HALF) + norm_eps)
    affinity = jax.nn.sigmoid((stat_out[0] + stat_in[0]) * inv) * mem_all[...]
    gates = route_scale * affinity / jnp.sum(affinity, axis=1, keepdims=True)
    coarse = gates.astype(BF16)
    fine = (gates - coarse.astype(F32)).astype(BF16)
    normed = (scaled * inv[:, 0:1]).astype(BF16)
    z, xx, yy = pos
    gath[core, 0, z, xx, yy] = normed[:, 0:640]
    gath[core, 1, z, xx, yy] = normed[:, 640:1280]
    gath[core, 2, z, xx, yy, :, 0:512] = normed[:, 1280:1792]
    gath[core, 2, z, xx, yy, :, 512:640] = jnp.where(core == 0, coarse, fine)

    whole = pl.ds(0, 4)
    halves = (pl.ds(0, 2), pl.ds(2, 2))

    def g_at(cls, spec):
        return gath.at[core, cls, spec[0], spec[1], spec[2]]

    def spec_of(order, values):
        spec = [None, None, None]
        for axis, value in zip(order, values):
            spec[axis] = value
        return spec

    def line(cls, e, f):
        a1, a2, a3 = ORDERS[cls]
        where = spec_of((a1, a2, a3), ((pos[a1] + 4 - e) % 4, (pos[a2] + 4 - f) % 4, pos[a3]))
        return g_at(cls, where)

    def quarter(cls, f, shift, half=whole):
        a1, a2, a3 = ORDERS[cls]
        at = (half, (pos[a2] + 4 - f) % 4, (pos[a3] + shift) % 4)
        return g_at(cls, spec_of((a1, a2, a3), at))

    def plane_at(cls, shift):
        a1, a2, a3 = ORDERS[cls]
        return tuple(spec_of((a1, a2, a3), (whole, whole, (pos[a3] + shift) % 4)))

    def to_pair(cls, k, shift):
        plane = gath.at[(core, cls) + plane_at(cls, shift)]
        remote(plane, plane, sib_s.at[cls, k], sib_r.at[cls, k], sibling)

    def second(cls, e):
        b = line(cls, e, 0)
        for d in (1, 3, 2):
            remote(b, b, ag2_s.at[cls, d, e], ag2_r.at[cls, d, e], along(ORDERS[cls][1], d))

    def third(cls, f):
        b = quarter(cls, f, 0)
        for k, d in ((0, 1), (1, 3)):
            remote(b, b, ag3_s.at[cls, f, k], ag3_r.at[cls, f, k], along(ORDERS[cls][2], d))

    for cls, order in enumerate(ORDERS):
        own = g_at(cls, pos)
        for d in (1, 3, 2):
            remote(own, own, ag1_s.at[cls, d], ag1_r.at[cls, d], along(order[0], d))
    for cls in range(3):
        second(cls, 0)
    for e in (1, 3, 2):
        for cls in range(3):
            landed(line(cls, e, 0), ag1_r.at[cls, e])
            second(cls, e)
    for cls in range(3):
        third(cls, 0)
    for f in (1, 3, 2):
        for cls in range(3):
            for e in range(4):
                landed(line(cls, e, f), ag2_r.at[cls, f, e])
            third(cls, f)
    for cls in range(3):
        to_pair(cls, 0, 0)
    for f in (0, 1, 3, 2):
        for cls, order in enumerate(ORDERS):
            landed(quarter(cls, f, 3), ag3_r.at[cls, f, 0])
            b = quarter(cls, f, 3, halves[0])
            remote(b, b, ag3_s.at[cls, f, 2], ag3_r.at[cls, f, 2], along(order[2], 1))
            landed(quarter(cls, f, 1), ag3_r.at[cls, f, 1])
            b = quarter(cls, f, 1, halves[1])
            remote(b, b, ag3_s.at[cls, f, 3], ag3_r.at[cls, f, 3], along(order[2], 3))
    for k, shift in ((1, 3), (2, 1)):
        for cls in range(3):
            to_pair(cls, k, shift)

    for copy in copies[2:]:
        copy.wait()

    def expert_in(h, cls, shift):
        at = plane_at(cls, shift)
        n = WIDTHS[cls]
        x = gath[(h, cls) + at].reshape(256, PART)[:, :n]
        rows = pl.ds(pl.multiple_of(h * HALF + cls * PART, 128), n)
        for k, w in enumerate((v_gate, v_up)):
            y = jnp.dot(x, w[0, rows, :], preferred_element_type=F32).reshape(4, 4, 16, 256)
            acc[(k,) + at] = acc[(k,) + at] + y

    def from_pair(cls, k, shift):
        landed(gath.at[(other, cls) + plane_at(cls, shift)], sib_r.at[cls, k])

    for cls in range(3):
        expert_in(core, cls, 0)
    for cls in range(3):
        from_pair(cls, 0, 0)
        expert_in(other, cls, 0)
    for k, shift in ((1, 3), (2, 1)):
        for cls in range(3):
            expert_in(core, cls, shift)
    for cls in range(3):
        for f in range(4):
            landed(quarter(cls, f, 2, halves[0]), ag3_r.at[cls, f, 2])
            landed(quarter(cls, f, 2, halves[1]), ag3_r.at[cls, f, 3])
        to_pair(cls, 3, 2)
    for k, shift in ((1, 3), (2, 1)):
        for cls in range(3):
            from_pair(cls, k, shift)
            expert_in(other, cls, shift)
    for cls in range(3):
        expert_in(core, cls, 2)
    for cls in range(3):
        from_pair(cls, 3, 2)
        expert_in(other, cls, 2)

    lane = lax.broadcasted_iota(jnp.int32, (256, 128), 1)

    def activate(i, _):
        both = gath[0, 2, i, :, :, :, 512:640].astype(F32) + gath[1, 2, i, :, :, :, 512:640].astype(F32)
        weight = jnp.sum(jnp.where(lane == dp, both.reshape(256, 128), 0.0), axis=1, keepdims=True)
        gate = acc[0, i].reshape(256, 256)
        act = gate / (1.0 + jnp.exp(-gate)) * acc[1, i].reshape(256, 256) * weight
        inner[i] = act.astype(BF16).reshape(4, 4, 16, 256)
        return 0

    lax.fori_loop(0, 4, activate, 0)

    def expert_out(half, cls, at):
        cols = pl.ds(pl.multiple_of(half * HALF + cls * PART, 128), WIDTHS[cls])
        act = inner[at].reshape(256, 256)
        y = jnp.dot(act, v_down[0, :, cols], preferred_element_type=F32)
        return y.reshape(4, 4, 16, WIDTHS[cls])

    def for_pair(shift):
        for cls in range(3):
            at = plane_at(cls, shift)
            b = (cls,) + at + (slice(None), pl.ds(0, WIDTHS[cls]))
            sib_out[b] = expert_out(other, cls, at).astype(BF16)
            remote(sib_out.at[b], sib_in.at[b], red_s.at[cls, shift], red_r.at[cls, shift], sibling)

    def for_self(shift):
        for cls in range(3):
            at = plane_at(cls, shift)
            b = (cls,) + at + (slice(None), pl.ds(0, WIDTHS[cls]))
            y = expert_out(core, cls, at)
            landed(sib_in.at[b], red_r.at[cls, shift])
            mix[b] = (y + sib_in[b].astype(F32)).astype(BF16)

    for phase in (2, 1):
        bt, bl, br = (t1, ul1, ur1) if phase == 2 else (t2, ul2, ur2)
        red = 0 if phase == 2 else 1

        def block(cls, shift, half):
            a1, a2, a3 = ORDERS[cls]
            if phase == 1:
                spec = spec_of((a1, a2, a3), (half, (pos[a2] + shift) % 4, pos[a3]))
            else:
                spec = spec_of((a1, a2, a3), (half, whole, (pos[a3] + shift) % 4))
            return (cls, spec[0], spec[1], spec[2], slice(None), pl.ds(0, WIDTHS[cls]))

        def temp(cls, half):
            a1, a2, a3 = ORDERS[cls]
            if phase == 1:
                return (cls, half, slice(None), pl.ds(0, WIDTHS[cls]))
            if a1 < a2:
                return (cls, half, whole, slice(None), pl.ds(0, WIDTHS[cls]))
            return (cls, whole, half, slice(None), pl.ds(0, WIDTHS[cls]))

        def send(cls, shift, half, buf, k, delta):
            remote(
                mix.at[block(cls, shift, halves[half])], buf.at[temp(cls, halves[half])],
                sum_s.at[cls, red, k], sum_r.at[cls, red, k], along(ORDERS[cls][phase], delta),
            )

        if phase == 2:
            for_pair(2)
            for_pair(1)
            for_self(2)
        for cls in range(3):
            send(cls, 2, 0, bt, 0, 1)
            send(cls, 2, 1, bt, 1, 3)
        if phase == 2:
            for_pair(3)
            for_self(1)
        for cls in range(3):
            send(cls, 1, 1, bl, 2, 1)
        if phase == 2:
            for_self(3)
        for cls in range(3):
            send(cls, 3, 0, br, 3, 3)
        for cls in range(3):
            for half, shift, buf, k, delta in ((0, 1, bl, 0, 1), (1, 3, br, 1, 3)):
                at, tmp = block(cls, shift, halves[half]), temp(cls, halves[half])
                landed(bt.at[tmp], sum_r.at[cls, red, k])
                mix[at] = (mix[at].astype(F32) + bt[tmp].astype(F32)).astype(BF16)
                send(cls, shift, half, buf, k + 4, delta)
        if phase == 2:
            for_pair(0)
            for_self(0)
        for cls in range(3):
            for half, ks in ((0, (4, 3)), (1, (2, 5))):
                at, tmp = block(cls, 0, halves[half]), temp(cls, halves[half])
                landed(bl.at[tmp], sum_r.at[cls, red, ks[0]])
                landed(br.at[tmp], sum_r.at[cls, red, ks[1]])
                total = mix[at].astype(F32) + bl[tmp].astype(F32) + br[tmp].astype(F32)
                mix[at] = total.astype(BF16)

    for cls, order in enumerate(ORDERS):
        a1 = order[0]
        for d in (1, 2, 3):
            coords = list(pos)
            coords[a1] = (pos[a1] + d) % 4
            src = mix.at[cls, coords[0], coords[1], coords[2], :, pl.ds(0, WIDTHS[cls])]
            dst = last.at[cls, d - 1, :, pl.ds(0, WIDTHS[cls])]
            remote(src, dst, sum_s.at[cls, 2, d], sum_r.at[cls, 2, d], along(a1, d))
    for cls in range(3):
        n = WIDTHS[cls]
        total = mix[cls, pos[0], pos[1], pos[2], :, 0:n].astype(F32)
        for d in (1, 2, 3):
            landed(last.at[cls, d - 1, :, pl.ds(0, n)], sum_r.at[cls, 2, d])
            total = total + last[cls, d - 1, :, 0:n].astype(F32)
        total = total + hidden[:, cls * PART : cls * PART + n]
        fin_out[0, :, cls * PART : cls * PART + n] = total[0:8]
        fin_out[1, :, cls * PART : cls * PART + n] = total[8:16]
    remote(fin_out.at[other], fin_in, pair_s.at[3], pair_r.at[3], sibling)
    for s in range(2):
        out_ref[s, :, half_cols] = fin_out[core, s * 4 : s * 4 + 4].astype(BF16)
    landed(fin_in, pair_r.at[3])
    for s in range(2):
        cols = pl.ds(pl.multiple_of(other * HALF, 128), HALF)
        out_ref[s, :, cols] = fin_in[s * 4 : s * 4 + 4].astype(BF16)
    for src, ssem in sent:
        pltpu.make_async_copy(src, src, ssem).wait()


def layer(attended, residual, routes, gain, router, w_uv, w_out, w_gate, w_up, w_down):
    vmem = pl.BlockSpec(memory_space=pltpu.VMEM)
    hbm = pl.BlockSpec(memory_space=pl.ANY)
    dma = pltpu.SemaphoreType.DMA
    grid = (3, 4, 4, 4, 16, PART)
    return pl.pallas_call(
        layer_kernel,
        out_shape=jax.ShapeDtypeStruct((2, 4, 2 * HALF), BF16),
        in_specs=[vmem] * 5 + [hbm] * 5,
        out_specs=vmem,
        scratch_shapes=[
            pltpu.VMEM((2, 8, HALF), F32),
            pltpu.VMEM((8, 128), F32),
            pltpu.VMEM((8, 64, LATENT), BF16),
            pltpu.VMEM((512, 1024), BF16),
            pltpu.VMEM((2, 4, 16, HALF), BF16),
            pltpu.VMEM((8, 16, HALF), BF16),
            pltpu.VMEM((16, HALF), F32),
            pltpu.VMEM((16, 128), F32),
            pltpu.VMEM((2, 16, 128), F32),
            pltpu.VMEM((2, 16, 128), F32),
            pltpu.VMEM((16, HALF), F32),
            pltpu.VMEM((2,) + grid, BF16),
            pltpu.VMEM(w_uv.shape, BF16),
            pltpu.VMEM(w_out.shape, BF16),
            pltpu.VMEM(w_gate.shape, BF16),
            pltpu.VMEM(w_up.shape, BF16),
            pltpu.VMEM(w_down.shape, BF16),
            pltpu.VMEM((2, 4, 4, 4, 16, 256), F32),
            pltpu.VMEM((4, 4, 4, 16, 256), BF16),
            pltpu.VMEM(grid, BF16),
            pltpu.VMEM(grid, BF16),
            pltpu.VMEM(grid, BF16),
            pltpu.VMEM((3, 4, 4, 16, PART), BF16),
            pltpu.VMEM((3, 4, 4, 16, PART), BF16),
            pltpu.VMEM((3, 4, 4, 16, PART), BF16),
            pltpu.VMEM((3, 4, 16, PART), BF16),
            pltpu.VMEM((3, 4, 16, PART), BF16),
            pltpu.VMEM((3, 4, 16, PART), BF16),
            pltpu.VMEM((3, 3, 16, PART), BF16),
            pltpu.VMEM((2, 8, HALF), F32),
            pltpu.VMEM((8, HALF), F32),
            dma((5,)), dma, dma((8,)), dma((8,)), dma((8,)), dma((8,)), dma((4,)), dma((4,)),
            dma((3, 4)), dma((3, 4)), dma((3, 4, 4)), dma((3, 4, 4)), dma((3, 4, 4)), dma((3, 4, 4)),
            dma((3, 4)), dma((3, 4)), dma((3, 4)), dma((3, 4)),
            dma((3, 3, 6)), dma((3, 3, 6)),
        ],
        compiler_params=pltpu.CompilerParams(
            collective_id=1, has_side_effects=True, vmem_limit_bytes=56 * 2**20
        ),
        name="layer",
    )(attended, residual, routes, gain, router, w_uv, w_out, w_gate, w_up, w_down)


def shards(
    cache_pool,
    page_table,
    page_counts,
    queries,
    new_latent,
    residual,
    w_uv,
    w_out,
    norm_gain,
    w_router,
    w_gate,
    w_up,
    w_down,
    routes,
):
    table = page_table.T
    incoming = exchange(table, jnp.transpose(cache_pool, (1, 2, 0))).reshape(-1, 3, 96, 128)
    attended = attend(table, page_counts, queries, new_latent, incoming)
    return layer(
        attended, residual, routes, norm_gain, w_router.T, w_uv, w_out, w_gate, w_up, w_down
    )


def solution(mesh):
    return jax.shard_map(
        shards,
        mesh=mesh,
        in_specs=(
            P(("dp", "ep"), None, None),
            P(),
            P(("dp", "ep"), None),
            P(None, ("dp", "ep"), None, None),
            P(None, ("dp", "ep"), None),
            P(None, ("dp", "ep"), None),
            P("ep", None, None),
            P("ep", None),
            P(),
            P(),
            P("dp", None, "ep"),
            P("dp", None, "ep"),
            P("dp", "ep", None),
            P(None, ("dp", "ep"), None),
        ),
        out_specs=P(None, ("dp", "ep"), None),
        check_vma=False,
    )
```

```python
import functools

import jax
import jax.numpy as jnp
from jax import lax
from jax.experimental import pallas as pl
from jax.experimental.pallas import tpu as pltpu
from jax.sharding import PartitionSpec as P

MESH = pl.DeviceIdType.MESH
F32 = jnp.float32
BF16 = jnp.bfloat16

LATENT = 512
ROPE = 64
PAGE = 64
TILE = 16
score_scale = 192.0 ** (-0.5)
route_scale = 2.5
norm_eps = 1e-06

HALF = 1792
PART = 640
ORDERS = ((0, 1, 2), (1, 2, 0), (2, 0, 1))
WIDTHS = (640, 640, 512)


def exchange_kernel(
    table, pool, out,
    pool_v, slots, held1, held2, stage,
    psem, lsem, csem, send1, recv1, send2, recv2, send3, recv3,
):
    dp = lax.axis_index("dp")
    ep = lax.axis_index("ep")
    pos = (dp // 4, dp % 4, ep // 2)
    core = ep % 2
    other = 1 - core
    whole = pl.ds(0, 4)

    loads = [
        pltpu.make_async_copy(
            pool.at[pl.ds(i * 16, 16)], pool_v.at[pl.ds(i * 16, 16)], psem.at[i]
        )
        for i in range(4)
    ]
    for load in loads:
        load.start()

    def along(axis, delta, c):
        coords = list(pos)
        coords[axis] = (coords[axis] + delta) % 4
        return (coords[0] * 4 + coords[1], coords[2] * 2 + c)

    def spec_of(order, values):
        spec = [None, None, None]
        for axis, value in zip(order, values):
            spec[axis] = value
        return tuple(spec)

    barrier = pltpu.get_barrier_semaphore()
    peers = [along(a, d, c) for a in range(3) for d in (1, 2, 3) for c in (core, other)]
    peers.append(along(0, 0, other))
    for peer in peers:
        pl.semaphore_signal(barrier, inc=1, device_id=peer, device_id_type=MESH)

    pages = table[...]
    wanted = jnp.where(pages // 128 == dp * 8 + ep, pages % 128, 0)
    wanted = jnp.sum(wanted, axis=0, keepdims=True)
    page = lax.broadcasted_iota(jnp.int32, (128, 128), 0)
    onehot = jnp.transpose(jnp.where(wanted == page, 1.0, 0.0)).astype(BF16)

    def put(cls, row, pieces):
        for j in range(0, 16, 4):
            x = jnp.concatenate(pieces(j), axis=0)
            y = lax.dot_general(onehot, x, (((1,), (1,)), ((), ())), preferred_element_type=F32)
            for i in range(4):
                stage[:, j + i, :] = y[:, i * 128 : (i + 1) * 128]
        block = stage[...].astype(BF16).reshape(4, 4, 4, 2, 16, 128)
        slots[cls, :, :, :, :, row : row + 16, :] = block

    def latent_rows(cls, chunk, unit, row):
        def pieces(j):
            t = unit * 16 + j
            return [pool_v[pl.ds(t, 4), chunk * 128 : (chunk + 1) * 128, :].reshape(512, 128)]

        put(cls, row, pieces)

    def rope_rows(cls, unit, row):
        def pieces(j):
            found = []
            for i in range(4):
                found.append(pool_v[unit * 16 + j + i, 512:576, :])
                found.append(pool_v[32 + unit * 16 + j + i, 512:576, :])
            return found

        put(cls, row, pieces)

    sends = []

    def remote(src, dst, ssem, rsem, peer):
        pltpu.make_async_remote_copy(
            src_ref=src, dst_ref=dst, send_sem=ssem, recv_sem=rsem,
            device_id=peer, device_id_type=MESH,
        ).start()
        sends.append((src, ssem))

    def landed(ref, sem):
        pltpu.make_async_copy(ref, ref, sem).wait()

    for part in range(6):
        rows = pl.ds(part * 16, 16)
        if part < 4:
            loads[part].wait()
        for cls, order in enumerate(ORDERS):
            a1, a2, a3 = order
            if part < 4:
                latent_rows(cls, cls, part, 16 * part)
            elif cls < 2:
                latent_rows(cls, 3, 2 * cls + part - 4, 16 * part)
            else:
                rope_rows(cls, part - 4, 16 * part)
            if part == 0 and cls == 0:
                pl.semaphore_wait(barrier, len(peers))
            for d in (1, 2, 3):
                src = spec_of(order, ((pos[a1] + d) % 4, whole, whole))
                dst = spec_of(order, (pos[a1], whole, whole))
                remote(
                    slots.at[(cls,) + src + (pl.ds(0, 2), rows)],
                    held1.at[(cls,) + dst + (pl.ds(0, 2), rows)],
                    send1.at[cls, d, part], recv1.at[cls, d, part], along(a1, d, core),
                )
            if part == 5:
                own = (cls,) + spec_of(order, (pos[a1], whole, whole))
                pltpu.make_async_copy(slots.at[own], held1.at[own], lsem.at[cls]).start()

    def second(cls, buf, e):
        a1, a2, a3 = order = ORDERS[cls]
        src1 = (pos[a1] + 4 - e) % 4
        for d in (1, 2, 3):
            src = spec_of(order, (src1, (pos[a2] + d) % 4, whole))
            dst = spec_of(order, (src1, pos[a2], whole))
            remote(
                buf.at[(cls,) + src], held2.at[(cls,) + dst],
                send2.at[cls, d, e], recv2.at[cls, d, e], along(a2, d, core),
            )

    def third(cls, buf, f):
        a1, a2, a3 = order = ORDERS[cls]
        src2 = (pos[a2] + 4 - f) % 4
        for d in (1, 2, 3, 0):
            for k, c in ((0, core), (1, other)):
                src = spec_of(order, (whole, src2, (pos[a3] + d) % 4))
                dst = spec_of(order, (whole, src2, pos[a3]))
                a = buf.at[(cls,) + src + (c,)]
                b = out.at[dst + (core, cls)]
                if d == 0 and k == 0:
                    pltpu.make_async_copy(a, b, csem.at[cls, f]).start()
                else:
                    remote(a, b, send3.at[cls, f, d, k], recv3.at[cls, f, d, k], along(a3, d, c))

    for cls in range(3):
        second(cls, slots, 0)
    for e in (1, 3, 2):
        for cls, order in enumerate(ORDERS):
            src1 = (pos[order[0]] + 4 - e) % 4
            at = spec_of(order, (src1, whole, whole))
            for part in range(6):
                rows = pl.ds(part * 16, 16)
                landed(held1.at[(cls,) + at + (pl.ds(0, 2), rows)], recv1.at[cls, e, part])
            second(cls, held1, e)
    for cls, order in enumerate(ORDERS):
        own = spec_of(order, (pos[order[0]], whole, whole))
        landed(held1.at[(cls,) + own], lsem.at[cls])
        third(cls, held1, 0)
    for f in (1, 3, 2):
        for cls, order in enumerate(ORDERS):
            a1, a2, a3 = order
            for e in range(4):
                at = spec_of(order, ((pos[a1] + 4 - e) % 4, (pos[a2] + 4 - f) % 4, whole))
                landed(held2.at[(cls,) + at], recv2.at[cls, f, e])
            third(cls, held2, f)
    for cls, order in enumerate(ORDERS):
        a1, a2, a3 = order
        for f in range(4):
            for d in range(4):
                for k, c in ((0, core), (1, other)):
                    at = spec_of(order, (whole, (pos[a2] + 4 - f) % 4, (pos[a3] + 4 - d) % 4))
                    ref = out.at[at + (c, cls)]
                    landed(ref, csem.at[cls, f] if d == 0 and k == 0 else recv3.at[cls, f, d, k])
    for src, ssem in sends:
        landed(src, ssem)


def exchange(table, pool):
    vmem = pl.BlockSpec(memory_space=pltpu.VMEM)
    hbm = pl.BlockSpec(memory_space=pl.ANY)
    dma = pltpu.SemaphoreType.DMA
    held = (3, 4, 4, 4, 2, 96, 128)
    return pl.pallas_call(
        exchange_kernel,
        out_shape=jax.ShapeDtypeStruct((4, 4, 4, 2, 3, 96, 128), BF16),
        in_specs=[vmem, hbm],
        out_specs=hbm,
        scratch_shapes=[
            pltpu.VMEM(pool.shape, BF16),
            pltpu.VMEM(held, BF16),
            pltpu.VMEM(held, BF16),
            pltpu.VMEM(held, BF16),
            pltpu.VMEM((128, 16, 128), F32),
            dma((4,)), dma((3,)), dma((3, 4)), dma((3, 4, 6)), dma((3, 4, 6)), dma((3, 4, 4)),
            dma((3, 4, 4)), dma((3, 4, 4, 2)), dma((3, 4, 4, 2)),
        ],
        compiler_params=pltpu.CompilerParams(
            collective_id=2, has_side_effects=True, vmem_limit_bytes=56 * 2**20
        ),
        name="exchange",
    )(table, pool)


def attend_kernel(
    table, counts, q_ref, new_ref, slots, out_ref, own_ref, keys, scores, sem
):
    pages = 64
    me = lax.axis_index("dp") * 8 + lax.axis_index("ep")

    def fetch(j, _):
        pltpu.make_async_copy(slots.at[table[j, me] // 128], keys.at[j], sem).start()
        return 0

    lax.fori_loop(0, pages, fetch, 0)

    def clear(j, _):
        keys[pages + j] = jnp.zeros((3, 96, 128), BF16)
        return 0

    lax.fori_loop(0, TILE, clear, 0)
    own_ref[...] = jnp.zeros_like(own_ref)
    for step in range(2):
        fresh = new_ref[step].astype(F32)
        for r in range(4):
            own_ref[r, step : step + 1, :] = fresh[r : r + 1]
    filled = keys.at[pl.ds(0, pages)]
    pltpu.make_async_copy(filled, filled, sem).wait()
    width = TILE * PAGE
    step_of = lax.broadcasted_iota(jnp.int32, (128, 16), 0) // 64
    token = lax.broadcasted_iota(jnp.int32, (128, 16), 1)
    low = lax.broadcasted_iota(jnp.int32, (TILE, 32, 128), 2) < ROPE

    def values_of(page):
        parts = [keys[pl.ds(page, TILE), k, 0:64, :].reshape(width, 128) for k in range(3)]
        parts.append(keys[pl.ds(page, TILE), 0:2, 64:96, :].reshape(width, 128))
        return jnp.concatenate(parts, axis=1)

    def request(r, start):
        q = jnp.concatenate([q_ref[0, r], q_ref[1, r]], axis=0)
        own = own_ref[r].astype(BF16)
        s_own = lax.dot_general(q, own, (((1,), (1,)), ((), ())), preferred_element_type=F32)
        s_own = jnp.where(token <= step_of, s_own * score_scale, -jnp.inf)
        q_rope = q[:, LATENT:]
        q_wide = jnp.concatenate([q[:, :LATENT], q_rope, q_rope], axis=1)
        length = counts[0, r] * PAGE
        tiles = (length + width - 1) // width

        def score(t, top):
            page = start + t * TILE
            rope = keys[pl.ds(page, TILE), 2, 64:96, :]
            zero = jnp.zeros_like(rope)
            pair = jnp.concatenate([jnp.where(low, rope, zero), jnp.where(low, zero, rope)], axis=1)
            key = jnp.concatenate([values_of(page), pair.reshape(width, 128)], axis=1)
            s = lax.dot_general(q_wide, key, (((1,), (1,)), ((), ())), preferred_element_type=F32)
            place = t * width + lax.broadcasted_iota(jnp.int32, (128, width), 1)
            s = jnp.where(place < length, s * score_scale, -jnp.inf)
            scores[t] = s
            return jnp.maximum(top, jnp.max(s, axis=1, keepdims=True))

        top = lax.fori_loop(0, tiles, score, jnp.max(s_own, axis=1, keepdims=True))
        p_own = jnp.exp(s_own - top)
        total = jnp.sum(p_own, axis=1, keepdims=True)
        acc = jnp.dot(p_own.astype(BF16), own[:, :LATENT], preferred_element_type=F32)

        def mix(t, carry):
            total, acc = carry
            p = jnp.exp(scores[t] - top)
            total = total + jnp.sum(p, axis=1, keepdims=True)
            acc = acc + jnp.dot(
                p.astype(BF16), values_of(start + t * TILE), preferred_element_type=F32
            )
            return total, acc

        total, acc = lax.fori_loop(0, tiles, mix, (total, acc))
        res = (acc / total).reshape(2, 8, 8, LATENT)
        at = pl.multiple_of(r * 16, 16)
        for g in range(8):
            block = jnp.concatenate([res[0, g], res[1, g]], axis=0)
            out_ref[g, pl.ds(at, 16), :] = block.astype(BF16)
        return start + counts[0, r]

    lax.fori_loop(0, 4, request, 0)


def attend(table, counts, queries, new_latent, slots):
    smem = pl.BlockSpec(memory_space=pltpu.SMEM)
    vmem = pl.BlockSpec(memory_space=pltpu.VMEM)
    return pl.pallas_call(
        attend_kernel,
        out_shape=jax.ShapeDtypeStruct((8, 64, LATENT), BF16),
        in_specs=[smem, smem, vmem, vmem, pl.BlockSpec(memory_space=pl.ANY)],
        out_specs=vmem,
        scratch_shapes=[
            pltpu.VMEM((4, 16, LATENT + ROPE), F32),
            pltpu.VMEM((64 + TILE, 3, 96, 128), BF16),
            pltpu.VMEM((32 // TILE, 128, TILE * PAGE), F32),
            pltpu.SemaphoreType.DMA,
        ],
        compiler_params=pltpu.CompilerParams(vmem_limit_bytes=60 * 2**20),
        name="attend",
    )(table, counts, queries, new_latent, slots)


def layer_kernel(
    attended, residual, routes, gain, router, w_uv, w_out, w_gate, w_up, w_down,
    out_ref,
    resid, member, heads_in, masked, part_out, part_in, res_all, mem_all, stat_out, stat_in, hidden,
    gath, v_uv, v_out, v_gate, v_up, v_down, acc, inner,
    mix, sib_out, sib_in, t1, ul1, ur1, t2, last, fin_out, fin_in,
    wsem, lsem, head_s, head_r, part_s, part_r, pair_s, pair_r,
    ag1_s, ag1_r, ag2_s, ag2_r, ag3_s, ag3_r, sib_s, sib_r, red_s, red_r, sum_s, sum_r,
):
    dp = lax.axis_index("dp")
    ep = lax.axis_index("ep")
    pos = (dp // 4, dp % 4, ep // 2)
    core = ep % 2
    other = 1 - core

    def device(coords, c):
        return (coords[0] * 4 + coords[1], coords[2] * 2 + c)

    def along(axis, delta):
        coords = [pos[0], pos[1], pos[2]]
        coords[axis] = (coords[axis] + delta) % 4
        return device(coords, core)

    sibling = device(pos, other)
    ep_peers = [(dp, (ep + o) % 8) for o in range(1, 8)]
    ring_peers = [along(a, d) for a in (0, 1) for d in (1, 2, 3)]

    def remote(src, dst, ssem, rsem, peer):
        copy = pltpu.make_async_remote_copy(
            src_ref=src, dst_ref=dst, send_sem=ssem, recv_sem=rsem,
            device_id=peer, device_id_type=MESH,
        )
        copy.start()
        sent.append((src, ssem))

    def landed(ref, rsem):
        pltpu.make_async_copy(ref, ref, rsem).wait()

    sent = []

    loads = [(w_uv, v_uv), (w_out, v_out), (w_gate, v_gate), (w_up, v_up), (w_down, v_down)]
    copies = [pltpu.make_async_copy(a, b, wsem.at[i]) for i, (a, b) in enumerate(loads)]
    for copy in copies:
        copy.start()

    barrier = pltpu.get_barrier_semaphore()
    for peer in ep_peers + ring_peers:
        pl.semaphore_signal(barrier, inc=1, device_id=peer, device_id_type=MESH)
    for h in range(2):
        cols = slice(h * HALF, (h + 1) * HALF)
        both = [residual[s, :, cols].astype(F32) for s in range(2)]
        resid[h] = jnp.concatenate(both, axis=0)
    route = jnp.concatenate([routes[0], routes[1]], axis=0)
    lanes = lax.broadcasted_iota(jnp.int32, (8, 128), 1)
    named = jnp.zeros((8, 128), F32)
    for k in range(8):
        named = jnp.where(route[:, k : k + 1] == lanes, 1.0, named)
    member[...] = named

    def clear(i, _):
        acc[0, i] = jnp.zeros((4, 4, 16, 256), F32)
        acc[1, i] = jnp.zeros((4, 4, 16, 256), F32)
        return 0

    lax.fori_loop(0, 4, clear, 0)
    pl.semaphore_wait(barrier, len(ep_peers) + len(ring_peers))

    for o in range(1, 8):
        to = (ep + o) % 8
        remote(attended.at[to], heads_in.at[ep], head_s.at[o], head_r.at[o], (dp, to))
    own_heads = pltpu.make_async_copy(attended.at[ep], heads_in.at[ep], lsem)
    own_heads.start()
    own_rows = pl.ds(pl.multiple_of(core * 8, 8), 8)
    other_rows = pl.ds(pl.multiple_of(other * 8, 8), 8)
    remote(resid.at[other], res_all.at[own_rows], pair_s.at[0], pair_r.at[0], sibling)
    remote(member, mem_all.at[own_rows], pair_s.at[1], pair_r.at[1], sibling)
    res_all[own_rows, :] = resid[core]
    mem_all[own_rows, :] = member[...]
    own_heads.wait()
    for o in range(1, 8):
        landed(heads_in.at[(ep + 8 - o) % 8], head_r.at[o])

    copies[0].wait()
    x = heads_in[...].reshape(512, LATENT)
    row_head = lax.broadcasted_iota(jnp.int32, (512, 128), 0) % 8
    for h in range(8):
        y = jnp.dot(x, v_uv[h], preferred_element_type=F32)
        masked[:, h * 128 : (h + 1) * 128] = jnp.where(row_head == h, y, 0.0).astype(BF16)
    to_row = lax.broadcasted_iota(jnp.int32, (64, 512), 0)
    from_row = lax.broadcasted_iota(jnp.int32, (64, 512), 1) // 8
    wanted = (to_row // 8) * 8 + (to_row % 4) * 2 + (to_row % 8) // 4
    pick = jnp.where(from_row == wanted, 1.0, 0.0).astype(BF16)
    flat = jnp.dot(pick, masked[...], preferred_element_type=F32).astype(BF16)

    copies[1].wait()
    for h, turns in ((other, (1, 3, 5, 7)), (core, (2, 4, 6))):
        for t in range(HALF // 256):
            cols = pl.ds(pl.multiple_of(h * HALF + t * 256, 256), 256)
            y = jnp.dot(flat, v_out[:, cols], preferred_element_type=F32)
            part_out[h, :, :, t * 256 : (t + 1) * 256] = y.astype(BF16).reshape(4, 16, 256)
        for o in turns:
            to = (ep + o) % 8
            remote(part_out.at[h, to // 2], part_in.at[ep], part_s.at[o], part_r.at[o], (dp, to))
    landed(res_all.at[other_rows], pair_r.at[0])
    landed(mem_all.at[other_rows], pair_r.at[1])
    hid = part_out[core, pos[2]].astype(F32)
    for o in range(1, 8):
        src = (ep + 8 - o) % 8
        landed(part_in.at[src], part_r.at[o])
        hid = hid + part_in[src].astype(F32)
    hid = hid + res_all[...]
    hidden[...] = hid

    half_cols = pl.ds(pl.multiple_of(core * HALF, 128), HALF)
    scaled = hid * gain[half_cols].reshape(1, HALF)
    stat_out[0] = jnp.zeros((16, 128), F32)
    stat_out[0, :, 0:16] = lax.dot_general(
        scaled, router[:, half_cols], (((1,), (1,)), ((), ())),
        preferred_element_type=F32, precision=lax.Precision.HIGHEST,
    )
    stat_out[1] = jnp.broadcast_to(jnp.sum(hid * hid, axis=1, keepdims=True), (16, 128))
    remote(stat_out, stat_in, pair_s.at[2], pair_r.at[2], sibling)
    landed(stat_in, pair_r.at[2])
    square = stat_out[1] + stat_in[1]
    inv = lax.rsqrt(square / (2 * HALF) + norm_eps)
    affinity = jax.nn.sigmoid((stat_out[0] + stat_in[0]) * inv) * mem_all[...]
    gates = route_scale * affinity / jnp.sum(affinity, axis=1, keepdims=True)
    coarse = gates.astype(BF16)
    fine = (gates - coarse.astype(F32)).astype(BF16)
    normed = (scaled * inv[:, 0:1]).astype(BF16)
    z, xx, yy = pos
    gath[core, 0, z, xx, yy] = normed[:, 0:640]
    gath[core, 1, z, xx, yy] = normed[:, 640:1280]
    gath[core, 2, z, xx, yy, :, 0:512] = normed[:, 1280:1792]
    gath[core, 2, z, xx, yy, :, 512:640] = jnp.where(core == 0, coarse, fine)

    whole = pl.ds(0, 4)
    halves = (pl.ds(0, 2), pl.ds(2, 2))

    def g_at(cls, spec):
        return gath.at[core, cls, spec[0], spec[1], spec[2]]

    def spec_of(order, values):
        spec = [None, None, None]
        for axis, value in zip(order, values):
            spec[axis] = value
        return spec

    def line(cls, e, f):
        a1, a2, a3 = ORDERS[cls]
        where = spec_of((a1, a2, a3), ((pos[a1] + 4 - e) % 4, (pos[a2] + 4 - f) % 4, pos[a3]))
        return g_at(cls, where)

    def quarter(cls, f, shift, half=whole):
        a1, a2, a3 = ORDERS[cls]
        at = (half, (pos[a2] + 4 - f) % 4, (pos[a3] + shift) % 4)
        return g_at(cls, spec_of((a1, a2, a3), at))

    def plane_at(cls, shift):
        a1, a2, a3 = ORDERS[cls]
        return tuple(spec_of((a1, a2, a3), (whole, whole, (pos[a3] + shift) % 4)))

    def to_pair(cls, k, shift):
        plane = gath.at[(core, cls) + plane_at(cls, shift)]
        remote(plane, plane, sib_s.at[cls, k], sib_r.at[cls, k], sibling)

    def second(cls, e):
        b = line(cls, e, 0)
        for d in (1, 3, 2):
            remote(b, b, ag2_s.at[cls, d, e], ag2_r.at[cls, d, e], along(ORDERS[cls][1], d))

    def third(cls, f):
        b = quarter(cls, f, 0)
        for k, d in ((0, 1), (1, 3)):
            remote(b, b, ag3_s.at[cls, f, k], ag3_r.at[cls, f, k], along(ORDERS[cls][2], d))

    for cls, order in enumerate(ORDERS):
        own = g_at(cls, pos)
        for d in (1, 3, 2):
            remote(own, own, ag1_s.at[cls, d], ag1_r.at[cls, d], along(order[0], d))
    for cls in range(3):
        second(cls, 0)
    for e in (1, 3, 2):
        for cls in range(3):
            landed(line(cls, e, 0), ag1_r.at[cls, e])
            second(cls, e)
    for cls in range(3):
        third(cls, 0)
    for f in (1, 3, 2):
        for cls in range(3):
            for e in range(4):
                landed(line(cls, e, f), ag2_r.at[cls, f, e])
            third(cls, f)
    for cls in range(3):
        to_pair(cls, 0, 0)
    for f in (0, 1, 3, 2):
        for cls, order in enumerate(ORDERS):
            landed(quarter(cls, f, 3), ag3_r.at[cls, f, 0])
            b = quarter(cls, f, 3, halves[0])
            remote(b, b, ag3_s.at[cls, f, 2], ag3_r.at[cls, f, 2], along(order[2], 1))
            landed(quarter(cls, f, 1), ag3_r.at[cls, f, 1])
            b = quarter(cls, f, 1, halves[1])
            remote(b, b, ag3_s.at[cls, f, 3], ag3_r.at[cls, f, 3], along(order[2], 3))
    for k, shift in ((1, 3), (2, 1)):
        for cls in range(3):
            to_pair(cls, k, shift)

    for copy in copies[2:]:
        copy.wait()

    def expert_in(h, cls, shift):
        at = plane_at(cls, shift)
        n = WIDTHS[cls]
        x = gath[(h, cls) + at].reshape(256, PART)[:, :n]
        rows = pl.ds(pl.multiple_of(h * HALF + cls * PART, 128), n)
        for k, w in enumerate((v_gate, v_up)):
            y = jnp.dot(x, w[0, rows, :], preferred_element_type=F32).reshape(4, 4, 16, 256)
            acc[(k,) + at] = acc[(k,) + at] + y

    def from_pair(cls, k, shift):
        landed(gath.at[(other, cls) + plane_at(cls, shift)], sib_r.at[cls, k])

    for cls in range(3):
        expert_in(core, cls, 0)
    for cls in range(3):
        from_pair(cls, 0, 0)
        expert_in(other, cls, 0)
    for k, shift in ((1, 3), (2, 1)):
        for cls in range(3):
            expert_in(core, cls, shift)
    for cls in range(3):
        for f in range(4):
            landed(quarter(cls, f, 2, halves[0]), ag3_r.at[cls, f, 2])
            landed(quarter(cls, f, 2, halves[1]), ag3_r.at[cls, f, 3])
        to_pair(cls, 3, 2)
    for k, shift in ((1, 3), (2, 1)):
        for cls in range(3):
            from_pair(cls, k, shift)
            expert_in(other, cls, shift)
    for cls in range(3):
        expert_in(core, cls, 2)
    for cls in range(3):
        from_pair(cls, 3, 2)
        expert_in(other, cls, 2)

    lane = lax.broadcasted_iota(jnp.int32, (256, 128), 1)

    def activate(i, _):
        both = gath[0, 2, i, :, :, :, 512:640].astype(F32) + gath[1, 2, i, :, :, :, 512:640].astype(F32)
        weight = jnp.sum(jnp.where(lane == dp, both.reshape(256, 128), 0.0), axis=1, keepdims=True)
        gate = acc[0, i].reshape(256, 256)
        act = gate / (1.0 + jnp.exp(-gate)) * acc[1, i].reshape(256, 256) * weight
        inner[i] = act.astype(BF16).reshape(4, 4, 16, 256)
        return 0

    lax.fori_loop(0, 4, activate, 0)

    def expert_out(half, cls, at):
        cols = pl.ds(pl.multiple_of(half * HALF + cls * PART, 128), WIDTHS[cls])
        act = inner[at].reshape(256, 256)
        y = jnp.dot(act, v_down[0, :, cols], preferred_element_type=F32)
        return y.reshape(4, 4, 16, WIDTHS[cls])

    def for_pair(shift):
        for cls in range(3):
            at = plane_at(cls, shift)
            b = (cls,) + at + (slice(None), pl.ds(0, WIDTHS[cls]))
            sib_out[b] = expert_out(other, cls, at).astype(BF16)
            remote(sib_out.at[b], sib_in.at[b], red_s.at[cls, shift], red_r.at[cls, shift], sibling)

    def for_self(shift):
        for cls in range(3):
            at = plane_at(cls, shift)
            b = (cls,) + at + (slice(None), pl.ds(0, WIDTHS[cls]))
            y = expert_out(core, cls, at)
            landed(sib_in.at[b], red_r.at[cls, shift])
            mix[b] = (y + sib_in[b].astype(F32)).astype(BF16)

    def block(cls, shift, half):
        a1, a2, a3 = ORDERS[cls]
        spec = spec_of((a1, a2, a3), (half, whole, (pos[a3] + shift) % 4))
        return (cls, spec[0], spec[1], spec[2], slice(None), pl.ds(0, WIDTHS[cls]))

    def temp(cls, half):
        a1, a2, a3 = ORDERS[cls]
        first, then = (half, whole) if a1 < a2 else (whole, half)
        return (cls, first, then, slice(None), pl.ds(0, WIDTHS[cls]))

    def send(cls, shift, half, buf, k, delta):
        remote(
            mix.at[block(cls, shift, halves[half])], buf.at[temp(cls, halves[half])],
            sum_s.at[cls, 0, k], sum_r.at[cls, 0, k], along(ORDERS[cls][2], delta),
        )

    for_pair(2)
    for_pair(1)
    for_self(2)
    for cls in range(3):
        send(cls, 2, 0, t1, 0, 1)
        send(cls, 2, 1, t1, 1, 3)
    for_pair(3)
    for_self(1)
    for cls in range(3):
        send(cls, 1, 1, ul1, 2, 1)
    for_self(3)
    for cls in range(3):
        send(cls, 3, 0, ur1, 3, 3)
    for cls in range(3):
        for half, shift, buf, k, delta in ((0, 1, ul1, 0, 1), (1, 3, ur1, 1, 3)):
            at, tmp = block(cls, shift, halves[half]), temp(cls, halves[half])
            landed(t1.at[tmp], sum_r.at[cls, 0, k])
            mix[at] = (mix[at].astype(F32) + t1[tmp].astype(F32)).astype(BF16)
            send(cls, shift, half, buf, k + 4, delta)
    for_pair(0)
    for_self(0)
    for cls, order in enumerate(ORDERS):
        a1, a2, a3 = order
        n = WIDTHS[cls]
        for half, ks in ((0, (4, 3)), (1, (2, 5))):
            tmp = temp(cls, halves[half])
            landed(ul1.at[tmp], sum_r.at[cls, 0, ks[0]])
            landed(ur1.at[tmp], sum_r.at[cls, 0, ks[1]])
        for d in (2, 1, 3, 0):
            where = (pos[a2] + d) % 4
            spec = spec_of(order, (whole, where, pos[a3]))
            at = (cls, spec[0], spec[1], spec[2], slice(None), pl.ds(0, n))
            first, then = (whole, where) if a1 < a2 else (where, whole)
            tmp = (cls, first, then, slice(None), pl.ds(0, n))
            total = mix[at].astype(F32) + ul1[tmp].astype(F32) + ur1[tmp].astype(F32)
            mix[at] = total.astype(BF16)
            if d:
                dst = t2.at[cls, d - 1, :, :, pl.ds(0, n)]
                remote(mix.at[at], dst, sum_s.at[cls, 1, d], sum_r.at[cls, 1, d], along(a2, d))
    for cls, order in enumerate(ORDERS):
        a1, a2, a3 = order
        n = WIDTHS[cls]
        for d in (1, 3, 2):
            landed(t2.at[cls, d - 1, :, :, pl.ds(0, n)], sum_r.at[cls, 1, d])
        for d in (2, 1, 3, 0):
            where = (pos[a1] + d) % 4
            coords = list(pos)
            coords[a1] = where
            at = (cls, coords[0], coords[1], coords[2], slice(None), pl.ds(0, n))
            total = mix[at].astype(F32)
            for k in range(3):
                total = total + t2[cls, k, where, :, 0:n].astype(F32)
            mix[at] = total.astype(BF16)
            if d:
                dst = last.at[cls, d - 1, :, pl.ds(0, n)]
                remote(mix.at[at], dst, sum_s.at[cls, 2, d], sum_r.at[cls, 2, d], along(a1, d))
    for cls in range(3):
        n = WIDTHS[cls]
        total = mix[cls, pos[0], pos[1], pos[2], :, 0:n].astype(F32)
        for d in (1, 2, 3):
            landed(last.at[cls, d - 1, :, pl.ds(0, n)], sum_r.at[cls, 2, d])
            total = total + last[cls, d - 1, :, 0:n].astype(F32)
        total = total + hidden[:, cls * PART : cls * PART + n]
        fin_out[0, :, cls * PART : cls * PART + n] = total[0:8]
        fin_out[1, :, cls * PART : cls * PART + n] = total[8:16]
    remote(fin_out.at[other], fin_in, pair_s.at[3], pair_r.at[3], sibling)
    for s in range(2):
        out_ref[s, :, half_cols] = fin_out[core, s * 4 : s * 4 + 4]
    landed(fin_in, pair_r.at[3])
    for s in range(2):
        cols = pl.ds(pl.multiple_of(other * HALF, 128), HALF)
        out_ref[s, :, cols] = fin_in[s * 4 : s * 4 + 4]
    for src, ssem in sent:
        pltpu.make_async_copy(src, src, ssem).wait()


def layer(attended, residual, routes, gain, router, w_uv, w_out, w_gate, w_up, w_down):
    vmem = pl.BlockSpec(memory_space=pltpu.VMEM)
    hbm = pl.BlockSpec(memory_space=pl.ANY)
    dma = pltpu.SemaphoreType.DMA
    grid = (3, 4, 4, 4, 16, PART)
    return pl.pallas_call(
        layer_kernel,
        out_shape=jax.ShapeDtypeStruct((2, 4, 2 * HALF), F32),
        in_specs=[vmem] * 5 + [hbm] * 5,
        out_specs=vmem,
        scratch_shapes=[
            pltpu.VMEM((2, 8, HALF), F32),
            pltpu.VMEM((8, 128), F32),
            pltpu.VMEM((8, 64, LATENT), BF16),
            pltpu.VMEM((512, 1024), BF16),
            pltpu.VMEM((2, 4, 16, HALF), BF16),
            pltpu.VMEM((8, 16, HALF), BF16),
            pltpu.VMEM((16, HALF), F32),
            pltpu.VMEM((16, 128), F32),
            pltpu.VMEM((2, 16, 128), F32),
            pltpu.VMEM((2, 16, 128), F32),
            pltpu.VMEM((16, HALF), F32),
            pltpu.VMEM((2,) + grid, BF16),
            pltpu.VMEM(w_uv.shape, BF16),
            pltpu.VMEM(w_out.shape, BF16),
            pltpu.VMEM(w_gate.shape, BF16),
            pltpu.VMEM(w_up.shape, BF16),
            pltpu.VMEM(w_down.shape, BF16),
            pltpu.VMEM((2, 4, 4, 4, 16, 256), F32),
            pltpu.VMEM((4, 4, 4, 16, 256), BF16),
            pltpu.VMEM(grid, BF16),
            pltpu.VMEM(grid, BF16),
            pltpu.VMEM(grid, BF16),
            pltpu.VMEM((3, 4, 4, 16, PART), BF16),
            pltpu.VMEM((3, 4, 4, 16, PART), BF16),
            pltpu.VMEM((3, 4, 4, 16, PART), BF16),
            pltpu.VMEM((3, 3, 4, 16, PART), BF16),
            pltpu.VMEM((3, 3, 16, PART), BF16),
            pltpu.VMEM((2, 8, HALF), F32),
            pltpu.VMEM((8, HALF), F32),
            dma((5,)), dma, dma((8,)), dma((8,)), dma((8,)), dma((8,)), dma((4,)), dma((4,)),
            dma((3, 4)), dma((3, 4)), dma((3, 4, 4)), dma((3, 4, 4)), dma((3, 4, 4)), dma((3, 4, 4)),
            dma((3, 4)), dma((3, 4)), dma((3, 4)), dma((3, 4)),
            dma((3, 3, 6)), dma((3, 3, 6)),
        ],
        compiler_params=pltpu.CompilerParams(
            collective_id=1, has_side_effects=True, vmem_limit_bytes=56 * 2**20
        ),
        name="layer",
    )(attended, residual, routes, gain, router, w_uv, w_out, w_gate, w_up, w_down)


def shards(
    cache_pool,
    page_table,
    page_counts,
    queries,
    new_latent,
    residual,
    w_uv,
    w_out,
    norm_gain,
    w_router,
    w_gate,
    w_up,
    w_down,
    routes,
):
    table = page_table.T
    incoming = exchange(table, jnp.transpose(cache_pool, (1, 2, 0))).reshape(-1, 3, 96, 128)
    attended = attend(table, page_counts, queries, new_latent, incoming)
    out = layer(
        attended, residual, routes, norm_gain, w_router.T, w_uv, w_out, w_gate, w_up, w_down
    )
    return out.astype(BF16)


def solution(mesh):
    return jax.shard_map(
        shards,
        mesh=mesh,
        in_specs=(
            P(("dp", "ep"), None, None),
            P(),
            P(("dp", "ep"), None),
            P(None, ("dp", "ep"), None, None),
            P(None, ("dp", "ep"), None),
            P(None, ("dp", "ep"), None),
            P("ep", None, None),
            P("ep", None),
            P(),
            P(),
            P("dp", None, "ep"),
            P("dp", None, "ep"),
            P("dp", "ep", None),
            P(None, ("dp", "ep"), None),
        ),
        out_specs=P(None, ("dp", "ep"), None),
        check_vma=False,
    )
```

```python
import functools

import jax
import jax.numpy as jnp
from jax import lax
from jax.experimental import pallas as pl
from jax.experimental.pallas import tpu as pltpu
from jax.sharding import PartitionSpec as P

MESH = pl.DeviceIdType.MESH
F32 = jnp.float32
BF16 = jnp.bfloat16

LATENT = 512
ROPE = 64
PAGE = 64
TILE = 16
score_scale = 192.0 ** (-0.5)
route_scale = 2.5
norm_eps = 1e-06

HALF = 1792
PART = 640
ORDERS = ((0, 1, 2), (1, 2, 0), (2, 0, 1))
WIDTHS = (640, 640, 512)


def exchange_kernel(
    table, pool, out,
    pool_v, slots, held1, held2, stage,
    psem, lsem, send1, recv1, send2, recv2, send3, recv3,
):
    dp = lax.axis_index("dp")
    ep = lax.axis_index("ep")
    pos = (dp // 4, dp % 4, ep // 2)
    core = ep % 2
    other = 1 - core
    whole = pl.ds(0, 4)

    loads = [
        pltpu.make_async_copy(
            pool.at[pl.ds(i * 16, 16)], pool_v.at[pl.ds(i * 16, 16)], psem.at[i]
        )
        for i in range(4)
    ]
    for load in loads:
        load.start()

    def along(axis, delta, c):
        coords = list(pos)
        coords[axis] = (coords[axis] + delta) % 4
        return (coords[0] * 4 + coords[1], coords[2] * 2 + c)

    def spec_of(order, values):
        spec = [None, None, None]
        for axis, value in zip(order, values):
            spec[axis] = value
        return tuple(spec)

    barrier = pltpu.get_barrier_semaphore()
    peers = [along(a, d, c) for a in range(3) for d in (1, 2, 3) for c in (core, other)]
    peers.append(along(0, 0, other))
    for peer in peers:
        pl.semaphore_signal(barrier, inc=1, device_id=peer, device_id_type=MESH)

    pages = table[...]
    wanted = jnp.where(pages // 128 == dp * 8 + ep, pages % 128, 0)
    wanted = jnp.sum(wanted, axis=0, keepdims=True)
    page = lax.broadcasted_iota(jnp.int32, (128, 128), 0)
    onehot = jnp.transpose(jnp.where(wanted == page, 1.0, 0.0)).astype(BF16)

    def put(cls, row, pieces):
        for j in range(0, 16, 4):
            x = jnp.concatenate(pieces(j), axis=0)
            y = lax.dot_general(onehot, x, (((1,), (1,)), ((), ())), preferred_element_type=F32)
            for i in range(4):
                stage[:, j + i, :] = y[:, i * 128 : (i + 1) * 128]
        block = stage[...].astype(BF16).reshape(4, 4, 4, 2, 16, 128)
        slots[cls, :, :, :, :, row : row + 16, :] = block

    def latent_rows(cls, chunk, unit, row):
        def pieces(j):
            t = unit * 16 + j
            return [pool_v[pl.ds(t, 4), chunk * 128 : (chunk + 1) * 128, :].reshape(512, 128)]

        put(cls, row, pieces)

    def rope_rows(cls, unit, row):
        def pieces(j):
            found = []
            for i in range(4):
                found.append(pool_v[unit * 16 + j + i, 512:576, :])
                found.append(pool_v[32 + unit * 16 + j + i, 512:576, :])
            return found

        put(cls, row, pieces)

    def remote(src, dst, ssem, rsem, peer):
        pltpu.make_async_remote_copy(
            src_ref=src, dst_ref=dst, send_sem=ssem, recv_sem=rsem,
            device_id=peer, device_id_type=MESH,
        ).start()

    def landed(ref, sem):
        pltpu.make_async_copy(ref, ref, sem).wait()

    for part in range(6):
        rows = pl.ds(part * 16, 16)
        if part < 4:
            loads[part].wait()
        for cls, order in enumerate(ORDERS):
            a1, a2, a3 = order
            if part < 4:
                latent_rows(cls, cls, part, 16 * part)
            elif cls < 2:
                latent_rows(cls, 3, 2 * cls + part - 4, 16 * part)
            else:
                rope_rows(cls, part - 4, 16 * part)
            if part == 0 and cls == 0:
                pl.semaphore_wait(barrier, len(peers))
            for d in (1, 2, 3):
                src = spec_of(order, ((pos[a1] + d) % 4, whole, whole))
                dst = spec_of(order, (pos[a1], whole, whole))
                remote(
                    slots.at[(cls,) + src + (pl.ds(0, 2), rows)],
                    held1.at[(cls,) + dst + (pl.ds(0, 2), rows)],
                    send1.at[cls], recv1.at[cls, d], along(a1, d, core),
                )
            if part == 5:
                own = (cls,) + spec_of(order, (pos[a1], whole, whole))
                pltpu.make_async_copy(slots.at[own], held1.at[own], lsem.at[cls]).start()

    def second(cls, buf, e):
        a1, a2, a3 = order = ORDERS[cls]
        src1 = (pos[a1] + 4 - e) % 4
        for d in (1, 2, 3):
            src = spec_of(order, (src1, (pos[a2] + d) % 4, whole))
            dst = spec_of(order, (src1, pos[a2], whole))
            remote(
                buf.at[(cls,) + src], held2.at[(cls,) + dst],
                send2.at[cls], recv2.at[cls, d], along(a2, d, core),
            )

    def third(cls, buf, f):
        a1, a2, a3 = order = ORDERS[cls]
        src2 = (pos[a2] + 4 - f) % 4
        for d in (1, 2, 3, 0):
            for k, c in ((0, core), (1, other)):
                src = spec_of(order, (whole, src2, (pos[a3] + d) % 4))
                dst = spec_of(order, (whole, src2, pos[a3]))
                a = buf.at[(cls,) + src + (c,)]
                b = out.at[dst + (core, cls)]
                if d == 0 and k == 0:
                    pltpu.make_async_copy(a, b, recv3.at[cls]).start()
                else:
                    remote(a, b, send3.at[cls, d], recv3.at[cls], along(a3, d, c))

    for cls in range(3):
        second(cls, slots, 0)
    for e in (1, 3, 2):
        for cls, order in enumerate(ORDERS):
            src1 = (pos[order[0]] + 4 - e) % 4
            landed(held1.at[(cls,) + spec_of(order, (src1, whole, whole))], recv1.at[cls, e])
            second(cls, held1, e)
    for cls, order in enumerate(ORDERS):
        own = spec_of(order, (pos[order[0]], whole, whole))
        landed(held1.at[(cls,) + own], lsem.at[cls])
        third(cls, held1, 0)
    for f in (1, 3, 2):
        for cls, order in enumerate(ORDERS):
            a1, a2, a3 = order
            at = spec_of(order, (whole, (pos[a2] + 4 - f) % 4, whole))
            landed(held2.at[(cls,) + at], recv2.at[cls, f])
            third(cls, held2, f)
    for cls in range(3):
        most = held1.at[cls, pl.ds(0, 3)]
        landed(most, send1.at[cls])
        landed(most, send2.at[cls])
    for cls in range(3):
        landed(held1.at[cls, 0, pl.ds(0, 2)], send3.at[cls, 0])
        for d in (1, 2, 3):
            landed(held1.at[cls, 0], send3.at[cls, d])
    for cls in range(3):
        landed(out.at[:, :, :, :, cls], recv3.at[cls])


def exchange(table, pool):
    vmem = pl.BlockSpec(memory_space=pltpu.VMEM)
    hbm = pl.BlockSpec(memory_space=pl.ANY)
    dma = pltpu.SemaphoreType.DMA
    held = (3, 4, 4, 4, 2, 96, 128)
    return pl.pallas_call(
        exchange_kernel,
        out_shape=jax.ShapeDtypeStruct((4, 4, 4, 2, 3, 96, 128), BF16),
        in_specs=[vmem, hbm],
        out_specs=hbm,
        scratch_shapes=[
            pltpu.VMEM(pool.shape, BF16),
            pltpu.VMEM(held, BF16),
            pltpu.VMEM(held, BF16),
            pltpu.VMEM(held, BF16),
            pltpu.VMEM((128, 16, 128), F32),
            dma((4,)), dma((3,)), dma((3,)), dma((3, 4)), dma((3,)), dma((3, 4)), dma((3, 4)), dma((3,)),
        ],
        compiler_params=pltpu.CompilerParams(
            collective_id=2, has_side_effects=True, vmem_limit_bytes=56 * 2**20
        ),
        name="exchange",
    )(table, pool)


def attend_kernel(
    table, counts, q_ref, new_ref, slots, out_ref, own_ref, keys, scores, sem
):
    pages = 64
    me = lax.axis_index("dp") * 8 + lax.axis_index("ep")

    def fetch(j, _):
        pltpu.make_async_copy(slots.at[table[j, me] // 128], keys.at[j], sem).start()
        return 0

    lax.fori_loop(0, pages, fetch, 0)

    def clear(j, _):
        keys[pages + j] = jnp.zeros((3, 96, 128), BF16)
        return 0

    lax.fori_loop(0, TILE, clear, 0)
    own_ref[...] = jnp.zeros_like(own_ref)
    for step in range(2):
        fresh = new_ref[step].astype(F32)
        for r in range(4):
            own_ref[r, step : step + 1, :] = fresh[r : r + 1]
    filled = keys.at[pl.ds(0, pages)]
    pltpu.make_async_copy(filled, filled, sem).wait()
    width = TILE * PAGE
    step_of = lax.broadcasted_iota(jnp.int32, (128, 16), 0) // 64
    token = lax.broadcasted_iota(jnp.int32, (128, 16), 1)
    low = lax.broadcasted_iota(jnp.int32, (TILE, 32, 128), 2) < ROPE

    def values_of(page):
        parts = [keys[pl.ds(page, TILE), k, 0:64, :].reshape(width, 128) for k in range(3)]
        parts.append(keys[pl.ds(page, TILE), 0:2, 64:96, :].reshape(width, 128))
        return jnp.concatenate(parts, axis=1)

    def request(r, start):
        q = jnp.concatenate([q_ref[0, r], q_ref[1, r]], axis=0)
        own = own_ref[r].astype(BF16)
        s_own = lax.dot_general(q, own, (((1,), (1,)), ((), ())), preferred_element_type=F32)
        s_own = jnp.where(token <= step_of, s_own * score_scale, -jnp.inf)
        q_rope = q[:, LATENT:]
        q_wide = jnp.concatenate([q[:, :LATENT], q_rope, q_rope], axis=1)
        length = counts[0, r] * PAGE
        tiles = (length + width - 1) // width

        def score(t, top):
            page = start + t * TILE
            rope = keys[pl.ds(page, TILE), 2, 64:96, :]
            zero = jnp.zeros_like(rope)
            pair = jnp.concatenate([jnp.where(low, rope, zero), jnp.where(low, zero, rope)], axis=1)
            key = jnp.concatenate([values_of(page), pair.reshape(width, 128)], axis=1)
            s = lax.dot_general(q_wide, key, (((1,), (1,)), ((), ())), preferred_element_type=F32)
            place = t * width + lax.broadcasted_iota(jnp.int32, (128, width), 1)
            s = jnp.where(place < length, s * score_scale, -jnp.inf)
            scores[t] = s
            return jnp.maximum(top, jnp.max(s, axis=1, keepdims=True))

        top = lax.fori_loop(0, tiles, score, jnp.max(s_own, axis=1, keepdims=True))
        p_own = jnp.exp(s_own - top)
        total = jnp.sum(p_own, axis=1, keepdims=True)
        acc = jnp.dot(p_own.astype(BF16), own[:, :LATENT], preferred_element_type=F32)

        def mix(t, carry):
            total, acc = carry
            p = jnp.exp(scores[t] - top)
            total = total + jnp.sum(p, axis=1, keepdims=True)
            acc = acc + jnp.dot(
                p.astype(BF16), values_of(start + t * TILE), preferred_element_type=F32
            )
            return total, acc

        total, acc = lax.fori_loop(0, tiles, mix, (total, acc))
        res = (acc / total).reshape(2, 8, 8, LATENT)
        at = pl.multiple_of(r * 16, 16)
        for g in range(8):
            block = jnp.concatenate([res[0, g], res[1, g]], axis=0)
            out_ref[g, pl.ds(at, 16), :] = block.astype(BF16)
        return start + counts[0, r]

    lax.fori_loop(0, 4, request, 0)


def attend(table, counts, queries, new_latent, slots):
    smem = pl.BlockSpec(memory_space=pltpu.SMEM)
    vmem = pl.BlockSpec(memory_space=pltpu.VMEM)
    return pl.pallas_call(
        attend_kernel,
        out_shape=jax.ShapeDtypeStruct((8, 64, LATENT), BF16),
        in_specs=[smem, smem, vmem, vmem, pl.BlockSpec(memory_space=pl.ANY)],
        out_specs=vmem,
        scratch_shapes=[
            pltpu.VMEM((4, 16, LATENT + ROPE), F32),
            pltpu.VMEM((64 + TILE, 3, 96, 128), BF16),
            pltpu.VMEM((32 // TILE, 128, TILE * PAGE), F32),
            pltpu.SemaphoreType.DMA,
        ],
        compiler_params=pltpu.CompilerParams(vmem_limit_bytes=60 * 2**20),
        name="attend",
    )(table, counts, queries, new_latent, slots)


def layer_kernel(
    attended, residual, routes, gain, router, w_uv, w_out, w_gate, w_up, w_down,
    out_ref,
    resid, member, heads_in, masked, part_out, part_in, res_all, mem_all, stat_out, stat_in, hidden,
    gath, v_uv, v_out, v_gate, v_up, v_down, acc, inner,
    mix, sib_out, sib_in, t1, ul1, ur1, t2, last, fin_out, fin_in,
    wsem, lsem, head_s, head_r, part_s, part_r, pair_s, pair_r,
    ag1_s, ag1_r, ag2_s, ag2_r, ag3_s, ag3_r, sib_s, sib_r, red_s, red_r, sum_s, sum_r,
):
    dp = lax.axis_index("dp")
    ep = lax.axis_index("ep")
    pos = (dp // 4, dp % 4, ep // 2)
    core = ep % 2
    other = 1 - core

    def device(coords, c):
        return (coords[0] * 4 + coords[1], coords[2] * 2 + c)

    def along(axis, delta):
        coords = [pos[0], pos[1], pos[2]]
        coords[axis] = (coords[axis] + delta) % 4
        return device(coords, core)

    sibling = device(pos, other)
    ep_peers = [(dp, (ep + o) % 8) for o in range(1, 8)]
    ring_peers = [along(a, d) for a in (0, 1) for d in (1, 2, 3)]

    def remote(src, dst, ssem, rsem, peer):
        copy = pltpu.make_async_remote_copy(
            src_ref=src, dst_ref=dst, send_sem=ssem, recv_sem=rsem,
            device_id=peer, device_id_type=MESH,
        )
        copy.start()
        sent.append((src, ssem))

    def landed(ref, rsem):
        pltpu.make_async_copy(ref, ref, rsem).wait()

    sent = []

    def settle():
        for src, ssem in sent:
            pltpu.make_async_copy(src, src, ssem).wait()
        sent.clear()

    loads = [(w_uv, v_uv), (w_out, v_out), (w_gate, v_gate), (w_up, v_up), (w_down, v_down)]
    copies = [pltpu.make_async_copy(a, b, wsem.at[i]) for i, (a, b) in enumerate(loads)]
    for copy in copies:
        copy.start()

    barrier = pltpu.get_barrier_semaphore()
    for peer in ep_peers + ring_peers:
        pl.semaphore_signal(barrier, inc=1, device_id=peer, device_id_type=MESH)
    for h in range(2):
        cols = slice(h * HALF, (h + 1) * HALF)
        both = [residual[s, :, cols].astype(F32) for s in range(2)]
        resid[h] = jnp.concatenate(both, axis=0)
    route = jnp.concatenate([routes[0], routes[1]], axis=0)
    lanes = lax.broadcasted_iota(jnp.int32, (8, 128), 1)
    named = jnp.zeros((8, 128), F32)
    for k in range(8):
        named = jnp.where(route[:, k : k + 1] == lanes, 1.0, named)
    member[...] = named

    def clear(i, _):
        acc[0, i] = jnp.zeros((4, 4, 16, 256), F32)
        acc[1, i] = jnp.zeros((4, 4, 16, 256), F32)
        return 0

    lax.fori_loop(0, 4, clear, 0)
    pl.semaphore_wait(barrier, len(ep_peers) + len(ring_peers))

    for o in range(1, 8):
        to = (ep + o) % 8
        remote(attended.at[to], heads_in.at[ep], head_s.at[o], head_r.at[o], (dp, to))
    own_heads = pltpu.make_async_copy(attended.at[ep], heads_in.at[ep], lsem)
    own_heads.start()
    own_rows = pl.ds(pl.multiple_of(core * 8, 8), 8)
    other_rows = pl.ds(pl.multiple_of(other * 8, 8), 8)
    remote(resid.at[other], res_all.at[own_rows], pair_s.at[0], pair_r.at[0], sibling)
    remote(member, mem_all.at[own_rows], pair_s.at[1], pair_r.at[1], sibling)
    res_all[own_rows, :] = resid[core]
    mem_all[own_rows, :] = member[...]
    own_heads.wait()
    for o in range(1, 8):
        landed(heads_in.at[(ep + 8 - o) % 8], head_r.at[o])

    copies[0].wait()
    x = heads_in[...].reshape(512, LATENT)
    row_head = lax.broadcasted_iota(jnp.int32, (512, 128), 0) % 8
    for h in range(8):
        y = jnp.dot(x, v_uv[h], preferred_element_type=F32)
        masked[:, h * 128 : (h + 1) * 128] = jnp.where(row_head == h, y, 0.0).astype(BF16)
    to_row = lax.broadcasted_iota(jnp.int32, (64, 512), 0)
    from_row = lax.broadcasted_iota(jnp.int32, (64, 512), 1) // 8
    wanted = (to_row // 8) * 8 + (to_row % 4) * 2 + (to_row % 8) // 4
    pick = jnp.where(from_row == wanted, 1.0, 0.0).astype(BF16)
    flat = jnp.dot(pick, masked[...], preferred_element_type=F32).astype(BF16)

    copies[1].wait()
    for h, turns in ((other, (1, 3, 5, 7)), (core, (2, 4, 6))):
        for t in range(HALF // 256):
            cols = pl.ds(pl.multiple_of(h * HALF + t * 256, 256), 256)
            y = jnp.dot(flat, v_out[:, cols], preferred_element_type=F32)
            part_out[h, :, :, t * 256 : (t + 1) * 256] = y.astype(BF16).reshape(4, 16, 256)
        for o in turns:
            to = (ep + o) % 8
            remote(part_out.at[h, to // 2], part_in.at[ep], part_s.at[o], part_r.at[o], (dp, to))
    landed(res_all.at[other_rows], pair_r.at[0])
    landed(mem_all.at[other_rows], pair_r.at[1])
    hid = part_out[core, pos[2]].astype(F32)
    settle()
    for o in range(1, 8):
        src = (ep + 8 - o) % 8
        landed(part_in.at[src], part_r.at[o])
        hid = hid + part_in[src].astype(F32)
    hid = hid + res_all[...]
    hidden[...] = hid

    half_cols = pl.ds(pl.multiple_of(core * HALF, 128), HALF)
    scaled = hid * gain[half_cols].reshape(1, HALF)
    stat_out[0] = jnp.zeros((16, 128), F32)
    stat_out[0, :, 0:16] = lax.dot_general(
        scaled, router[:, half_cols], (((1,), (1,)), ((), ())),
        preferred_element_type=F32, precision=lax.Precision.HIGHEST,
    )
    stat_out[1] = jnp.broadcast_to(jnp.sum(hid * hid, axis=1, keepdims=True), (16, 128))
    remote(stat_out, stat_in, pair_s.at[2], pair_r.at[2], sibling)
    landed(stat_in, pair_r.at[2])
    square = stat_out[1] + stat_in[1]
    inv = lax.rsqrt(square / (2 * HALF) + norm_eps)
    affinity = jax.nn.sigmoid((stat_out[0] + stat_in[0]) * inv) * mem_all[...]
    gates = route_scale * affinity / jnp.sum(affinity, axis=1, keepdims=True)
    coarse = gates.astype(BF16)
    fine = (gates - coarse.astype(F32)).astype(BF16)
    normed = (scaled * inv[:, 0:1]).astype(BF16)
    z, xx, yy = pos
    gath[core, 0, z, xx, yy] = normed[:, 0:640]
    gath[core, 1, z, xx, yy] = normed[:, 640:1280]
    gath[core, 2, z, xx, yy, :, 0:512] = normed[:, 1280:1792]
    gath[core, 2, z, xx, yy, :, 512:640] = jnp.where(core == 0, coarse, fine)

    whole = pl.ds(0, 4)
    halves = (pl.ds(0, 2), pl.ds(2, 2))

    def g_at(cls, spec):
        return gath.at[core, cls, spec[0], spec[1], spec[2]]

    def spec_of(order, values):
        spec = [None, None, None]
        for axis, value in zip(order, values):
            spec[axis] = value
        return spec

    def line(cls, e, f):
        a1, a2, a3 = ORDERS[cls]
        where = spec_of((a1, a2, a3), ((pos[a1] + 4 - e) % 4, (pos[a2] + 4 - f) % 4, pos[a3]))
        return g_at(cls, where)

    def quarter(cls, f, shift, half=whole):
        a1, a2, a3 = ORDERS[cls]
        at = (half, (pos[a2] + 4 - f) % 4, (pos[a3] + shift) % 4)
        return g_at(cls, spec_of((a1, a2, a3), at))

    def plane_at(cls, shift):
        a1, a2, a3 = ORDERS[cls]
        return tuple(spec_of((a1, a2, a3), (whole, whole, (pos[a3] + shift) % 4)))

    def to_pair(cls, k, shift):
        plane = gath.at[(core, cls) + plane_at(cls, shift)]
        remote(plane, plane, sib_s.at[cls, k], sib_r.at[cls, k], sibling)

    def second(cls, e):
        b = line(cls, e, 0)
        for d in (1, 3, 2):
            remote(b, b, ag2_s.at[cls, d, e], ag2_r.at[cls, d, e], along(ORDERS[cls][1], d))

    def third(cls, f):
        b = quarter(cls, f, 0)
        for k, d in ((0, 1), (1, 3)):
            remote(b, b, ag3_s.at[cls, f, k], ag3_r.at[cls, f, k], along(ORDERS[cls][2], d))

    for cls, order in enumerate(ORDERS):
        own = g_at(cls, pos)
        for d in (1, 3, 2):
            remote(own, own, ag1_s.at[cls, d], ag1_r.at[cls, d], along(order[0], d))
    for cls in range(3):
        second(cls, 0)
    for e in (1, 3, 2):
        for cls in range(3):
            landed(line(cls, e, 0), ag1_r.at[cls, e])
            second(cls, e)
    for cls in range(3):
        third(cls, 0)
    for f in (1, 3, 2):
        for cls in range(3):
            for e in range(4):
                landed(line(cls, e, f), ag2_r.at[cls, f, e])
            third(cls, f)
    for cls in range(3):
        to_pair(cls, 0, 0)
    for f in (0, 1, 3, 2):
        for cls, order in enumerate(ORDERS):
            landed(quarter(cls, f, 3), ag3_r.at[cls, f, 0])
            b = quarter(cls, f, 3, halves[0])
            remote(b, b, ag3_s.at[cls, f, 2], ag3_r.at[cls, f, 2], along(order[2], 1))
            landed(quarter(cls, f, 1), ag3_r.at[cls, f, 1])
            b = quarter(cls, f, 1, halves[1])
            remote(b, b, ag3_s.at[cls, f, 3], ag3_r.at[cls, f, 3], along(order[2], 3))
    for k, shift in ((1, 3), (2, 1)):
        for cls in range(3):
            to_pair(cls, k, shift)

    for copy in copies[2:]:
        copy.wait()

    def expert_in(h, cls, shift):
        at = plane_at(cls, shift)
        n = WIDTHS[cls]
        x = gath[(h, cls) + at].reshape(256, PART)[:, :n]
        rows = pl.ds(pl.multiple_of(h * HALF + cls * PART, 128), n)
        for k, w in enumerate((v_gate, v_up)):
            y = jnp.dot(x, w[0, rows, :], preferred_element_type=F32).reshape(4, 4, 16, 256)
            acc[(k,) + at] = acc[(k,) + at] + y

    def from_pair(cls, k, shift):
        landed(gath.at[(other, cls) + plane_at(cls, shift)], sib_r.at[cls, k])

    for cls in range(3):
        expert_in(core, cls, 0)
    for cls in range(3):
        from_pair(cls, 0, 0)
        expert_in(other, cls, 0)
    for k, shift in ((1, 3), (2, 1)):
        for cls in range(3):
            expert_in(core, cls, shift)
    for cls in range(3):
        for f in range(4):
            landed(quarter(cls, f, 2, halves[0]), ag3_r.at[cls, f, 2])
            landed(quarter(cls, f, 2, halves[1]), ag3_r.at[cls, f, 3])
        to_pair(cls, 3, 2)
    for k, shift in ((1, 3), (2, 1)):
        for cls in range(3):
            from_pair(cls, k, shift)
            expert_in(other, cls, shift)
    for cls in range(3):
        expert_in(core, cls, 2)
    for cls in range(3):
        from_pair(cls, 3, 2)
        expert_in(other, cls, 2)

    lane = lax.broadcasted_iota(jnp.int32, (256, 128), 1)

    def activate(i, _):
        both = gath[0, 2, i, :, :, :, 512:640].astype(F32) + gath[1, 2, i, :, :, :, 512:640].astype(F32)
        weight = jnp.sum(jnp.where(lane == dp, both.reshape(256, 128), 0.0), axis=1, keepdims=True)
        gate = acc[0, i].reshape(256, 256)
        act = gate / (1.0 + jnp.exp(-gate)) * acc[1, i].reshape(256, 256) * weight
        inner[i] = act.astype(BF16).reshape(4, 4, 16, 256)
        return 0

    lax.fori_loop(0, 4, activate, 0)

    def expert_out(half, cls, at):
        cols = pl.ds(pl.multiple_of(half * HALF + cls * PART, 128), WIDTHS[cls])
        act = inner[at].reshape(256, 256)
        y = jnp.dot(act, v_down[0, :, cols], preferred_element_type=F32)
        return y.reshape(4, 4, 16, WIDTHS[cls])

    def for_pair(shift):
        for cls in range(3):
            at = plane_at(cls, shift)
            b = (cls,) + at + (slice(None), pl.ds(0, WIDTHS[cls]))
            sib_out[b] = expert_out(other, cls, at).astype(BF16)
            remote(sib_out.at[b], sib_in.at[b], red_s.at[cls, shift], red_r.at[cls, shift], sibling)

    def for_self(shift):
        for cls in range(3):
            at = plane_at(cls, shift)
            b = (cls,) + at + (slice(None), pl.ds(0, WIDTHS[cls]))
            y = expert_out(core, cls, at)
            landed(sib_in.at[b], red_r.at[cls, shift])
            mix[b] = (y + sib_in[b].astype(F32)).astype(BF16)

    def block(cls, shift, half):
        a1, a2, a3 = ORDERS[cls]
        spec = spec_of((a1, a2, a3), (half, whole, (pos[a3] + shift) % 4))
        return (cls, spec[0], spec[1], spec[2], slice(None), pl.ds(0, WIDTHS[cls]))

    def temp(cls, half):
        a1, a2, a3 = ORDERS[cls]
        first, then = (half, whole) if a1 < a2 else (whole, half)
        return (cls, first, then, slice(None), pl.ds(0, WIDTHS[cls]))

    def send(cls, shift, half, buf, k, delta):
        remote(
            mix.at[block(cls, shift, halves[half])], buf.at[temp(cls, halves[half])],
            sum_s.at[cls, 0, k], sum_r.at[cls, 0, k], along(ORDERS[cls][2], delta),
        )

    for_pair(2)
    for_pair(1)
    for_self(2)
    for cls in range(3):
        send(cls, 2, 0, t1, 0, 1)
        send(cls, 2, 1, t1, 1, 3)
    for_pair(3)
    for_self(1)
    for cls in range(3):
        send(cls, 1, 1, ul1, 2, 1)
    for_self(3)
    for cls in range(3):
        send(cls, 3, 0, ur1, 3, 3)
    for cls in range(3):
        for half, shift, buf, k, delta in ((0, 1, ul1, 0, 1), (1, 3, ur1, 1, 3)):
            at, tmp = block(cls, shift, halves[half]), temp(cls, halves[half])
            landed(t1.at[tmp], sum_r.at[cls, 0, k])
            mix[at] = (mix[at].astype(F32) + t1[tmp].astype(F32)).astype(BF16)
            send(cls, shift, half, buf, k + 4, delta)
    for_pair(0)
    for_self(0)
    settle()
    for cls, order in enumerate(ORDERS):
        a1, a2, a3 = order
        n = WIDTHS[cls]
        for half, ks in ((0, (4, 3)), (1, (2, 5))):
            tmp = temp(cls, halves[half])
            landed(ul1.at[tmp], sum_r.at[cls, 0, ks[0]])
            landed(ur1.at[tmp], sum_r.at[cls, 0, ks[1]])
        for d in (2, 1, 3, 0):
            where = (pos[a2] + d) % 4
            spec = spec_of(order, (whole, where, pos[a3]))
            at = (cls, spec[0], spec[1], spec[2], slice(None), pl.ds(0, n))
            first, then = (whole, where) if a1 < a2 else (where, whole)
            tmp = (cls, first, then, slice(None), pl.ds(0, n))
            total = mix[at].astype(F32) + ul1[tmp].astype(F32) + ur1[tmp].astype(F32)
            mix[at] = total.astype(BF16)
            if d:
                dst = t2.at[cls, d - 1, :, :, pl.ds(0, n)]
                remote(mix.at[at], dst, sum_s.at[cls, 1, d], sum_r.at[cls, 1, d], along(a2, d))
    for cls, order in enumerate(ORDERS):
        a1, a2, a3 = order
        n = WIDTHS[cls]
        for d in (1, 3, 2):
            landed(t2.at[cls, d - 1, :, :, pl.ds(0, n)], sum_r.at[cls, 1, d])
        for d in (2, 1, 3, 0):
            where = (pos[a1] + d) % 4
            coords = list(pos)
            coords[a1] = where
            at = (cls, coords[0], coords[1], coords[2], slice(None), pl.ds(0, n))
            total = mix[at].astype(F32)
            for k in range(3):
                total = total + t2[cls, k, where, :, 0:n].astype(F32)
            mix[at] = total.astype(BF16)
            if d:
                dst = last.at[cls, d - 1, :, pl.ds(0, n)]
                remote(mix.at[at], dst, sum_s.at[cls, 2, d], sum_r.at[cls, 2, d], along(a1, d))
    for cls in range(3):
        n = WIDTHS[cls]
        total = mix[cls, pos[0], pos[1], pos[2], :, 0:n].astype(F32)
        for d in (1, 2, 3):
            landed(last.at[cls, d - 1, :, pl.ds(0, n)], sum_r.at[cls, 2, d])
            total = total + last[cls, d - 1, :, 0:n].astype(F32)
        total = total + hidden[:, cls * PART : cls * PART + n]
        fin_out[0, :, cls * PART : cls * PART + n] = total[0:8]
        fin_out[1, :, cls * PART : cls * PART + n] = total[8:16]
    remote(fin_out.at[other], fin_in, pair_s.at[3], pair_r.at[3], sibling)
    for s in range(2):
        out_ref[s, :, half_cols] = fin_out[core, s * 4 : s * 4 + 4]
    settle()
    landed(fin_in, pair_r.at[3])
    for s in range(2):
        cols = pl.ds(pl.multiple_of(other * HALF, 128), HALF)
        out_ref[s, :, cols] = fin_in[s * 4 : s * 4 + 4]


def layer(attended, residual, routes, gain, router, w_uv, w_out, w_gate, w_up, w_down):
    vmem = pl.BlockSpec(memory_space=pltpu.VMEM)
    hbm = pl.BlockSpec(memory_space=pl.ANY)
    dma = pltpu.SemaphoreType.DMA
    grid = (3, 4, 4, 4, 16, PART)
    return pl.pallas_call(
        layer_kernel,
        out_shape=jax.ShapeDtypeStruct((2, 4, 2 * HALF), F32),
        in_specs=[hbm] + [vmem] * 4 + [hbm] * 5,
        out_specs=vmem,
        scratch_shapes=[
            pltpu.VMEM((2, 8, HALF), F32),
            pltpu.VMEM((8, 128), F32),
            pltpu.VMEM((8, 64, LATENT), BF16),
            pltpu.VMEM((512, 1024), BF16),
            pltpu.VMEM((2, 4, 16, HALF), BF16),
            pltpu.VMEM((8, 16, HALF), BF16),
            pltpu.VMEM((16, HALF), F32),
            pltpu.VMEM((16, 128), F32),
            pltpu.VMEM((2, 16, 128), F32),
            pltpu.VMEM((2, 16, 128), F32),
            pltpu.VMEM((16, HALF), F32),
            pltpu.VMEM((2,) + grid, BF16),
            pltpu.VMEM(w_uv.shape, BF16),
            pltpu.VMEM(w_out.shape, BF16),
            pltpu.VMEM(w_gate.shape, BF16),
            pltpu.VMEM(w_up.shape, BF16),
            pltpu.VMEM(w_down.shape, BF16),
            pltpu.VMEM((2, 4, 4, 4, 16, 256), F32),
            pltpu.VMEM((4, 4, 4, 16, 256), BF16),
            pltpu.VMEM(grid, BF16),
            pltpu.VMEM(grid, BF16),
            pltpu.VMEM(grid, BF16),
            pltpu.VMEM((3, 4, 4, 16, PART), BF16),
            pltpu.VMEM((3, 4, 4, 16, PART), BF16),
            pltpu.VMEM((3, 4, 4, 16, PART), BF16),
            pltpu.VMEM((3, 3, 4, 16, PART), BF16),
            pltpu.VMEM((3, 3, 16, PART), BF16),
            pltpu.VMEM((2, 8, HALF), F32),
            pltpu.VMEM((8, HALF), F32),
            dma((5,)), dma, dma((8,)), dma((8,)), dma((8,)), dma((8,)), dma((4,)), dma((4,)),
            dma((3, 4)), dma((3, 4)), dma((3, 4, 4)), dma((3, 4, 4)), dma((3, 4, 4)), dma((3, 4, 4)),
            dma((3, 4)), dma((3, 4)), dma((3, 4)), dma((3, 4)),
            dma((3, 3, 6)), dma((3, 3, 6)),
        ],
        compiler_params=pltpu.CompilerParams(
            collective_id=1, has_side_effects=True, vmem_limit_bytes=56 * 2**20
        ),
        name="layer",
    )(attended, residual, routes, gain, router, w_uv, w_out, w_gate, w_up, w_down)


def shards(
    cache_pool,
    page_table,
    page_counts,
    queries,
    new_latent,
    residual,
    w_uv,
    w_out,
    norm_gain,
    w_router,
    w_gate,
    w_up,
    w_down,
    routes,
):
    table = page_table.T
    incoming = exchange(table, jnp.transpose(cache_pool, (1, 2, 0))).reshape(-1, 3, 96, 128)
    attended = attend(table, page_counts, queries, new_latent, incoming)
    out = layer(
        attended, residual, routes, norm_gain, w_router.T, w_uv, w_out, w_gate, w_up, w_down
    )
    return out.astype(BF16)


def solution(mesh):
    return jax.shard_map(
        shards,
        mesh=mesh,
        in_specs=(
            P(("dp", "ep"), None, None),
            P(),
            P(("dp", "ep"), None),
            P(None, ("dp", "ep"), None, None),
            P(None, ("dp", "ep"), None),
            P(None, ("dp", "ep"), None),
            P("ep", None, None),
            P("ep", None),
            P(),
            P(),
            P("dp", None, "ep"),
            P("dp", None, "ep"),
            P("dp", "ep", None),
            P(None, ("dp", "ep"), None),
        ),
        out_specs=P(None, ("dp", "ep"), None),
        check_vma=False,
    )
```

```python
import functools

import jax
import jax.numpy as jnp
from jax import lax
from jax.experimental import pallas as pl
from jax.experimental.pallas import tpu as pltpu
from jax.sharding import PartitionSpec as P

MESH = pl.DeviceIdType.MESH
F32 = jnp.float32
BF16 = jnp.bfloat16

LATENT = 512
ROPE = 64
PAGE = 64
TILE = 16
score_scale = 192.0 ** (-0.5)
route_scale = 2.5
norm_eps = 1e-06

HALF = 1792
PART = 640
ORDERS = ((0, 1, 2), (1, 2, 0), (2, 0, 1))
WIDTHS = (640, 640, 512)


def exchange_kernel(
    table, pool, out,
    table_v, pool_v, slots, held1, held2, stage,
    psem, lsem, send1, recv1, send2, recv2, send3, recv3,
):
    dp = lax.axis_index("dp")
    ep = lax.axis_index("ep")
    pos = (dp // 4, dp % 4, ep // 2)
    core = ep % 2
    other = 1 - core
    whole = pl.ds(0, 4)

    loads = [
        pltpu.make_async_copy(
            pool.at[pl.ds(i * 16, 16)], pool_v.at[pl.ds(i * 16, 16)], psem.at[i]
        )
        for i in range(4)
    ]
    table_load = pltpu.make_async_copy(table, table_v, psem.at[4])
    table_load.start()
    for load in loads:
        load.start()

    def along(axis, delta, c):
        coords = list(pos)
        coords[axis] = (coords[axis] + delta) % 4
        return (coords[0] * 4 + coords[1], coords[2] * 2 + c)

    def spec_of(order, values):
        spec = [None, None, None]
        for axis, value in zip(order, values):
            spec[axis] = value
        return tuple(spec)

    barrier = pltpu.get_barrier_semaphore()
    peers = [along(a, d, c) for a in range(3) for d in (1, 2, 3) for c in (core, other)]
    peers.append(along(0, 0, other))
    for peer in peers:
        pl.semaphore_signal(barrier, inc=1, device_id=peer, device_id_type=MESH)

    table_load.wait()
    pages = table_v[...]
    wanted = jnp.where(pages // 128 == dp * 8 + ep, pages % 128, 0)
    wanted = jnp.sum(wanted, axis=0, keepdims=True)
    page = lax.broadcasted_iota(jnp.int32, (128, 128), 0)
    onehot = jnp.transpose(jnp.where(wanted == page, 1.0, 0.0)).astype(BF16)

    def put(cls, row, pieces):
        for j in range(0, 16, 4):
            x = jnp.concatenate(pieces(j), axis=0)
            y = lax.dot_general(onehot, x, (((1,), (1,)), ((), ())), preferred_element_type=F32)
            for i in range(4):
                stage[:, j + i, :] = y[:, i * 128 : (i + 1) * 128]
        block = stage[...].astype(BF16).reshape(4, 4, 4, 2, 16, 128)
        slots[cls, :, :, :, :, row : row + 16, :] = block

    def latent_rows(cls, chunk, unit, row):
        def pieces(j):
            t = unit * 16 + j
            return [pool_v[pl.ds(t, 4), chunk * 128 : (chunk + 1) * 128, :].reshape(512, 128)]

        put(cls, row, pieces)

    def rope_rows(cls, unit, row):
        def pieces(j):
            found = []
            for i in range(4):
                found.append(pool_v[unit * 16 + j + i, 512:576, :])
                found.append(pool_v[32 + unit * 16 + j + i, 512:576, :])
            return found

        put(cls, row, pieces)

    def remote(src, dst, ssem, rsem, peer):
        pltpu.make_async_remote_copy(
            src_ref=src, dst_ref=dst, send_sem=ssem, recv_sem=rsem,
            device_id=peer, device_id_type=MESH,
        ).start()

    def landed(ref, sem):
        pltpu.make_async_copy(ref, ref, sem).wait()

    for part in range(6):
        rows = pl.ds(part * 16, 16)
        if part < 4:
            loads[part].wait()
        for cls, order in enumerate(ORDERS):
            a1, a2, a3 = order
            if part < 4:
                latent_rows(cls, cls, part, 16 * part)
            elif cls < 2:
                latent_rows(cls, 3, 2 * cls + part - 4, 16 * part)
            else:
                rope_rows(cls, part - 4, 16 * part)
            if part == 0 and cls == 0:
                pl.semaphore_wait(barrier, len(peers))
            for d in (1, 2, 3):
                src = spec_of(order, ((pos[a1] + d) % 4, whole, whole))
                dst = spec_of(order, (pos[a1], whole, whole))
                remote(
                    slots.at[(cls,) + src + (pl.ds(0, 2), rows)],
                    held1.at[(cls,) + dst + (pl.ds(0, 2), rows)],
                    send1.at[cls], recv1.at[cls, d], along(a1, d, core),
                )
            if part == 5:
                own = (cls,) + spec_of(order, (pos[a1], whole, whole))
                pltpu.make_async_copy(slots.at[own], held1.at[own], lsem.at[cls]).start()

    def second(cls, buf, e):
        a1, a2, a3 = order = ORDERS[cls]
        src1 = (pos[a1] + 4 - e) % 4
        for d in (1, 2, 3):
            src = spec_of(order, (src1, (pos[a2] + d) % 4, whole))
            dst = spec_of(order, (src1, pos[a2], whole))
            remote(
                buf.at[(cls,) + src], held2.at[(cls,) + dst],
                send2.at[cls], recv2.at[cls, d], along(a2, d, core),
            )

    def third(cls, buf, f):
        a1, a2, a3 = order = ORDERS[cls]
        src2 = (pos[a2] + 4 - f) % 4
        for d in (1, 2, 3, 0):
            for k, c in ((0, core), (1, other)):
                src = spec_of(order, (whole, src2, (pos[a3] + d) % 4))
                dst = spec_of(order, (whole, src2, pos[a3]))
                a = buf.at[(cls,) + src + (c,)]
                b = out.at[dst + (core, cls)]
                if d == 0 and k == 0:
                    pltpu.make_async_copy(a, b, recv3.at[cls]).start()
                else:
                    remote(a, b, send3.at[cls, d], recv3.at[cls], along(a3, d, c))

    for cls in range(3):
        second(cls, slots, 0)
    for e in (1, 3, 2):
        for cls, order in enumerate(ORDERS):
            src1 = (pos[order[0]] + 4 - e) % 4
            landed(held1.at[(cls,) + spec_of(order, (src1, whole, whole))], recv1.at[cls, e])
            second(cls, held1, e)
    for cls, order in enumerate(ORDERS):
        own = spec_of(order, (pos[order[0]], whole, whole))
        landed(held1.at[(cls,) + own], lsem.at[cls])
        third(cls, held1, 0)
    for f in (1, 3, 2):
        for cls, order in enumerate(ORDERS):
            a1, a2, a3 = order
            at = spec_of(order, (whole, (pos[a2] + 4 - f) % 4, whole))
            landed(held2.at[(cls,) + at], recv2.at[cls, f])
            third(cls, held2, f)
    for cls in range(3):
        most = held1.at[cls, pl.ds(0, 3)]
        landed(most, send1.at[cls])
        landed(most, send2.at[cls])
    for cls in range(3):
        landed(held1.at[cls, 0, pl.ds(0, 2)], send3.at[cls, 0])
        for d in (1, 2, 3):
            landed(held1.at[cls, 0], send3.at[cls, d])
    for cls in range(3):
        landed(out.at[:, :, :, :, cls], recv3.at[cls])


def exchange(table, pool):
    hbm = pl.BlockSpec(memory_space=pl.ANY)
    dma = pltpu.SemaphoreType.DMA
    held = (3, 4, 4, 4, 2, 96, 128)
    return pl.pallas_call(
        exchange_kernel,
        out_shape=jax.ShapeDtypeStruct((4, 4, 4, 2, 3, 96, 128), BF16),
        in_specs=[hbm, hbm],
        out_specs=hbm,
        scratch_shapes=[
            pltpu.VMEM(table.shape, jnp.int32),
            pltpu.VMEM(pool.shape, BF16),
            pltpu.VMEM(held, BF16),
            pltpu.VMEM(held, BF16),
            pltpu.VMEM(held, BF16),
            pltpu.VMEM((128, 16, 128), F32),
            dma((5,)), dma((3,)), dma((3,)), dma((3, 4)), dma((3,)), dma((3, 4)), dma((3, 4)), dma((3,)),
        ],
        compiler_params=pltpu.CompilerParams(
            collective_id=2, has_side_effects=True, vmem_limit_bytes=56 * 2**20
        ),
        name="exchange",
    )(table, pool)


def attend_kernel(
    table, counts, queries, new, slots, out_ref, q_ref, new_ref, own_ref, keys, scores, sem, in_sem
):
    pages = 64
    me = lax.axis_index("dp") * 8 + lax.axis_index("ep")

    loads = [
        pltpu.make_async_copy(queries, q_ref, in_sem.at[0]),
        pltpu.make_async_copy(new, new_ref, in_sem.at[1]),
    ]
    loads[1].start()

    def fetch(j, _):
        pltpu.make_async_copy(slots.at[table[j, me] // 128], keys.at[j], sem).start()
        return 0

    lax.fori_loop(0, pages, fetch, 0)
    loads[0].start()

    def clear(j, _):
        keys[pages + j] = jnp.zeros((3, 96, 128), BF16)
        return 0

    lax.fori_loop(0, TILE, clear, 0)
    own_ref[...] = jnp.zeros_like(own_ref)
    loads[1].wait()
    for step in range(2):
        fresh = new_ref[step].astype(F32)
        for r in range(4):
            own_ref[r, step : step + 1, :] = fresh[r : r + 1]
    loads[0].wait()
    filled = keys.at[pl.ds(0, pages)]
    pltpu.make_async_copy(filled, filled, sem).wait()
    width = TILE * PAGE
    step_of = lax.broadcasted_iota(jnp.int32, (128, 16), 0) // 64
    token = lax.broadcasted_iota(jnp.int32, (128, 16), 1)
    low = lax.broadcasted_iota(jnp.int32, (TILE, 32, 128), 2) < ROPE

    def values_of(page):
        parts = [keys[pl.ds(page, TILE), k, 0:64, :].reshape(width, 128) for k in range(3)]
        parts.append(keys[pl.ds(page, TILE), 0:2, 64:96, :].reshape(width, 128))
        return jnp.concatenate(parts, axis=1)

    def request(r, start):
        q = jnp.concatenate([q_ref[0, r], q_ref[1, r]], axis=0)
        own = own_ref[r].astype(BF16)
        s_own = lax.dot_general(q, own, (((1,), (1,)), ((), ())), preferred_element_type=F32)
        s_own = jnp.where(token <= step_of, s_own * score_scale, -jnp.inf)
        q_rope = q[:, LATENT:]
        q_wide = jnp.concatenate([q[:, :LATENT], q_rope, q_rope], axis=1)
        length = counts[0, r] * PAGE
        tiles = (length + width - 1) // width

        def score(t, top):
            page = start + t * TILE
            rope = keys[pl.ds(page, TILE), 2, 64:96, :]
            zero = jnp.zeros_like(rope)
            pair = jnp.concatenate([jnp.where(low, rope, zero), jnp.where(low, zero, rope)], axis=1)
            key = jnp.concatenate([values_of(page), pair.reshape(width, 128)], axis=1)
            s = lax.dot_general(q_wide, key, (((1,), (1,)), ((), ())), preferred_element_type=F32)
            place = t * width + lax.broadcasted_iota(jnp.int32, (128, width), 1)
            s = jnp.where(place < length, s * score_scale, -jnp.inf)
            scores[t] = s
            return jnp.maximum(top, jnp.max(s, axis=1, keepdims=True))

        top = lax.fori_loop(0, tiles, score, jnp.max(s_own, axis=1, keepdims=True))
        p_own = jnp.exp(s_own - top)
        total = jnp.sum(p_own, axis=1, keepdims=True)
        acc = jnp.dot(p_own.astype(BF16), own[:, :LATENT], preferred_element_type=F32)

        def mix(t, carry):
            total, acc = carry
            p = jnp.exp(scores[t] - top)
            total = total + jnp.sum(p, axis=1, keepdims=True)
            acc = acc + jnp.dot(
                p.astype(BF16), values_of(start + t * TILE), preferred_element_type=F32
            )
            return total, acc

        total, acc = lax.fori_loop(0, tiles, mix, (total, acc))
        res = (acc / total).reshape(2, 8, 8, LATENT)
        at = pl.multiple_of(r * 16, 16)
        for g in range(8):
            block = jnp.concatenate([res[0, g], res[1, g]], axis=0)
            out_ref[g, pl.ds(at, 16), :] = block.astype(BF16)
        return start + counts[0, r]

    lax.fori_loop(0, 4, request, 0)


def attend(table, counts, queries, new_latent, slots):
    smem = pl.BlockSpec(memory_space=pltpu.SMEM)
    vmem = pl.BlockSpec(memory_space=pltpu.VMEM)
    return pl.pallas_call(
        attend_kernel,
        out_shape=jax.ShapeDtypeStruct((8, 64, LATENT), BF16),
        in_specs=[smem, smem] + [pl.BlockSpec(memory_space=pl.ANY)] * 3,
        out_specs=vmem,
        scratch_shapes=[
            pltpu.VMEM(queries.shape, BF16),
            pltpu.VMEM(new_latent.shape, BF16),
            pltpu.VMEM((4, 16, LATENT + ROPE), F32),
            pltpu.VMEM((64 + TILE, 3, 96, 128), BF16),
            pltpu.VMEM((32 // TILE, 128, TILE * PAGE), F32),
            pltpu.SemaphoreType.DMA,
            pltpu.SemaphoreType.DMA((2,)),
        ],
        compiler_params=pltpu.CompilerParams(vmem_limit_bytes=60 * 2**20),
        name="attend",
    )(table, counts, queries, new_latent, slots)


def layer_kernel(
    attended, residual_in, routes_in, gain_in, router_in, w_uv, w_out, w_gate, w_up, w_down,
    out_ref,
    residual, routes, gain, router, resid, member, heads_in, masked, part_out, part_in, res_all, mem_all, stat_out, stat_in, hidden,
    gath, v_uv, v_out, v_gate, v_up, v_down, acc, inner,
    mix, sib_out, sib_in, t1, ul1, ur1, t2, last, fin_out, fin_in,
    wsem, lsem, head_s, head_r, part_s, part_r, pair_s, pair_r,
    ag1_s, ag1_r, ag2_s, ag2_r, ag3_s, ag3_r, sib_s, sib_r, red_s, red_r, sum_s, sum_r,
):
    dp = lax.axis_index("dp")
    ep = lax.axis_index("ep")
    pos = (dp // 4, dp % 4, ep // 2)
    core = ep % 2
    other = 1 - core

    def device(coords, c):
        return (coords[0] * 4 + coords[1], coords[2] * 2 + c)

    def along(axis, delta):
        coords = [pos[0], pos[1], pos[2]]
        coords[axis] = (coords[axis] + delta) % 4
        return device(coords, core)

    sibling = device(pos, other)
    ep_peers = [(dp, (ep + o) % 8) for o in range(1, 8)]
    ring_peers = [along(a, d) for a in (0, 1) for d in (1, 2, 3)]

    def remote(src, dst, ssem, rsem, peer):
        copy = pltpu.make_async_remote_copy(
            src_ref=src, dst_ref=dst, send_sem=ssem, recv_sem=rsem,
            device_id=peer, device_id_type=MESH,
        )
        copy.start()
        sent.append((src, ssem))

    def landed(ref, rsem):
        pltpu.make_async_copy(ref, ref, rsem).wait()

    sent = []

    def settle():
        for src, ssem in sent:
            pltpu.make_async_copy(src, src, ssem).wait()
        sent.clear()

    barrier = pltpu.get_barrier_semaphore()
    for peer in ep_peers + ring_peers:
        pl.semaphore_signal(barrier, inc=1, device_id=peer, device_id_type=MESH)

    loads = [(residual_in, residual), (routes_in, routes), (gain_in, gain), (router_in, router)]
    small = [pltpu.make_async_copy(a, b, lsem.at[1 + i]) for i, (a, b) in enumerate(loads)]
    loads = [(w_uv, v_uv), (w_out, v_out), (w_gate, v_gate), (w_up, v_up), (w_down, v_down)]
    copies = [pltpu.make_async_copy(a, b, wsem.at[i]) for i, (a, b) in enumerate(loads)]
    for copy in small + copies:
        copy.start()
    pl.semaphore_wait(barrier, len(ep_peers) + len(ring_peers))

    for o in range(1, 8):
        to = (ep + o) % 8
        remote(attended.at[to], heads_in.at[ep], head_s.at[o], head_r.at[o], (dp, to))
    own_heads = pltpu.make_async_copy(attended.at[ep], heads_in.at[ep], lsem.at[0])
    own_heads.start()

    for copy in small:
        copy.wait()
    for h in range(2):
        cols = slice(h * HALF, (h + 1) * HALF)
        both = [residual[s, :, cols].astype(F32) for s in range(2)]
        resid[h] = jnp.concatenate(both, axis=0)
    route = jnp.concatenate([routes[0], routes[1]], axis=0)
    lanes = lax.broadcasted_iota(jnp.int32, (8, 128), 1)
    named = jnp.zeros((8, 128), F32)
    for k in range(8):
        named = jnp.where(route[:, k : k + 1] == lanes, 1.0, named)
    member[...] = named
    own_rows = pl.ds(pl.multiple_of(core * 8, 8), 8)
    other_rows = pl.ds(pl.multiple_of(other * 8, 8), 8)
    remote(resid.at[other], res_all.at[own_rows], pair_s.at[0], pair_r.at[0], sibling)
    remote(member, mem_all.at[own_rows], pair_s.at[1], pair_r.at[1], sibling)
    res_all[own_rows, :] = resid[core]
    mem_all[own_rows, :] = member[...]

    def clear(i, _):
        acc[0, i] = jnp.zeros((4, 4, 16, 256), F32)
        acc[1, i] = jnp.zeros((4, 4, 16, 256), F32)
        return 0

    lax.fori_loop(0, 4, clear, 0)
    own_heads.wait()
    for o in range(1, 8):
        landed(heads_in.at[(ep + 8 - o) % 8], head_r.at[o])

    copies[0].wait()
    x = heads_in[...].reshape(512, LATENT)
    row_head = lax.broadcasted_iota(jnp.int32, (512, 128), 0) % 8
    for h in range(8):
        y = jnp.dot(x, v_uv[h], preferred_element_type=F32)
        masked[:, h * 128 : (h + 1) * 128] = jnp.where(row_head == h, y, 0.0).astype(BF16)
    to_row = lax.broadcasted_iota(jnp.int32, (64, 512), 0)
    from_row = lax.broadcasted_iota(jnp.int32, (64, 512), 1) // 8
    wanted = (to_row // 8) * 8 + (to_row % 4) * 2 + (to_row % 8) // 4
    pick = jnp.where(from_row == wanted, 1.0, 0.0).astype(BF16)
    flat = jnp.dot(pick, masked[...], preferred_element_type=F32).astype(BF16)

    copies[1].wait()
    for h, turns in ((other, (1, 3, 5, 7)), (core, (2, 4, 6))):
        for t in range(HALF // 256):
            cols = pl.ds(pl.multiple_of(h * HALF + t * 256, 256), 256)
            y = jnp.dot(flat, v_out[:, cols], preferred_element_type=F32)
            part_out[h, :, :, t * 256 : (t + 1) * 256] = y.astype(BF16).reshape(4, 16, 256)
        for o in turns:
            to = (ep + o) % 8
            remote(part_out.at[h, to // 2], part_in.at[ep], part_s.at[o], part_r.at[o], (dp, to))
    landed(res_all.at[other_rows], pair_r.at[0])
    landed(mem_all.at[other_rows], pair_r.at[1])
    hid = part_out[core, pos[2]].astype(F32)
    settle()
    for o in range(1, 8):
        src = (ep + 8 - o) % 8
        landed(part_in.at[src], part_r.at[o])
        hid = hid + part_in[src].astype(F32)
    hid = hid + res_all[...]
    hidden[...] = hid

    half_cols = pl.ds(pl.multiple_of(core * HALF, 128), HALF)
    scaled = hid * gain[half_cols].reshape(1, HALF)
    stat_out[0] = jnp.zeros((16, 128), F32)
    stat_out[0, :, 0:16] = lax.dot_general(
        scaled, router[:, half_cols], (((1,), (1,)), ((), ())),
        preferred_element_type=F32, precision=lax.Precision.HIGHEST,
    )
    stat_out[1] = jnp.broadcast_to(jnp.sum(hid * hid, axis=1, keepdims=True), (16, 128))
    remote(stat_out, stat_in, pair_s.at[2], pair_r.at[2], sibling)
    landed(stat_in, pair_r.at[2])
    square = stat_out[1] + stat_in[1]
    inv = lax.rsqrt(square / (2 * HALF) + norm_eps)
    affinity = jax.nn.sigmoid((stat_out[0] + stat_in[0]) * inv) * mem_all[...]
    gates = route_scale * affinity / jnp.sum(affinity, axis=1, keepdims=True)
    coarse = gates.astype(BF16)
    fine = (gates - coarse.astype(F32)).astype(BF16)
    normed = (scaled * inv[:, 0:1]).astype(BF16)
    z, xx, yy = pos
    gath[core, 0, z, xx, yy] = normed[:, 0:640]
    gath[core, 1, z, xx, yy] = normed[:, 640:1280]
    gath[core, 2, z, xx, yy, :, 0:512] = normed[:, 1280:1792]
    gath[core, 2, z, xx, yy, :, 512:640] = jnp.where(core == 0, coarse, fine)

    whole = pl.ds(0, 4)
    halves = (pl.ds(0, 2), pl.ds(2, 2))

    def g_at(cls, spec):
        return gath.at[core, cls, spec[0], spec[1], spec[2]]

    def spec_of(order, values):
        spec = [None, None, None]
        for axis, value in zip(order, values):
            spec[axis] = value
        return spec

    def line(cls, e, f):
        a1, a2, a3 = ORDERS[cls]
        where = spec_of((a1, a2, a3), ((pos[a1] + 4 - e) % 4, (pos[a2] + 4 - f) % 4, pos[a3]))
        return g_at(cls, where)

    def quarter(cls, f, shift, half=whole):
        a1, a2, a3 = ORDERS[cls]
        at = (half, (pos[a2] + 4 - f) % 4, (pos[a3] + shift) % 4)
        return g_at(cls, spec_of((a1, a2, a3), at))

    def plane_at(cls, shift):
        a1, a2, a3 = ORDERS[cls]
        return tuple(spec_of((a1, a2, a3), (whole, whole, (pos[a3] + shift) % 4)))

    def to_pair(cls, k, shift):
        plane = gath.at[(core, cls) + plane_at(cls, shift)]
        remote(plane, plane, sib_s.at[cls, k], sib_r.at[cls, k], sibling)

    def second(cls, e):
        b = line(cls, e, 0)
        for d in (1, 3, 2):
            remote(b, b, ag2_s.at[cls, d, e], ag2_r.at[cls, d], along(ORDERS[cls][1], d))

    def third(cls, f):
        b = quarter(cls, f, 0)
        for k, d in ((0, 1), (1, 3)):
            remote(b, b, ag3_s.at[cls, f, k], ag3_r.at[cls, f, k], along(ORDERS[cls][2], d))

    for cls, order in enumerate(ORDERS):
        own = g_at(cls, pos)
        for d in (1, 3, 2):
            remote(own, own, ag1_s.at[cls, d], ag1_r.at[cls, d], along(order[0], d))
    for cls in range(3):
        second(cls, 0)
    for e in (1, 3, 2):
        for cls in range(3):
            landed(line(cls, e, 0), ag1_r.at[cls, e])
            second(cls, e)
    for cls in range(3):
        third(cls, 0)
    for f in (1, 3, 2):
        for cls in range(3):
            landed(quarter(cls, f, 0), ag2_r.at[cls, f])
            third(cls, f)
    for cls in range(3):
        to_pair(cls, 0, 0)
    for f in (0, 1, 3, 2):
        for cls, order in enumerate(ORDERS):
            landed(quarter(cls, f, 3), ag3_r.at[cls, f, 0])
            b = quarter(cls, f, 3, halves[0])
            remote(b, b, ag3_s.at[cls, f, 2], ag3_r.at[cls, f, 2], along(order[2], 1))
            landed(quarter(cls, f, 1), ag3_r.at[cls, f, 1])
            b = quarter(cls, f, 1, halves[1])
            remote(b, b, ag3_s.at[cls, f, 3], ag3_r.at[cls, f, 3], along(order[2], 3))
    for k, shift in ((1, 3), (2, 1)):
        for cls in range(3):
            to_pair(cls, k, shift)

    for copy in copies[2:]:
        copy.wait()

    def expert_in(h, cls, shift):
        at = plane_at(cls, shift)
        n = WIDTHS[cls]
        x = gath[(h, cls) + at].reshape(256, PART)[:, :n]
        rows = pl.ds(pl.multiple_of(h * HALF + cls * PART, 128), n)
        for k, w in enumerate((v_gate, v_up)):
            y = jnp.dot(x, w[0, rows, :], preferred_element_type=F32).reshape(4, 4, 16, 256)
            acc[(k,) + at] = acc[(k,) + at] + y

    def from_pair(cls, k, shift):
        landed(gath.at[(other, cls) + plane_at(cls, shift)], sib_r.at[cls, k])

    for cls in range(3):
        expert_in(core, cls, 0)
    for cls in range(3):
        from_pair(cls, 0, 0)
        expert_in(other, cls, 0)
    for k, shift in ((1, 3), (2, 1)):
        for cls in range(3):
            expert_in(core, cls, shift)
    for cls in range(3):
        for f in range(4):
            landed(quarter(cls, f, 2, halves[0]), ag3_r.at[cls, f, 2])
            landed(quarter(cls, f, 2, halves[1]), ag3_r.at[cls, f, 3])
        to_pair(cls, 3, 2)
    for k, shift in ((1, 3), (2, 1)):
        for cls in range(3):
            from_pair(cls, k, shift)
            expert_in(other, cls, shift)
    for cls in range(3):
        expert_in(core, cls, 2)
    for cls in range(3):
        from_pair(cls, 3, 2)
        expert_in(other, cls, 2)

    lane = lax.broadcasted_iota(jnp.int32, (256, 128), 1)

    def activate(i, _):
        both = gath[0, 2, i, :, :, :, 512:640].astype(F32) + gath[1, 2, i, :, :, :, 512:640].astype(F32)
        weight = jnp.sum(jnp.where(lane == dp, both.reshape(256, 128), 0.0), axis=1, keepdims=True)
        gate = acc[0, i].reshape(256, 256)
        act = gate / (1.0 + jnp.exp(-gate)) * acc[1, i].reshape(256, 256) * weight
        inner[i] = act.astype(BF16).reshape(4, 4, 16, 256)
        return 0

    lax.fori_loop(0, 4, activate, 0)

    def expert_out(half, cls, at):
        cols = pl.ds(pl.multiple_of(half * HALF + cls * PART, 128), WIDTHS[cls])
        act = inner[at].reshape(256, 256)
        y = jnp.dot(act, v_down[0, :, cols], preferred_element_type=F32)
        return y.reshape(4, 4, 16, WIDTHS[cls])

    def for_pair(shift):
        for cls in range(3):
            at = plane_at(cls, shift)
            b = (cls,) + at + (slice(None), pl.ds(0, WIDTHS[cls]))
            sib_out[b] = expert_out(other, cls, at).astype(BF16)
            remote(sib_out.at[b], sib_in.at[b], red_s.at[cls, shift], red_r.at[cls, shift], sibling)

    def for_self(shift):
        for cls in range(3):
            at = plane_at(cls, shift)
            b = (cls,) + at + (slice(None), pl.ds(0, WIDTHS[cls]))
            y = expert_out(core, cls, at)
            landed(sib_in.at[b], red_r.at[cls, shift])
            mix[b] = (y + sib_in[b].astype(F32)).astype(BF16)

    def block(cls, shift, half):
        a1, a2, a3 = ORDERS[cls]
        spec = spec_of((a1, a2, a3), (half, whole, (pos[a3] + shift) % 4))
        return (cls, spec[0], spec[1], spec[2], slice(None), pl.ds(0, WIDTHS[cls]))

    def temp(cls, half):
        a1, a2, a3 = ORDERS[cls]
        first, then = (half, whole) if a1 < a2 else (whole, half)
        return (cls, first, then, slice(None), pl.ds(0, WIDTHS[cls]))

    def send(cls, shift, half, buf, k, delta):
        remote(
            mix.at[block(cls, shift, halves[half])], buf.at[temp(cls, halves[half])],
            sum_s.at[cls, 0, k], sum_r.at[cls, 0, k], along(ORDERS[cls][2], delta),
        )

    for_pair(2)
    for_pair(1)
    for_self(2)
    for cls in range(3):
        send(cls, 2, 0, t1, 0, 1)
        send(cls, 2, 1, t1, 1, 3)
    for_pair(3)
    for_self(1)
    for cls in range(3):
        send(cls, 1, 1, ul1, 2, 1)
    for_self(3)
    for cls in range(3):
        send(cls, 3, 0, ur1, 3, 3)
    for cls in range(3):
        for half, shift, buf, k, delta in ((0, 1, ul1, 0, 1), (1, 3, ur1, 1, 3)):
            at, tmp = block(cls, shift, halves[half]), temp(cls, halves[half])
            landed(t1.at[tmp], sum_r.at[cls, 0, k])
            mix[at] = (mix[at].astype(F32) + t1[tmp].astype(F32)).astype(BF16)
            send(cls, shift, half, buf, k + 4, delta)
    for_pair(0)
    for_self(0)
    settle()
    for cls, order in enumerate(ORDERS):
        a1, a2, a3 = order
        n = WIDTHS[cls]
        for half, ks in ((0, (4, 3)), (1, (2, 5))):
            tmp = temp(cls, halves[half])
            landed(ul1.at[tmp], sum_r.at[cls, 0, ks[0]])
            landed(ur1.at[tmp], sum_r.at[cls, 0, ks[1]])
        for d in (2, 1, 3, 0):
            where = (pos[a2] + d) % 4
            spec = spec_of(order, (whole, where, pos[a3]))
            at = (cls, spec[0], spec[1], spec[2], slice(None), pl.ds(0, n))
            first, then = (whole, where) if a1 < a2 else (where, whole)
            tmp = (cls, first, then, slice(None), pl.ds(0, n))
            total = mix[at].astype(F32) + ul1[tmp].astype(F32) + ur1[tmp].astype(F32)
            mix[at] = total.astype(BF16)
            if d:
                dst = t2.at[cls, d - 1, :, :, pl.ds(0, n)]
                remote(mix.at[at], dst, sum_s.at[cls, 1, d], sum_r.at[cls, 1, d], along(a2, d))
    for cls, order in enumerate(ORDERS):
        a1, a2, a3 = order
        n = WIDTHS[cls]
        for d in (1, 3, 2):
            landed(t2.at[cls, d - 1, :, :, pl.ds(0, n)], sum_r.at[cls, 1, d])
        for d in (2, 1, 3, 0):
            where = (pos[a1] + d) % 4
            coords = list(pos)
            coords[a1] = where
            at = (cls, coords[0], coords[1], coords[2], slice(None), pl.ds(0, n))
            total = mix[at].astype(F32)
            for k in range(3):
                total = total + t2[cls, k, where, :, 0:n].astype(F32)
            mix[at] = total.astype(BF16)
            if d:
                dst = last.at[cls, d - 1, :, pl.ds(0, n)]
                remote(mix.at[at], dst, sum_s.at[cls, 2, d], sum_r.at[cls, 2, d], along(a1, d))
    for cls in range(3):
        n = WIDTHS[cls]
        total = mix[cls, pos[0], pos[1], pos[2], :, 0:n].astype(F32)
        for d in (1, 2, 3):
            landed(last.at[cls, d - 1, :, pl.ds(0, n)], sum_r.at[cls, 2, d])
            total = total + last[cls, d - 1, :, 0:n].astype(F32)
        total = total + hidden[:, cls * PART : cls * PART + n]
        fin_out[0, :, cls * PART : cls * PART + n] = total[0:8]
        fin_out[1, :, cls * PART : cls * PART + n] = total[8:16]
    remote(fin_out.at[other], fin_in, pair_s.at[3], pair_r.at[3], sibling)
    for s in range(2):
        out_ref[s, :, half_cols] = fin_out[core, s * 4 : s * 4 + 4]
    settle()
    landed(fin_in, pair_r.at[3])
    for s in range(2):
        cols = pl.ds(pl.multiple_of(other * HALF, 128), HALF)
        out_ref[s, :, cols] = fin_in[s * 4 : s * 4 + 4]


def layer(attended, residual, routes, gain, router, w_uv, w_out, w_gate, w_up, w_down):
    vmem = pl.BlockSpec(memory_space=pltpu.VMEM)
    hbm = pl.BlockSpec(memory_space=pl.ANY)
    dma = pltpu.SemaphoreType.DMA
    grid = (3, 4, 4, 4, 16, PART)
    return pl.pallas_call(
        layer_kernel,
        out_shape=jax.ShapeDtypeStruct((2, 4, 2 * HALF), F32),
        in_specs=[hbm] * 10,
        out_specs=vmem,
        scratch_shapes=[
            pltpu.VMEM(residual.shape, BF16),
            pltpu.VMEM(routes.shape, jnp.int32),
            pltpu.VMEM(gain.shape, F32),
            pltpu.VMEM(router.shape, F32),
            pltpu.VMEM((2, 8, HALF), F32),
            pltpu.VMEM((8, 128), F32),
            pltpu.VMEM((8, 64, LATENT), BF16),
            pltpu.VMEM((512, 1024), BF16),
            pltpu.VMEM((2, 4, 16, HALF), BF16),
            pltpu.VMEM((8, 16, HALF), BF16),
            pltpu.VMEM((16, HALF), F32),
            pltpu.VMEM((16, 128), F32),
            pltpu.VMEM((2, 16, 128), F32),
            pltpu.VMEM((2, 16, 128), F32),
            pltpu.VMEM((16, HALF), F32),
            pltpu.VMEM((2,) + grid, BF16),
            pltpu.VMEM(w_uv.shape, BF16),
            pltpu.VMEM(w_out.shape, BF16),
            pltpu.VMEM(w_gate.shape, BF16),
            pltpu.VMEM(w_up.shape, BF16),
            pltpu.VMEM(w_down.shape, BF16),
            pltpu.VMEM((2, 4, 4, 4, 16, 256), F32),
            pltpu.VMEM((4, 4, 4, 16, 256), BF16),
            pltpu.VMEM(grid, BF16),
            pltpu.VMEM(grid, BF16),
            pltpu.VMEM(grid, BF16),
            pltpu.VMEM((3, 4, 4, 16, PART), BF16),
            pltpu.VMEM((3, 4, 4, 16, PART), BF16),
            pltpu.VMEM((3, 4, 4, 16, PART), BF16),
            pltpu.VMEM((3, 3, 4, 16, PART), BF16),
            pltpu.VMEM((3, 3, 16, PART), BF16),
            pltpu.VMEM((2, 8, HALF), F32),
            pltpu.VMEM((8, HALF), F32),
            dma((5,)), dma((5,)), dma((8,)), dma((8,)), dma((8,)), dma((8,)), dma((4,)), dma((4,)),
            dma((3, 4)), dma((3, 4)), dma((3, 4, 4)), dma((3, 4)), dma((3, 4, 4)), dma((3, 4, 4)),
            dma((3, 4)), dma((3, 4)), dma((3, 4)), dma((3, 4)),
            dma((3, 3, 6)), dma((3, 3, 6)),
        ],
        compiler_params=pltpu.CompilerParams(
            collective_id=1, has_side_effects=True, vmem_limit_bytes=56 * 2**20
        ),
        name="layer",
    )(attended, residual, routes, gain, router, w_uv, w_out, w_gate, w_up, w_down)


def shards(
    cache_pool,
    page_table,
    page_counts,
    queries,
    new_latent,
    residual,
    w_uv,
    w_out,
    norm_gain,
    w_router,
    w_gate,
    w_up,
    w_down,
    routes,
):
    table = page_table.T
    incoming = exchange(table, jnp.transpose(cache_pool, (1, 2, 0))).reshape(-1, 3, 96, 128)
    attended = attend(table, page_counts, queries, new_latent, incoming)
    out = layer(
        attended, residual, routes, norm_gain, w_router.T, w_uv, w_out, w_gate, w_up, w_down
    )
    return out.astype(BF16)


def solution(mesh):
    return jax.shard_map(
        shards,
        mesh=mesh,
        in_specs=(
            P(("dp", "ep"), None, None),
            P(),
            P(("dp", "ep"), None),
            P(None, ("dp", "ep"), None, None),
            P(None, ("dp", "ep"), None),
            P(None, ("dp", "ep"), None),
            P("ep", None, None),
            P("ep", None),
            P(),
            P(),
            P("dp", None, "ep"),
            P("dp", None, "ep"),
            P("dp", "ep", None),
            P(None, ("dp", "ep"), None),
        ),
        out_specs=P(None, ("dp", "ep"), None),
        check_vma=False,
    )
```

```python
import functools

import jax
import jax.numpy as jnp
from jax import lax
from jax.experimental import pallas as pl
from jax.experimental.pallas import tpu as pltpu
from jax.sharding import PartitionSpec as P

MESH = pl.DeviceIdType.MESH
F32 = jnp.float32
BF16 = jnp.bfloat16

LATENT = 512
ROPE = 64
PAGE = 64
TILE = 16
score_scale = 192.0 ** (-0.5)
route_scale = 2.5
norm_eps = 1e-06

HALF = 1792
PART = 640
ORDERS = ((0, 1, 2), (1, 2, 0), (2, 0, 1))
WIDTHS = (640, 640, 512)


def exchange_kernel(
    table, pool, out,
    table_v, pool_v, slots, held1, held2, stage,
    psem, lsem, send1, recv1, send2, recv2, send3, recv3,
):
    dp = lax.axis_index("dp")
    ep = lax.axis_index("ep")
    pos = (dp // 4, dp % 4, ep // 2)
    core = ep % 2
    other = 1 - core
    whole = pl.ds(0, 4)

    loads = [
        pltpu.make_async_copy(
            pool.at[pl.ds(i * 16, 16)], pool_v.at[pl.ds(i * 16, 16)], psem.at[i]
        )
        for i in range(4)
    ]
    table_load = pltpu.make_async_copy(table, table_v, psem.at[4])
    table_load.start()
    for load in loads:
        load.start()

    def along(axis, delta, c):
        coords = list(pos)
        coords[axis] = (coords[axis] + delta) % 4
        return (coords[0] * 4 + coords[1], coords[2] * 2 + c)

    def spec_of(order, values):
        spec = [None, None, None]
        for axis, value in zip(order, values):
            spec[axis] = value
        return tuple(spec)

    barrier = pltpu.get_barrier_semaphore()
    peers = [along(a, d, c) for a in range(3) for d in (1, 2, 3) for c in (core, other)]
    peers.append(along(0, 0, other))
    for peer in peers:
        pl.semaphore_signal(barrier, inc=1, device_id=peer, device_id_type=MESH)

    table_load.wait()
    pages = table_v[...]
    wanted = jnp.where(pages // 128 == dp * 8 + ep, pages % 128, 0)
    wanted = jnp.sum(wanted, axis=0, keepdims=True)
    page = lax.broadcasted_iota(jnp.int32, (128, 128), 0)
    onehot = jnp.transpose(jnp.where(wanted == page, 1.0, 0.0)).astype(BF16)

    def put(cls, row, pieces):
        for j in range(0, 16, 4):
            x = jnp.concatenate(pieces(j), axis=0)
            y = lax.dot_general(onehot, x, (((1,), (1,)), ((), ())), preferred_element_type=F32)
            for i in range(4):
                stage[:, j + i, :] = y[:, i * 128 : (i + 1) * 128]
        block = stage[...].astype(BF16).reshape(4, 4, 4, 2, 16, 128)
        slots[cls, :, :, :, :, row : row + 16, :] = block

    def latent_rows(cls, chunk, unit, row):
        def pieces(j):
            t = unit * 16 + j
            return [pool_v[pl.ds(t, 4), chunk * 128 : (chunk + 1) * 128, :].reshape(512, 128)]

        put(cls, row, pieces)

    def rope_rows(cls, unit, row):
        def pieces(j):
            found = []
            for i in range(4):
                found.append(pool_v[unit * 16 + j + i, 512:576, :])
                found.append(pool_v[32 + unit * 16 + j + i, 512:576, :])
            return found

        put(cls, row, pieces)

    def remote(src, dst, ssem, rsem, peer):
        pltpu.make_async_remote_copy(
            src_ref=src, dst_ref=dst, send_sem=ssem, recv_sem=rsem,
            device_id=peer, device_id_type=MESH,
        ).start()

    def landed(ref, sem):
        pltpu.make_async_copy(ref, ref, sem).wait()

    for part in range(6):
        rows = pl.ds(part * 16, 16)
        if part < 4:
            loads[part].wait()
        for cls, order in enumerate(ORDERS):
            a1, a2, a3 = order
            if part < 4:
                latent_rows(cls, cls, part, 16 * part)
            elif cls < 2:
                latent_rows(cls, 3, 2 * cls + part - 4, 16 * part)
            else:
                rope_rows(cls, part - 4, 16 * part)
            if part == 0 and cls == 0:
                pl.semaphore_wait(barrier, len(peers))
            for d in (1, 2, 3):
                src = spec_of(order, ((pos[a1] + d) % 4, whole, whole))
                dst = spec_of(order, (pos[a1], whole, whole))
                remote(
                    slots.at[(cls,) + src + (pl.ds(0, 2), rows)],
                    held1.at[(cls,) + dst + (pl.ds(0, 2), rows)],
                    send1.at[cls], recv1.at[cls, d], along(a1, d, core),
                )
            if part == 5:
                own = (cls,) + spec_of(order, (pos[a1], whole, whole))
                pltpu.make_async_copy(slots.at[own], held1.at[own], lsem.at[cls]).start()

    def second(cls, buf, e):
        a1, a2, a3 = order = ORDERS[cls]
        src1 = (pos[a1] + 4 - e) % 4
        for d in (1, 2, 3):
            src = spec_of(order, (src1, (pos[a2] + d) % 4, whole))
            dst = spec_of(order, (src1, pos[a2], whole))
            remote(
                buf.at[(cls,) + src], held2.at[(cls,) + dst],
                send2.at[cls], recv2.at[cls, d], along(a2, d, core),
            )

    def third(cls, buf, f):
        a1, a2, a3 = order = ORDERS[cls]
        src2 = (pos[a2] + 4 - f) % 4
        for d in (1, 2, 3, 0):
            for k, c in ((0, core), (1, other)):
                src = spec_of(order, (whole, src2, (pos[a3] + d) % 4))
                dst = spec_of(order, (whole, src2, pos[a3]))
                a = buf.at[(cls,) + src + (c,)]
                b = out.at[dst + (core, cls)]
                if d == 0 and k == 0:
                    pltpu.make_async_copy(a, b, recv3.at[cls]).start()
                else:
                    remote(a, b, send3.at[cls, d], recv3.at[cls], along(a3, d, c))

    for cls in range(3):
        second(cls, slots, 0)
    for e in (1, 3, 2):
        for cls, order in enumerate(ORDERS):
            src1 = (pos[order[0]] + 4 - e) % 4
            landed(held1.at[(cls,) + spec_of(order, (src1, whole, whole))], recv1.at[cls, e])
            second(cls, held1, e)
    for cls, order in enumerate(ORDERS):
        own = spec_of(order, (pos[order[0]], whole, whole))
        landed(held1.at[(cls,) + own], lsem.at[cls])
        third(cls, held1, 0)
    for f in (1, 3, 2):
        for cls, order in enumerate(ORDERS):
            a1, a2, a3 = order
            at = spec_of(order, (whole, (pos[a2] + 4 - f) % 4, whole))
            landed(held2.at[(cls,) + at], recv2.at[cls, f])
            third(cls, held2, f)
    for cls in range(3):
        most = held1.at[cls, pl.ds(0, 3)]
        landed(most, send1.at[cls])
        landed(most, send2.at[cls])
    for cls in range(3):
        landed(held1.at[cls, 0, pl.ds(0, 2)], send3.at[cls, 0])
        for d in (1, 2, 3):
            landed(held1.at[cls, 0], send3.at[cls, d])
    for cls in range(3):
        landed(out.at[:, :, :, :, cls], recv3.at[cls])


def exchange(table, pool):
    hbm = pl.BlockSpec(memory_space=pl.ANY)
    dma = pltpu.SemaphoreType.DMA
    held = (3, 4, 4, 4, 2, 96, 128)
    return pl.pallas_call(
        exchange_kernel,
        out_shape=jax.ShapeDtypeStruct((4, 4, 4, 2, 3, 96, 128), BF16),
        in_specs=[hbm, hbm],
        out_specs=hbm,
        scratch_shapes=[
            pltpu.VMEM(table.shape, jnp.int32),
            pltpu.VMEM(pool.shape, BF16),
            pltpu.VMEM(held, BF16),
            pltpu.VMEM(held, BF16),
            pltpu.VMEM(held, BF16),
            pltpu.VMEM((128, 16, 128), F32),
            dma((5,)), dma((3,)), dma((3,)), dma((3, 4)), dma((3,)), dma((3, 4)), dma((3, 4)), dma((3,)),
        ],
        compiler_params=pltpu.CompilerParams(
            collective_id=2, has_side_effects=True, vmem_limit_bytes=56 * 2**20
        ),
        name="exchange",
    )(table, pool)


def attend_kernel(
    table, counts, queries, new, slots, out_ref, q_ref, new_ref, own_ref, keys, scores, sem, in_sem
):
    pages = 64
    me = lax.axis_index("dp") * 8 + lax.axis_index("ep")

    loads = [
        pltpu.make_async_copy(queries, q_ref, in_sem.at[0]),
        pltpu.make_async_copy(new, new_ref, in_sem.at[1]),
    ]
    for load in loads:
        load.start()

    def page_copy(j):
        return pltpu.make_async_copy(slots.at[table[j, me] // 128], keys.at[j], sem.at[j])

    def fetch(j, _):
        page_copy(j).start()
        return 0

    lax.fori_loop(0, pages, fetch, 0)

    def clear(j, _):
        keys[pages + j] = jnp.zeros((3, 96, 128), BF16)
        return 0

    lax.fori_loop(0, TILE, clear, 0)
    own_ref[...] = jnp.zeros_like(own_ref)
    loads[1].wait()
    for step in range(2):
        fresh = new_ref[step].astype(F32)
        for r in range(4):
            own_ref[r, step : step + 1, :] = fresh[r : r + 1]
    loads[0].wait()
    width = TILE * PAGE
    step_of = lax.broadcasted_iota(jnp.int32, (128, 16), 0) // 64
    token = lax.broadcasted_iota(jnp.int32, (128, 16), 1)
    low = lax.broadcasted_iota(jnp.int32, (TILE, 32, 128), 2) < ROPE

    def values_of(page):
        parts = [keys[pl.ds(page, TILE), k, 0:64, :].reshape(width, 128) for k in range(3)]
        parts.append(keys[pl.ds(page, TILE), 0:2, 64:96, :].reshape(width, 128))
        return jnp.concatenate(parts, axis=1)

    def arrive(j, _):
        pltpu.make_async_copy(keys.at[j], keys.at[j], sem.at[j]).wait()
        return 0

    def request(r, carry):
        start, seen = carry
        q = jnp.concatenate([q_ref[0, r], q_ref[1, r]], axis=0)
        own = own_ref[r].astype(BF16)
        s_own = lax.dot_general(q, own, (((1,), (1,)), ((), ())), preferred_element_type=F32)
        s_own = jnp.where(token <= step_of, s_own * score_scale, -jnp.inf)
        q_rope = q[:, LATENT:]
        q_wide = jnp.concatenate([q[:, :LATENT], q_rope, q_rope], axis=1)
        length = counts[0, r] * PAGE
        tiles = (length + width - 1) // width
        needed = jnp.minimum(start + tiles * TILE, pages)
        lax.fori_loop(seen, needed, arrive, 0)

        def score(t, top):
            page = start + t * TILE
            rope = keys[pl.ds(page, TILE), 2, 64:96, :]
            zero = jnp.zeros_like(rope)
            pair = jnp.concatenate([jnp.where(low, rope, zero), jnp.where(low, zero, rope)], axis=1)
            key = jnp.concatenate([values_of(page), pair.reshape(width, 128)], axis=1)
            s = lax.dot_general(q_wide, key, (((1,), (1,)), ((), ())), preferred_element_type=F32)
            place = t * width + lax.broadcasted_iota(jnp.int32, (128, width), 1)
            s = jnp.where(place < length, s * score_scale, -jnp.inf)
            scores[t] = s
            return jnp.maximum(top, jnp.max(s, axis=1, keepdims=True))

        top = lax.fori_loop(0, tiles, score, jnp.max(s_own, axis=1, keepdims=True))
        p_own = jnp.exp(s_own - top)
        total = jnp.sum(p_own, axis=1, keepdims=True)
        acc = jnp.dot(p_own.astype(BF16), own[:, :LATENT], preferred_element_type=F32)

        def mix(t, carry):
            total, acc = carry
            p = jnp.exp(scores[t] - top)
            total = total + jnp.sum(p, axis=1, keepdims=True)
            acc = acc + jnp.dot(
                p.astype(BF16), values_of(start + t * TILE), preferred_element_type=F32
            )
            return total, acc

        total, acc = lax.fori_loop(0, tiles, mix, (total, acc))
        res = (acc / total).reshape(2, 8, 8, LATENT)
        at = pl.multiple_of(r * 16, 16)
        for g in range(8):
            block = jnp.concatenate([res[0, g], res[1, g]], axis=0)
            out_ref[g, pl.ds(at, 16), :] = block.astype(BF16)
        return start + counts[0, r], jnp.maximum(seen, needed)

    lax.fori_loop(0, 4, request, (jnp.int32(0), jnp.int32(0)))


def attend(table, counts, queries, new_latent, slots):
    smem = pl.BlockSpec(memory_space=pltpu.SMEM)
    vmem = pl.BlockSpec(memory_space=pltpu.VMEM)
    return pl.pallas_call(
        attend_kernel,
        out_shape=jax.ShapeDtypeStruct((8, 64, LATENT), BF16),
        in_specs=[smem, smem] + [pl.BlockSpec(memory_space=pl.ANY)] * 3,
        out_specs=vmem,
        scratch_shapes=[
            pltpu.VMEM(queries.shape, BF16),
            pltpu.VMEM(new_latent.shape, BF16),
            pltpu.VMEM((4, 16, LATENT + ROPE), F32),
            pltpu.VMEM((64 + TILE, 3, 96, 128), BF16),
            pltpu.VMEM((32 // TILE, 128, TILE * PAGE), F32),
            pltpu.SemaphoreType.DMA((64,)),
            pltpu.SemaphoreType.DMA((2,)),
        ],
        compiler_params=pltpu.CompilerParams(vmem_limit_bytes=60 * 2**20),
        name="attend",
    )(table, counts, queries, new_latent, slots)


def layer_kernel(
    attended, residual_in, routes_in, gain_in, router_in, w_uv, w_out, w_gate, w_up, w_down,
    out_ref,
    residual, routes, gain, router, resid, member, heads_in, masked, part_out, part_pair, part_in, res_all, mem_all, stat_out, stat_in, hidden,
    gath, v_uv, v_out, v_gate, v_up, v_down, acc, inner,
    mix, sib_out, sib_in, t1, ul1, ur1, t2, last, fin_out, fin_in,
    wsem, lsem, head_s, head_r, part_s, part_r, pair_s, pair_r,
    ag1_s, ag1_r, ag2_s, ag2_r, ag3_s, ag3_r, sib_s, sib_r, red_s, red_r, sum_s, sum_r,
):
    dp = lax.axis_index("dp")
    ep = lax.axis_index("ep")
    pos = (dp // 4, dp % 4, ep // 2)
    core = ep % 2
    other = 1 - core

    def device(coords, c):
        return (coords[0] * 4 + coords[1], coords[2] * 2 + c)

    def along(axis, delta):
        coords = [pos[0], pos[1], pos[2]]
        coords[axis] = (coords[axis] + delta) % 4
        return device(coords, core)

    sibling = device(pos, other)
    ep_peers = [(dp, (ep + o) % 8) for o in range(1, 8)]
    ring_peers = [along(a, d) for a in (0, 1) for d in (1, 2, 3)]

    def remote(src, dst, ssem, rsem, peer):
        copy = pltpu.make_async_remote_copy(
            src_ref=src, dst_ref=dst, send_sem=ssem, recv_sem=rsem,
            device_id=peer, device_id_type=MESH,
        )
        copy.start()
        sent.append((src, ssem))

    def landed(ref, rsem):
        pltpu.make_async_copy(ref, ref, rsem).wait()

    sent = []

    def settle():
        for src, ssem in sent:
            pltpu.make_async_copy(src, src, ssem).wait()
        sent.clear()

    barrier = pltpu.get_barrier_semaphore()
    for peer in ep_peers + ring_peers:
        pl.semaphore_signal(barrier, inc=1, device_id=peer, device_id_type=MESH)

    loads = [(residual_in, residual), (routes_in, routes), (gain_in, gain), (router_in, router)]
    small = [pltpu.make_async_copy(a, b, lsem.at[1 + i]) for i, (a, b) in enumerate(loads)]
    loads = [(w_uv, v_uv), (w_out, v_out), (w_gate, v_gate), (w_up, v_up), (w_down, v_down)]
    copies = [pltpu.make_async_copy(a, b, wsem.at[i]) for i, (a, b) in enumerate(loads)]
    for copy in small + copies:
        copy.start()
    pl.semaphore_wait(barrier, len(ep_peers) + len(ring_peers))

    for o in range(1, 8):
        to = (ep + o) % 8
        remote(attended.at[to], heads_in.at[ep], head_s.at[o], head_r.at[o], (dp, to))
    own_heads = pltpu.make_async_copy(attended.at[ep], heads_in.at[ep], lsem.at[0])
    own_heads.start()

    for copy in small:
        copy.wait()
    for h in range(2):
        cols = slice(h * HALF, (h + 1) * HALF)
        both = [residual[s, :, cols].astype(F32) for s in range(2)]
        resid[h] = jnp.concatenate(both, axis=0)
    route = jnp.concatenate([routes[0], routes[1]], axis=0)
    lanes = lax.broadcasted_iota(jnp.int32, (8, 128), 1)
    named = jnp.zeros((8, 128), F32)
    for k in range(8):
        named = jnp.where(route[:, k : k + 1] == lanes, 1.0, named)
    member[...] = named
    own_rows = pl.ds(pl.multiple_of(core * 8, 8), 8)
    other_rows = pl.ds(pl.multiple_of(other * 8, 8), 8)
    remote(resid.at[other], res_all.at[own_rows], pair_s.at[0], pair_r.at[0], sibling)
    remote(member, mem_all.at[own_rows], pair_s.at[1], pair_r.at[1], sibling)
    res_all[own_rows, :] = resid[core]
    mem_all[own_rows, :] = member[...]

    def clear(i, _):
        acc[0, i] = jnp.zeros((4, 4, 16, 256), F32)
        acc[1, i] = jnp.zeros((4, 4, 16, 256), F32)
        return 0

    lax.fori_loop(0, 4, clear, 0)
    own_heads.wait()
    for o in range(1, 8):
        landed(heads_in.at[(ep + 8 - o) % 8], head_r.at[o])

    copies[0].wait()
    x = heads_in[...].reshape(512, LATENT)
    row_head = lax.broadcasted_iota(jnp.int32, (512, 128), 0) % 8
    for h in range(8):
        y = jnp.dot(x, v_uv[h], preferred_element_type=F32)
        masked[:, h * 128 : (h + 1) * 128] = jnp.where(row_head == h, y, 0.0).astype(BF16)
    to_row = lax.broadcasted_iota(jnp.int32, (64, 512), 0)
    from_row = lax.broadcasted_iota(jnp.int32, (64, 512), 1) // 8
    wanted = (to_row // 8) * 8 + (to_row % 4) * 2 + (to_row % 8) // 4
    pick = jnp.where(from_row == wanted, 1.0, 0.0).astype(BF16)
    flat = jnp.dot(pick, masked[...], preferred_element_type=F32).astype(BF16)

    copies[1].wait()
    for k, h in ((0, other), (1, core)):
        for t in range(HALF // 256):
            cols = pl.ds(pl.multiple_of(h * HALF + t * 256, 256), 256)
            y = jnp.dot(flat, v_out[:, cols], preferred_element_type=F32)
            part_out[k, :, :, t * 256 : (t + 1) * 256] = y.astype(BF16).reshape(4, 16, 256)
        if k == 0:
            remote(part_out.at[0], part_pair, part_s.at[0], part_r.at[0], sibling)
    landed(part_pair, part_r.at[0])
    for d in (2, 1, 3, 0):
        to = (pos[2] + d) % 4
        both = part_out[1, to].astype(F32) + part_pair[to].astype(F32)
        part_out[1, to] = both.astype(BF16)
        if d:
            remote(
                part_out.at[1, to], part_in.at[d - 1], part_s.at[d], part_r.at[d], along(2, d)
            )
    landed(res_all.at[other_rows], pair_r.at[0])
    landed(mem_all.at[other_rows], pair_r.at[1])
    hid = part_out[1, pos[2]].astype(F32)
    settle()
    for d in (1, 3, 2):
        landed(part_in.at[d - 1], part_r.at[d])
        hid = hid + part_in[d - 1].astype(F32)
    hid = hid + res_all[...]
    hidden[...] = hid

    half_cols = pl.ds(pl.multiple_of(core * HALF, 128), HALF)
    scaled = hid * gain[half_cols].reshape(1, HALF)
    stat_out[0] = jnp.zeros((16, 128), F32)
    stat_out[0, :, 0:16] = lax.dot_general(
        scaled, router[:, half_cols], (((1,), (1,)), ((), ())),
        preferred_element_type=F32, precision=lax.Precision.HIGHEST,
    )
    stat_out[1] = jnp.broadcast_to(jnp.sum(hid * hid, axis=1, keepdims=True), (16, 128))
    remote(stat_out, stat_in, pair_s.at[2], pair_r.at[2], sibling)
    landed(stat_in, pair_r.at[2])
    square = stat_out[1] + stat_in[1]
    inv = lax.rsqrt(square / (2 * HALF) + norm_eps)
    affinity = jax.nn.sigmoid((stat_out[0] + stat_in[0]) * inv) * mem_all[...]
    gates = route_scale * affinity / jnp.sum(affinity, axis=1, keepdims=True)
    coarse = gates.astype(BF16)
    fine = (gates - coarse.astype(F32)).astype(BF16)
    normed = (scaled * inv[:, 0:1]).astype(BF16)
    z, xx, yy = pos
    gath[core, 0, z, xx, yy] = normed[:, 0:640]
    gath[core, 1, z, xx, yy] = normed[:, 640:1280]
    gath[core, 2, z, xx, yy, :, 0:512] = normed[:, 1280:1792]
    gath[core, 2, z, xx, yy, :, 512:640] = jnp.where(core == 0, coarse, fine)

    whole = pl.ds(0, 4)
    halves = (pl.ds(0, 2), pl.ds(2, 2))

    def g_at(cls, spec):
        return gath.at[core, cls, spec[0], spec[1], spec[2]]

    def spec_of(order, values):
        spec = [None, None, None]
        for axis, value in zip(order, values):
            spec[axis] = value
        return spec

    def line(cls, e, f):
        a1, a2, a3 = ORDERS[cls]
        where = spec_of((a1, a2, a3), ((pos[a1] + 4 - e) % 4, (pos[a2] + 4 - f) % 4, pos[a3]))
        return g_at(cls, where)

    def quarter(cls, f, shift, half=whole):
        a1, a2, a3 = ORDERS[cls]
        at = (half, (pos[a2] + 4 - f) % 4, (pos[a3] + shift) % 4)
        return g_at(cls, spec_of((a1, a2, a3), at))

    def plane_at(cls, shift):
        a1, a2, a3 = ORDERS[cls]
        return tuple(spec_of((a1, a2, a3), (whole, whole, (pos[a3] + shift) % 4)))

    def to_pair(cls, k, shift):
        plane = gath.at[(core, cls) + plane_at(cls, shift)]
        remote(plane, plane, sib_s.at[cls, k], sib_r.at[cls, k], sibling)

    def second(cls, e):
        b = line(cls, e, 0)
        for d in (1, 3, 2):
            remote(b, b, ag2_s.at[cls, d, e], ag2_r.at[cls, d], along(ORDERS[cls][1], d))

    def third(cls, f):
        b = quarter(cls, f, 0)
        for k, d in ((0, 1), (1, 3)):
            remote(b, b, ag3_s.at[cls, f, k], ag3_r.at[cls, f, k], along(ORDERS[cls][2], d))

    for cls, order in enumerate(ORDERS):
        own = g_at(cls, pos)
        for d in (1, 3, 2):
            remote(own, own, ag1_s.at[cls, d], ag1_r.at[cls, d], along(order[0], d))
    for cls in range(3):
        second(cls, 0)
    for e in (1, 3, 2):
        for cls in range(3):
            landed(line(cls, e, 0), ag1_r.at[cls, e])
            second(cls, e)
    for cls in range(3):
        third(cls, 0)
    for f in (1, 3, 2):
        for cls in range(3):
            landed(quarter(cls, f, 0), ag2_r.at[cls, f])
            third(cls, f)
    for cls in range(3):
        to_pair(cls, 0, 0)
    for f in (0, 1, 3, 2):
        for cls, order in enumerate(ORDERS):
            landed(quarter(cls, f, 3), ag3_r.at[cls, f, 0])
            b = quarter(cls, f, 3, halves[0])
            remote(b, b, ag3_s.at[cls, f, 2], ag3_r.at[cls, f, 2], along(order[2], 1))
            landed(quarter(cls, f, 1), ag3_r.at[cls, f, 1])
            b = quarter(cls, f, 1, halves[1])
            remote(b, b, ag3_s.at[cls, f, 3], ag3_r.at[cls, f, 3], along(order[2], 3))
    for k, shift in ((1, 3), (2, 1)):
        for cls in range(3):
            to_pair(cls, k, shift)

    for copy in copies[2:]:
        copy.wait()

    def expert_in(h, cls, shift):
        at = plane_at(cls, shift)
        n = WIDTHS[cls]
        x = gath[(h, cls) + at].reshape(256, PART)[:, :n]
        rows = pl.ds(pl.multiple_of(h * HALF + cls * PART, 128), n)
        for k, w in enumerate((v_gate, v_up)):
            y = jnp.dot(x, w[0, rows, :], preferred_element_type=F32).reshape(4, 4, 16, 256)
            acc[(k,) + at] = acc[(k,) + at] + y

    def from_pair(cls, k, shift):
        landed(gath.at[(other, cls) + plane_at(cls, shift)], sib_r.at[cls, k])

    for cls in range(3):
        expert_in(core, cls, 0)
    for cls in range(3):
        from_pair(cls, 0, 0)
        expert_in(other, cls, 0)
    for k, shift in ((1, 3), (2, 1)):
        for cls in range(3):
            expert_in(core, cls, shift)
    for cls in range(3):
        for f in range(4):
            landed(quarter(cls, f, 2, halves[0]), ag3_r.at[cls, f, 2])
            landed(quarter(cls, f, 2, halves[1]), ag3_r.at[cls, f, 3])
        to_pair(cls, 3, 2)
    for k, shift in ((1, 3), (2, 1)):
        for cls in range(3):
            from_pair(cls, k, shift)
            expert_in(other, cls, shift)
    for cls in range(3):
        expert_in(core, cls, 2)
    for cls in range(3):
        from_pair(cls, 3, 2)
        expert_in(other, cls, 2)

    lane = lax.broadcasted_iota(jnp.int32, (256, 128), 1)

    def activate(i, _):
        both = gath[0, 2, i, :, :, :, 512:640].astype(F32) + gath[1, 2, i, :, :, :, 512:640].astype(F32)
        weight = jnp.sum(jnp.where(lane == dp, both.reshape(256, 128), 0.0), axis=1, keepdims=True)
        gate = acc[0, i].reshape(256, 256)
        act = gate / (1.0 + jnp.exp(-gate)) * acc[1, i].reshape(256, 256) * weight
        inner[i] = act.astype(BF16).reshape(4, 4, 16, 256)
        return 0

    lax.fori_loop(0, 4, activate, 0)

    def expert_out(half, cls, at):
        cols = pl.ds(pl.multiple_of(half * HALF + cls * PART, 128), WIDTHS[cls])
        act = inner[at].reshape(256, 256)
        y = jnp.dot(act, v_down[0, :, cols], preferred_element_type=F32)
        return y.reshape(4, 4, 16, WIDTHS[cls])

    def for_pair(shift):
        for cls in range(3):
            at = plane_at(cls, shift)
            b = (cls,) + at + (slice(None), pl.ds(0, WIDTHS[cls]))
            sib_out[b] = expert_out(other, cls, at).astype(BF16)
            remote(sib_out.at[b], sib_in.at[b], red_s.at[cls, shift], red_r.at[cls, shift], sibling)

    def for_self(shift):
        for cls in range(3):
            at = plane_at(cls, shift)
            b = (cls,) + at + (slice(None), pl.ds(0, WIDTHS[cls]))
            y = expert_out(core, cls, at)
            landed(sib_in.at[b], red_r.at[cls, shift])
            mix[b] = (y + sib_in[b].astype(F32)).astype(BF16)

    def block(cls, shift, half):
        a1, a2, a3 = ORDERS[cls]
        spec = spec_of((a1, a2, a3), (half, whole, (pos[a3] + shift) % 4))
        return (cls, spec[0], spec[1], spec[2], slice(None), pl.ds(0, WIDTHS[cls]))

    def temp(cls, half):
        a1, a2, a3 = ORDERS[cls]
        first, then = (half, whole) if a1 < a2 else (whole, half)
        return (cls, first, then, slice(None), pl.ds(0, WIDTHS[cls]))

    def send(cls, shift, half, buf, k, delta):
        remote(
            mix.at[block(cls, shift, halves[half])], buf.at[temp(cls, halves[half])],
            sum_s.at[cls, 0, k], sum_r.at[cls, 0, k], along(ORDERS[cls][2], delta),
        )

    for_pair(2)
    for_pair(1)
    for_self(2)
    for cls in range(3):
        send(cls, 2, 0, t1, 0, 1)
        send(cls, 2, 1, t1, 1, 3)
    for_pair(3)
    for_self(1)
    for cls in range(3):
        send(cls, 1, 1, ul1, 2, 1)
    for_self(3)
    for cls in range(3):
        send(cls, 3, 0, ur1, 3, 3)
    for cls in range(3):
        for half, shift, buf, k, delta in ((0, 1, ul1, 0, 1), (1, 3, ur1, 1, 3)):
            at, tmp = block(cls, shift, halves[half]), temp(cls, halves[half])
            landed(t1.at[tmp], sum_r.at[cls, 0, k])
            mix[at] = (mix[at].astype(F32) + t1[tmp].astype(F32)).astype(BF16)
            send(cls, shift, half, buf, k + 4, delta)
    for_pair(0)
    for_self(0)
    settle()
    for cls, order in enumerate(ORDERS):
        a1, a2, a3 = order
        n = WIDTHS[cls]
        for half, ks in ((0, (4, 3)), (1, (2, 5))):
            tmp = temp(cls, halves[half])
            landed(ul1.at[tmp], sum_r.at[cls, 0, ks[0]])
            landed(ur1.at[tmp], sum_r.at[cls, 0, ks[1]])
        for d in (2, 1, 3, 0):
            where = (pos[a2] + d) % 4
            spec = spec_of(order, (whole, where, pos[a3]))
            at = (cls, spec[0], spec[1], spec[2], slice(None), pl.ds(0, n))
            first, then = (whole, where) if a1 < a2 else (where, whole)
            tmp = (cls, first, then, slice(None), pl.ds(0, n))
            total = mix[at].astype(F32) + ul1[tmp].astype(F32) + ur1[tmp].astype(F32)
            mix[at] = total.astype(BF16)
            if d:
                dst = t2.at[cls, d - 1, :, :, pl.ds(0, n)]
                remote(mix.at[at], dst, sum_s.at[cls, 1, d], sum_r.at[cls, 1, d], along(a2, d))
    for cls, order in enumerate(ORDERS):
        a1, a2, a3 = order
        n = WIDTHS[cls]
        for d in (1, 3, 2):
            landed(t2.at[cls, d - 1, :, :, pl.ds(0, n)], sum_r.at[cls, 1, d])
        for d in (2, 1, 3, 0):
            where = (pos[a1] + d) % 4
            coords = list(pos)
            coords[a1] = where
            at = (cls, coords[0], coords[1], coords[2], slice(None), pl.ds(0, n))
            total = mix[at].astype(F32)
            for k in range(3):
                total = total + t2[cls, k, where, :, 0:n].astype(F32)
            mix[at] = total.astype(BF16)
            if d:
                dst = last.at[cls, d - 1, :, pl.ds(0, n)]
                remote(mix.at[at], dst, sum_s.at[cls, 2, d], sum_r.at[cls, 2, d], along(a1, d))
    for cls in range(3):
        n = WIDTHS[cls]
        total = mix[cls, pos[0], pos[1], pos[2], :, 0:n].astype(F32)
        for d in (1, 2, 3):
            landed(last.at[cls, d - 1, :, pl.ds(0, n)], sum_r.at[cls, 2, d])
            total = total + last[cls, d - 1, :, 0:n].astype(F32)
        total = total + hidden[:, cls * PART : cls * PART + n]
        fin_out[0, :, cls * PART : cls * PART + n] = total[0:8]
        fin_out[1, :, cls * PART : cls * PART + n] = total[8:16]
    remote(fin_out.at[other], fin_in, pair_s.at[3], pair_r.at[3], sibling)
    for s in range(2):
        out_ref[s, :, half_cols] = fin_out[core, s * 4 : s * 4 + 4]
    settle()
    landed(fin_in, pair_r.at[3])
    for s in range(2):
        cols = pl.ds(pl.multiple_of(other * HALF, 128), HALF)
        out_ref[s, :, cols] = fin_in[s * 4 : s * 4 + 4]


def layer(attended, residual, routes, gain, router, w_uv, w_out, w_gate, w_up, w_down):
    vmem = pl.BlockSpec(memory_space=pltpu.VMEM)
    hbm = pl.BlockSpec(memory_space=pl.ANY)
    dma = pltpu.SemaphoreType.DMA
    grid = (3, 4, 4, 4, 16, PART)
    return pl.pallas_call(
        layer_kernel,
        out_shape=jax.ShapeDtypeStruct((2, 4, 2 * HALF), F32),
        in_specs=[hbm] * 10,
        out_specs=vmem,
        scratch_shapes=[
            pltpu.VMEM(residual.shape, BF16),
            pltpu.VMEM(routes.shape, jnp.int32),
            pltpu.VMEM(gain.shape, F32),
            pltpu.VMEM(router.shape, F32),
            pltpu.VMEM((2, 8, HALF), F32),
            pltpu.VMEM((8, 128), F32),
            pltpu.VMEM((8, 64, LATENT), BF16),
            pltpu.VMEM((512, 1024), BF16),
            pltpu.VMEM((2, 4, 16, HALF), BF16),
            pltpu.VMEM((4, 16, HALF), BF16),
            pltpu.VMEM((3, 16, HALF), BF16),
            pltpu.VMEM((16, HALF), F32),
            pltpu.VMEM((16, 128), F32),
            pltpu.VMEM((2, 16, 128), F32),
            pltpu.VMEM((2, 16, 128), F32),
            pltpu.VMEM((16, HALF), F32),
            pltpu.VMEM((2,) + grid, BF16),
            pltpu.VMEM(w_uv.shape, BF16),
            pltpu.VMEM(w_out.shape, BF16),
            pltpu.VMEM(w_gate.shape, BF16),
            pltpu.VMEM(w_up.shape, BF16),
            pltpu.VMEM(w_down.shape, BF16),
            pltpu.VMEM((2, 4, 4, 4, 16, 256), F32),
            pltpu.VMEM((4, 4, 4, 16, 256), BF16),
            pltpu.VMEM(grid, BF16),
            pltpu.VMEM(grid, BF16),
            pltpu.VMEM(grid, BF16),
            pltpu.VMEM((3, 4, 4, 16, PART), BF16),
            pltpu.VMEM((3, 4, 4, 16, PART), BF16),
            pltpu.VMEM((3, 4, 4, 16, PART), BF16),
            pltpu.VMEM((3, 3, 4, 16, PART), BF16),
            pltpu.VMEM((3, 3, 16, PART), BF16),
            pltpu.VMEM((2, 8, HALF), F32),
            pltpu.VMEM((8, HALF), F32),
            dma((5,)), dma((5,)), dma((8,)), dma((8,)), dma((4,)), dma((4,)), dma((4,)), dma((4,)),
            dma((3, 4)), dma((3, 4)), dma((3, 4, 4)), dma((3, 4)), dma((3, 4, 4)), dma((3, 4, 4)),
            dma((3, 4)), dma((3, 4)), dma((3, 4)), dma((3, 4)),
            dma((3, 3, 6)), dma((3, 3, 6)),
        ],
        compiler_params=pltpu.CompilerParams(
            collective_id=1, has_side_effects=True, vmem_limit_bytes=56 * 2**20
        ),
        name="layer",
    )(attended, residual, routes, gain, router, w_uv, w_out, w_gate, w_up, w_down)


def shards(
    cache_pool,
    page_table,
    page_counts,
    queries,
    new_latent,
    residual,
    w_uv,
    w_out,
    norm_gain,
    w_router,
    w_gate,
    w_up,
    w_down,
    routes,
):
    table = page_table.T
    incoming = exchange(table, jnp.transpose(cache_pool, (1, 2, 0))).reshape(-1, 3, 96, 128)
    attended = attend(table, page_counts, queries, new_latent, incoming)
    out = layer(
        attended, residual, routes, norm_gain, w_router.T, w_uv, w_out, w_gate, w_up, w_down
    )
    return out.astype(BF16)


def solution(mesh):
    return jax.shard_map(
        shards,
        mesh=mesh,
        in_specs=(
            P(("dp", "ep"), None, None),
            P(),
            P(("dp", "ep"), None),
            P(None, ("dp", "ep"), None, None),
            P(None, ("dp", "ep"), None),
            P(None, ("dp", "ep"), None),
            P("ep", None, None),
            P("ep", None),
            P(),
            P(),
            P("dp", None, "ep"),
            P("dp", None, "ep"),
            P("dp", "ep", None),
            P(None, ("dp", "ep"), None),
        ),
        out_specs=P(None, ("dp", "ep"), None),
        check_vma=False,
    )
```

```python
import functools

import jax
import jax.numpy as jnp
from jax import lax
from jax.experimental import pallas as pl
from jax.experimental.pallas import tpu as pltpu
from jax.sharding import PartitionSpec as P

MESH = pl.DeviceIdType.MESH
F32 = jnp.float32
BF16 = jnp.bfloat16

LATENT = 512
ROPE = 64
PAGE = 64
TILE = 16
score_scale = 192.0 ** (-0.5)
route_scale = 2.5
norm_eps = 1e-06

HALF = 1792
PART = 640
ORDERS = ((0, 1, 2), (1, 2, 0), (2, 0, 1))
WIDTHS = (640, 640, 512)


def exchange_kernel(
    table, pool, out,
    table_v, pool_v, slots, held1, held2, stage,
    psem, lsem, send1, recv1, send2, recv2, send3, recv3,
):
    dp = lax.axis_index("dp")
    ep = lax.axis_index("ep")
    pos = (dp // 4, dp % 4, ep // 2)
    core = ep % 2
    other = 1 - core
    whole = pl.ds(0, 4)

    loads = [
        pltpu.make_async_copy(
            pool.at[pl.ds(i * 16, 16)], pool_v.at[pl.ds(i * 16, 16)], psem.at[i]
        )
        for i in range(4)
    ]
    table_load = pltpu.make_async_copy(table, table_v, psem.at[4])
    table_load.start()
    for load in loads:
        load.start()

    def along(axis, delta, c):
        coords = list(pos)
        coords[axis] = (coords[axis] + delta) % 4
        return (coords[0] * 4 + coords[1], coords[2] * 2 + c)

    def spec_of(order, values):
        spec = [None, None, None]
        for axis, value in zip(order, values):
            spec[axis] = value
        return tuple(spec)

    barrier = pltpu.get_barrier_semaphore()
    peers = [along(a, d, c) for a in range(3) for d in (1, 2, 3) for c in (core, other)]
    peers.append(along(0, 0, other))
    for peer in peers:
        pl.semaphore_signal(barrier, inc=1, device_id=peer, device_id_type=MESH)

    table_load.wait()
    pages = table_v[...]
    wanted = jnp.where(pages // 128 == dp * 8 + ep, pages % 128, 0)
    wanted = jnp.sum(wanted, axis=0, keepdims=True)
    page = lax.broadcasted_iota(jnp.int32, (128, 128), 0)
    onehot = jnp.transpose(jnp.where(wanted == page, 1.0, 0.0)).astype(BF16)

    def put(cls, row, pieces):
        for j in range(0, 16, 4):
            x = jnp.concatenate(pieces(j), axis=0)
            y = lax.dot_general(onehot, x, (((1,), (1,)), ((), ())), preferred_element_type=F32)
            for i in range(4):
                stage[:, j + i, :] = y[:, i * 128 : (i + 1) * 128]
        block = stage[...].astype(BF16).reshape(4, 4, 4, 2, 16, 128)
        slots[cls, :, :, :, :, row : row + 16, :] = block

    def latent_rows(cls, chunk, unit, row):
        def pieces(j):
            t = unit * 16 + j
            return [pool_v[pl.ds(t, 4), chunk * 128 : (chunk + 1) * 128, :].reshape(512, 128)]

        put(cls, row, pieces)

    def rope_rows(cls, unit, row):
        def pieces(j):
            found = []
            for i in range(4):
                found.append(pool_v[unit * 16 + j + i, 512:576, :])
                found.append(pool_v[32 + unit * 16 + j + i, 512:576, :])
            return found

        put(cls, row, pieces)

    def remote(src, dst, ssem, rsem, peer):
        pltpu.make_async_remote_copy(
            src_ref=src, dst_ref=dst, send_sem=ssem, recv_sem=rsem,
            device_id=peer, device_id_type=MESH,
        ).start()

    def landed(ref, sem):
        pltpu.make_async_copy(ref, ref, sem).wait()

    for part in range(6):
        rows = pl.ds(part * 16, 16)
        if part < 4:
            loads[part].wait()
        for cls, order in enumerate(ORDERS):
            a1, a2, a3 = order
            if part < 4:
                latent_rows(cls, cls, part, 16 * part)
            elif cls < 2:
                latent_rows(cls, 3, 2 * cls + part - 4, 16 * part)
            else:
                rope_rows(cls, part - 4, 16 * part)
            if part == 0 and cls == 0:
                pl.semaphore_wait(barrier, len(peers))
            for d in (1, 2, 3):
                src = spec_of(order, ((pos[a1] + d) % 4, whole, whole))
                dst = spec_of(order, (pos[a1], whole, whole))
                remote(
                    slots.at[(cls,) + src + (pl.ds(0, 2), rows)],
                    held1.at[(cls,) + dst + (pl.ds(0, 2), rows)],
                    send1.at[cls], recv1.at[cls, d], along(a1, d, core),
                )
            if part == 5:
                own = (cls,) + spec_of(order, (pos[a1], whole, whole))
                pltpu.make_async_copy(slots.at[own], held1.at[own], lsem.at[cls]).start()

    def second(cls, buf, e):
        a1, a2, a3 = order = ORDERS[cls]
        src1 = (pos[a1] + 4 - e) % 4
        for d in (1, 2, 3):
            src = spec_of(order, (src1, (pos[a2] + d) % 4, whole))
            dst = spec_of(order, (src1, pos[a2], whole))
            remote(
                buf.at[(cls,) + src], held2.at[(cls,) + dst],
                send2.at[cls], recv2.at[cls, d], along(a2, d, core),
            )

    def third(cls, buf, f):
        a1, a2, a3 = order = ORDERS[cls]
        src2 = (pos[a2] + 4 - f) % 4
        for d in (1, 2, 3, 0):
            for k, c in ((0, core), (1, other)):
                src = spec_of(order, (whole, src2, (pos[a3] + d) % 4))
                dst = spec_of(order, (whole, src2, pos[a3]))
                a = buf.at[(cls,) + src + (c,)]
                b = out.at[dst + (core, cls)]
                if d == 0 and k == 0:
                    pltpu.make_async_copy(a, b, recv3.at[cls]).start()
                else:
                    remote(a, b, send3.at[cls, d], recv3.at[cls], along(a3, d, c))

    for cls in range(3):
        second(cls, slots, 0)
    for e in (1, 3, 2):
        for cls, order in enumerate(ORDERS):
            src1 = (pos[order[0]] + 4 - e) % 4
            landed(held1.at[(cls,) + spec_of(order, (src1, whole, whole))], recv1.at[cls, e])
            second(cls, held1, e)
    for cls, order in enumerate(ORDERS):
        own = spec_of(order, (pos[order[0]], whole, whole))
        landed(held1.at[(cls,) + own], lsem.at[cls])
        third(cls, held1, 0)
    for f in (1, 3, 2):
        for cls, order in enumerate(ORDERS):
            a1, a2, a3 = order
            at = spec_of(order, (whole, (pos[a2] + 4 - f) % 4, whole))
            landed(held2.at[(cls,) + at], recv2.at[cls, f])
            third(cls, held2, f)
    for cls in range(3):
        most = held1.at[cls, pl.ds(0, 3)]
        landed(most, send1.at[cls])
        landed(most, send2.at[cls])
    for cls in range(3):
        landed(held1.at[cls, 0, pl.ds(0, 2)], send3.at[cls, 0])
        for d in (1, 2, 3):
            landed(held1.at[cls, 0], send3.at[cls, d])
    for cls in range(3):
        landed(out.at[:, :, :, :, cls], recv3.at[cls])


def exchange(table, pool):
    hbm = pl.BlockSpec(memory_space=pl.ANY)
    dma = pltpu.SemaphoreType.DMA
    held = (3, 4, 4, 4, 2, 96, 128)
    return pl.pallas_call(
        exchange_kernel,
        out_shape=jax.ShapeDtypeStruct((4, 4, 4, 2, 3, 96, 128), BF16),
        in_specs=[hbm, hbm],
        out_specs=hbm,
        scratch_shapes=[
            pltpu.VMEM(table.shape, jnp.int32),
            pltpu.VMEM(pool.shape, BF16),
            pltpu.VMEM(held, BF16),
            pltpu.VMEM(held, BF16),
            pltpu.VMEM(held, BF16),
            pltpu.VMEM((128, 16, 128), F32),
            dma((5,)), dma((3,)), dma((3,)), dma((3, 4)), dma((3,)), dma((3, 4)), dma((3, 4)), dma((3,)),
        ],
        compiler_params=pltpu.CompilerParams(
            collective_id=2, has_side_effects=True, vmem_limit_bytes=56 * 2**20
        ),
        name="exchange",
    )(table, pool)


def attend_kernel(
    table, counts, queries, new, slots, out_ref, q_ref, new_ref, own_ref, keys, scores, sem, in_sem
):
    pages = 64
    me = lax.axis_index("dp") * 8 + lax.axis_index("ep")

    loads = [
        pltpu.make_async_copy(queries, q_ref, in_sem.at[0]),
        pltpu.make_async_copy(new, new_ref, in_sem.at[1]),
    ]
    for load in loads:
        load.start()

    def page_copy(j):
        return pltpu.make_async_copy(slots.at[table[j, me] // 128], keys.at[j], sem.at[j])

    def fetch(j, _):
        page_copy(j).start()
        return 0

    lax.fori_loop(0, pages, fetch, 0)

    def clear(j, _):
        keys[pages + j] = jnp.zeros((3, 96, 128), BF16)
        return 0

    lax.fori_loop(0, TILE, clear, 0)
    own_ref[...] = jnp.zeros_like(own_ref)
    loads[1].wait()
    for step in range(2):
        fresh = new_ref[step].astype(F32)
        for r in range(4):
            own_ref[r, step : step + 1, :] = fresh[r : r + 1]
    loads[0].wait()
    width = TILE * PAGE
    step_of = lax.broadcasted_iota(jnp.int32, (16, 128), 1) // 64
    token = lax.broadcasted_iota(jnp.int32, (16, 128), 0)
    low = lax.broadcasted_iota(jnp.int32, (TILE, 32, 128), 2) < ROPE

    def values_of(page):
        parts = [keys[pl.ds(page, TILE), k, 0:64, :].reshape(width, 128) for k in range(3)]
        parts.append(keys[pl.ds(page, TILE), 0:2, 64:96, :].reshape(width, 128))
        return jnp.concatenate(parts, axis=1)

    def arrive(j, _):
        pltpu.make_async_copy(keys.at[j], keys.at[j], sem.at[j]).wait()
        return 0

    def request(r, carry):
        start, seen = carry
        q = jnp.concatenate([q_ref[0, r], q_ref[1, r]], axis=0)
        own = own_ref[r].astype(BF16)
        s_own = lax.dot_general(own, q, (((1,), (1,)), ((), ())), preferred_element_type=F32)
        s_own = jnp.where(token <= step_of, s_own * score_scale, -jnp.inf)
        q_rope = q[:, LATENT:]
        q_wide = jnp.concatenate([q[:, :LATENT], q_rope, q_rope], axis=1)
        q_turned = jnp.transpose(q_wide)
        length = counts[0, r] * PAGE
        tiles = (length + width - 1) // width
        needed = jnp.minimum(start + tiles * TILE, pages)
        lax.fori_loop(seen, needed, arrive, 0)

        def score(t, top):
            page = start + t * TILE
            rope = keys[pl.ds(page, TILE), 2, 64:96, :]
            zero = jnp.zeros_like(rope)
            pair = jnp.concatenate([jnp.where(low, rope, zero), jnp.where(low, zero, rope)], axis=1)
            key = jnp.concatenate([values_of(page), pair.reshape(width, 128)], axis=1)
            s = jnp.dot(key, q_turned, preferred_element_type=F32)
            place = t * width + lax.broadcasted_iota(jnp.int32, (width, 128), 0)
            s = jnp.where(place < length, s * score_scale, -jnp.inf)
            scores[t] = s
            return jnp.maximum(top, jnp.max(s, axis=0, keepdims=True))

        top = lax.fori_loop(0, tiles, score, jnp.max(s_own, axis=0, keepdims=True))
        p_own = jnp.exp(s_own - top)
        total = jnp.sum(p_own, axis=0, keepdims=True)

        def weigh(p, values):
            turned = jnp.transpose(p).astype(BF16)
            return jnp.dot(turned, values, preferred_element_type=F32)

        acc = weigh(p_own, own[:, :LATENT])

        def mix(t, carry):
            total, acc = carry
            p = jnp.exp(scores[t] - top)
            total = total + jnp.sum(p, axis=0, keepdims=True)
            acc = acc + weigh(p, values_of(start + t * TILE))
            return total, acc

        total, acc = lax.fori_loop(0, tiles, mix, (total, acc))
        scale = jnp.transpose(jnp.broadcast_to(1.0 / total, (128, 128)))[:, 0:1]
        res = (acc * scale).reshape(2, 8, 8, LATENT)
        at = pl.multiple_of(r * 16, 16)
        for g in range(8):
            block = jnp.concatenate([res[0, g], res[1, g]], axis=0)
            out_ref[g, pl.ds(at, 16), :] = block.astype(BF16)
        return start + counts[0, r], jnp.maximum(seen, needed)

    lax.fori_loop(0, 4, request, (jnp.int32(0), jnp.int32(0)), unroll=True)


def attend(table, counts, queries, new_latent, slots):
    smem = pl.BlockSpec(memory_space=pltpu.SMEM)
    vmem = pl.BlockSpec(memory_space=pltpu.VMEM)
    return pl.pallas_call(
        attend_kernel,
        out_shape=jax.ShapeDtypeStruct((8, 64, LATENT), BF16),
        in_specs=[smem, smem] + [pl.BlockSpec(memory_space=pl.ANY)] * 3,
        out_specs=vmem,
        scratch_shapes=[
            pltpu.VMEM(queries.shape, BF16),
            pltpu.VMEM(new_latent.shape, BF16),
            pltpu.VMEM((4, 16, LATENT + ROPE), F32),
            pltpu.VMEM((64 + TILE, 3, 96, 128), BF16),
            pltpu.VMEM((32 // TILE, TILE * PAGE, 128), F32),
            pltpu.SemaphoreType.DMA((64,)),
            pltpu.SemaphoreType.DMA((2,)),
        ],
        compiler_params=pltpu.CompilerParams(vmem_limit_bytes=60 * 2**20),
        name="attend",
    )(table, counts, queries, new_latent, slots)


def layer_kernel(
    attended, residual_in, routes_in, gain_in, router_in, w_uv, w_out, w_gate, w_up, w_down,
    out_ref,
    residual, routes, gain, router, resid, member, heads_in, masked, part_out, part_pair, part_in, res_all, mem_all, stat_out, stat_in, hidden,
    gath, v_uv, v_out, v_gate, v_up, v_down, acc, inner,
    mix, sib_out, sib_in, t1, ul1, ur1, t2, last, fin_out, fin_in,
    wsem, lsem, head_s, head_r, part_s, part_r, pair_s, pair_r,
    ag1_s, ag1_r, ag2_s, ag2_r, ag3_s, ag3_r, sib_s, sib_r, red_s, red_r, sum_s, sum_r,
):
    dp = lax.axis_index("dp")
    ep = lax.axis_index("ep")
    pos = (dp // 4, dp % 4, ep // 2)
    core = ep % 2
    other = 1 - core

    def device(coords, c):
        return (coords[0] * 4 + coords[1], coords[2] * 2 + c)

    def along(axis, delta):
        coords = [pos[0], pos[1], pos[2]]
        coords[axis] = (coords[axis] + delta) % 4
        return device(coords, core)

    sibling = device(pos, other)
    ep_peers = [(dp, (ep + o) % 8) for o in range(1, 8)]
    ring_peers = [along(a, d) for a in (0, 1) for d in (1, 2, 3)]

    def remote(src, dst, ssem, rsem, peer):
        copy = pltpu.make_async_remote_copy(
            src_ref=src, dst_ref=dst, send_sem=ssem, recv_sem=rsem,
            device_id=peer, device_id_type=MESH,
        )
        copy.start()
        sent.append((src, ssem))

    def landed(ref, rsem):
        pltpu.make_async_copy(ref, ref, rsem).wait()

    sent = []

    def settle(count=None):
        for src, ssem in sent[:count]:
            pltpu.make_async_copy(src, src, ssem).wait()
        del sent[:count]

    barrier = pltpu.get_barrier_semaphore()
    for peer in ep_peers + ring_peers:
        pl.semaphore_signal(barrier, inc=1, device_id=peer, device_id_type=MESH)

    loads = [(residual_in, residual), (routes_in, routes), (gain_in, gain), (router_in, router)]
    small = [pltpu.make_async_copy(a, b, lsem.at[1 + i]) for i, (a, b) in enumerate(loads)]
    loads = [(w_uv, v_uv), (w_out, v_out), (w_gate, v_gate), (w_up, v_up), (w_down, v_down)]
    copies = [pltpu.make_async_copy(a, b, wsem.at[i]) for i, (a, b) in enumerate(loads)]
    for copy in small + copies:
        copy.start()
    pl.semaphore_wait(barrier, len(ep_peers) + len(ring_peers))

    for o in range(1, 8):
        to = (ep + o) % 8
        remote(attended.at[to], heads_in.at[ep], head_s.at[o], head_r.at[o], (dp, to))
    own_heads = pltpu.make_async_copy(attended.at[ep], heads_in.at[ep], lsem.at[0])
    own_heads.start()

    for copy in small:
        copy.wait()
    for h in range(2):
        cols = slice(h * HALF, (h + 1) * HALF)
        both = [residual[s, :, cols].astype(F32) for s in range(2)]
        resid[h] = jnp.concatenate(both, axis=0)
    route = jnp.concatenate([routes[0], routes[1]], axis=0)
    lanes = lax.broadcasted_iota(jnp.int32, (8, 128), 1)
    named = jnp.zeros((8, 128), F32)
    for k in range(8):
        named = jnp.where(route[:, k : k + 1] == lanes, 1.0, named)
    member[...] = named
    own_rows = pl.ds(pl.multiple_of(core * 8, 8), 8)
    other_rows = pl.ds(pl.multiple_of(other * 8, 8), 8)
    remote(resid.at[other], res_all.at[own_rows], pair_s.at[0], pair_r.at[0], sibling)
    remote(member, mem_all.at[own_rows], pair_s.at[1], pair_r.at[1], sibling)
    res_all[own_rows, :] = resid[core]
    mem_all[own_rows, :] = member[...]

    def clear(i, _):
        acc[0, i] = jnp.zeros((4, 4, 16, 256), F32)
        acc[1, i] = jnp.zeros((4, 4, 16, 256), F32)
        return 0

    lax.fori_loop(0, 4, clear, 0)
    own_heads.wait()
    for o in range(1, 8):
        landed(heads_in.at[(ep + 8 - o) % 8], head_r.at[o])

    copies[0].wait()
    x = heads_in[...].reshape(512, LATENT)
    row_head = lax.broadcasted_iota(jnp.int32, (512, 128), 0) % 8
    for h in range(8):
        y = jnp.dot(x, v_uv[h], preferred_element_type=F32)
        masked[:, h * 128 : (h + 1) * 128] = jnp.where(row_head == h, y, 0.0).astype(BF16)
    to_row = lax.broadcasted_iota(jnp.int32, (64, 512), 0)
    from_row = lax.broadcasted_iota(jnp.int32, (64, 512), 1) // 8
    wanted = (to_row // 8) * 8 + (to_row % 4) * 2 + (to_row % 8) // 4
    pick = jnp.where(from_row == wanted, 1.0, 0.0).astype(BF16)
    flat = jnp.dot(pick, masked[...], preferred_element_type=F32).astype(BF16)

    copies[1].wait()
    for k, h in ((0, other), (1, core)):
        for t in range(HALF // 256):
            cols = pl.ds(pl.multiple_of(h * HALF + t * 256, 256), 256)
            y = jnp.dot(flat, v_out[:, cols], preferred_element_type=F32)
            part_out[k, :, :, t * 256 : (t + 1) * 256] = y.astype(BF16).reshape(4, 16, 256)
        if k == 0:
            remote(part_out.at[0], part_pair, part_s.at[0], part_r.at[0], sibling)
    landed(part_pair, part_r.at[0])
    for d in (2, 1, 3, 0):
        to = (pos[2] + d) % 4
        both = part_out[1, to].astype(F32) + part_pair[to].astype(F32)
        part_out[1, to] = both.astype(BF16)
        if d:
            remote(
                part_out.at[1, to], part_in.at[d - 1], part_s.at[d], part_r.at[d], along(2, d)
            )
    landed(res_all.at[other_rows], pair_r.at[0])
    landed(mem_all.at[other_rows], pair_r.at[1])
    hid = part_out[1, pos[2]].astype(F32)
    settle()
    for d in (1, 3, 2):
        landed(part_in.at[d - 1], part_r.at[d])
        hid = hid + part_in[d - 1].astype(F32)
    hid = hid + res_all[...]
    hidden[...] = hid

    half_cols = pl.ds(pl.multiple_of(core * HALF, 128), HALF)
    scaled = hid * gain[half_cols].reshape(1, HALF)
    stat_out[0] = jnp.zeros((16, 128), F32)
    stat_out[0, :, 0:16] = lax.dot_general(
        scaled, router[:, half_cols], (((1,), (1,)), ((), ())),
        preferred_element_type=F32, precision=lax.Precision.HIGHEST,
    )
    stat_out[1] = jnp.broadcast_to(jnp.sum(hid * hid, axis=1, keepdims=True), (16, 128))
    remote(stat_out, stat_in, pair_s.at[2], pair_r.at[2], sibling)
    landed(stat_in, pair_r.at[2])
    square = stat_out[1] + stat_in[1]
    inv = lax.rsqrt(square / (2 * HALF) + norm_eps)
    affinity = jax.nn.sigmoid((stat_out[0] + stat_in[0]) * inv) * mem_all[...]
    gates = route_scale * affinity / jnp.sum(affinity, axis=1, keepdims=True)
    coarse = gates.astype(BF16)
    fine = (gates - coarse.astype(F32)).astype(BF16)
    normed = (scaled * inv[:, 0:1]).astype(BF16)
    z, xx, yy = pos
    gath[core, 0, z, xx, yy] = normed[:, 0:640]
    gath[core, 1, z, xx, yy] = normed[:, 640:1280]
    gath[core, 2, z, xx, yy, :, 0:512] = normed[:, 1280:1792]
    gath[core, 2, z, xx, yy, :, 512:640] = jnp.where(core == 0, coarse, fine)

    whole = pl.ds(0, 4)
    halves = (pl.ds(0, 2), pl.ds(2, 2))

    def g_at(cls, spec):
        return gath.at[core, cls, spec[0], spec[1], spec[2]]

    def spec_of(order, values):
        spec = [None, None, None]
        for axis, value in zip(order, values):
            spec[axis] = value
        return spec

    def line(cls, e, f):
        a1, a2, a3 = ORDERS[cls]
        where = spec_of((a1, a2, a3), ((pos[a1] + 4 - e) % 4, (pos[a2] + 4 - f) % 4, pos[a3]))
        return g_at(cls, where)

    def quarter(cls, f, shift, half=whole):
        a1, a2, a3 = ORDERS[cls]
        at = (half, (pos[a2] + 4 - f) % 4, (pos[a3] + shift) % 4)
        return g_at(cls, spec_of((a1, a2, a3), at))

    def plane_at(cls, shift):
        a1, a2, a3 = ORDERS[cls]
        return tuple(spec_of((a1, a2, a3), (whole, whole, (pos[a3] + shift) % 4)))

    def to_pair(cls, k, shift):
        plane = gath.at[(core, cls) + plane_at(cls, shift)]
        remote(plane, plane, sib_s.at[cls, k], sib_r.at[cls, k], sibling)

    def second(cls, e):
        b = line(cls, e, 0)
        for d in (1, 3, 2):
            remote(b, b, ag2_s.at[cls, d, e], ag2_r.at[cls, d], along(ORDERS[cls][1], d))

    def third(cls, f):
        b = quarter(cls, f, 0)
        for k, d in ((0, 1), (1, 3)):
            remote(b, b, ag3_s.at[cls, f, k], ag3_r.at[cls, f, k], along(ORDERS[cls][2], d))

    for cls, order in enumerate(ORDERS):
        own = g_at(cls, pos)
        for d in (1, 3, 2):
            remote(own, own, ag1_s.at[cls, d], ag1_r.at[cls, d], along(order[0], d))
    for cls in range(3):
        second(cls, 0)
    for e in (1, 3, 2):
        for cls in range(3):
            landed(line(cls, e, 0), ag1_r.at[cls, e])
            second(cls, e)
    for cls in range(3):
        third(cls, 0)
    for f in (1, 3, 2):
        for cls in range(3):
            landed(quarter(cls, f, 0), ag2_r.at[cls, f])
            third(cls, f)
    for cls in range(3):
        to_pair(cls, 0, 0)
    for copy in copies[2:]:
        copy.wait()

    def expert_in(h, cls, shift):
        at = plane_at(cls, shift)
        n = WIDTHS[cls]
        x = gath[(h, cls) + at].reshape(256, PART)[:, :n]
        rows = pl.ds(pl.multiple_of(h * HALF + cls * PART, 128), n)
        for k, w in enumerate((v_gate, v_up)):
            y = jnp.dot(x, w[0, rows, :], preferred_element_type=F32).reshape(4, 4, 16, 256)
            acc[(k,) + at] = acc[(k,) + at] + y

    def from_pair(cls, k, shift):
        landed(gath.at[(other, cls) + plane_at(cls, shift)], sib_r.at[cls, k])

    for f in (0, 1, 3, 2):
        for cls, order in enumerate(ORDERS):
            landed(quarter(cls, f, 3), ag3_r.at[cls, f, 0])
            b = quarter(cls, f, 3, halves[0])
            remote(b, b, ag3_s.at[cls, f, 2], ag3_r.at[cls, f, 2], along(order[2], 1))
            landed(quarter(cls, f, 1), ag3_r.at[cls, f, 1])
            b = quarter(cls, f, 1, halves[1])
            remote(b, b, ag3_s.at[cls, f, 3], ag3_r.at[cls, f, 3], along(order[2], 3))
        if f == 1:
            for cls in range(3):
                expert_in(core, cls, 0)
        if f == 3:
            for cls in range(3):
                from_pair(cls, 0, 0)
                expert_in(other, cls, 0)
    for k, shift in ((1, 3), (2, 1)):
        for cls in range(3):
            to_pair(cls, k, shift)

    for k, shift in ((1, 3), (2, 1)):
        for cls in range(3):
            expert_in(core, cls, shift)
    for k, shift in ((1, 3), (2, 1)):
        for cls in range(3):
            from_pair(cls, k, shift)
            expert_in(other, cls, shift)
    for cls in range(3):
        for f in range(4):
            landed(quarter(cls, f, 2, halves[0]), ag3_r.at[cls, f, 2])
            landed(quarter(cls, f, 2, halves[1]), ag3_r.at[cls, f, 3])
        to_pair(cls, 3, 2)
    for cls in range(3):
        expert_in(core, cls, 2)
    for cls in range(3):
        from_pair(cls, 3, 2)
        expert_in(other, cls, 2)

    lane = lax.broadcasted_iota(jnp.int32, (256, 128), 1)

    def activate(i, _):
        both = gath[0, 2, i, :, :, :, 512:640].astype(F32) + gath[1, 2, i, :, :, :, 512:640].astype(F32)
        weight = jnp.sum(jnp.where(lane == dp, both.reshape(256, 128), 0.0), axis=1, keepdims=True)
        gate = acc[0, i].reshape(256, 256)
        act = gate / (1.0 + jnp.exp(-gate)) * acc[1, i].reshape(256, 256) * weight
        inner[i] = act.astype(BF16).reshape(4, 4, 16, 256)
        return 0

    lax.fori_loop(0, 4, activate, 0)

    def expert_out(half, cls, at):
        cols = pl.ds(pl.multiple_of(half * HALF + cls * PART, 128), WIDTHS[cls])
        act = inner[at].reshape(256, 256)
        y = jnp.dot(act, v_down[0, :, cols], preferred_element_type=F32)
        return y.reshape(4, 4, 16, WIDTHS[cls])

    def for_pair(shift):
        for cls in range(3):
            at = plane_at(cls, shift)
            b = (cls,) + at + (slice(None), pl.ds(0, WIDTHS[cls]))
            sib_out[b] = expert_out(other, cls, at).astype(BF16)
            remote(sib_out.at[b], sib_in.at[b], red_s.at[cls, shift], red_r.at[cls, shift], sibling)

    def for_self(shift):
        for cls in range(3):
            at = plane_at(cls, shift)
            b = (cls,) + at + (slice(None), pl.ds(0, WIDTHS[cls]))
            y = expert_out(core, cls, at)
            landed(sib_in.at[b], red_r.at[cls, shift])
            mix[b] = (y + sib_in[b].astype(F32)).astype(BF16)

    def block(cls, shift, half):
        a1, a2, a3 = ORDERS[cls]
        spec = spec_of((a1, a2, a3), (half, whole, (pos[a3] + shift) % 4))
        return (cls, spec[0], spec[1], spec[2], slice(None), pl.ds(0, WIDTHS[cls]))

    def temp(cls, half):
        a1, a2, a3 = ORDERS[cls]
        first, then = (half, whole) if a1 < a2 else (whole, half)
        return (cls, first, then, slice(None), pl.ds(0, WIDTHS[cls]))

    def send(cls, shift, half, buf, k, delta):
        remote(
            mix.at[block(cls, shift, halves[half])], buf.at[temp(cls, halves[half])],
            sum_s.at[cls, 0, k], sum_r.at[cls, 0, k], along(ORDERS[cls][2], delta),
        )

    gathered = len(sent)
    for_pair(2)
    for_pair(1)
    for_self(2)
    for cls in range(3):
        send(cls, 2, 0, t1, 0, 1)
        send(cls, 2, 1, t1, 1, 3)
    for_pair(3)
    for_self(1)
    for cls in range(3):
        send(cls, 1, 1, ul1, 2, 1)
    for_self(3)
    for cls in range(3):
        send(cls, 3, 0, ur1, 3, 3)
    settle(gathered)
    for cls in range(3):
        for half, shift, buf, k, delta in ((0, 1, ul1, 0, 1), (1, 3, ur1, 1, 3)):
            at, tmp = block(cls, shift, halves[half]), temp(cls, halves[half])
            landed(t1.at[tmp], sum_r.at[cls, 0, k])
            mix[at] = (mix[at].astype(F32) + t1[tmp].astype(F32)).astype(BF16)
            send(cls, shift, half, buf, k + 4, delta)
    for_pair(0)
    for_self(0)
    first_axis = len(sent)
    for cls, order in enumerate(ORDERS):
        a1, a2, a3 = order
        n = WIDTHS[cls]
        for half, ks in ((0, (4, 3)), (1, (2, 5))):
            tmp = temp(cls, halves[half])
            landed(ul1.at[tmp], sum_r.at[cls, 0, ks[0]])
            landed(ur1.at[tmp], sum_r.at[cls, 0, ks[1]])
        for d in (2, 1, 3, 0):
            where = (pos[a2] + d) % 4
            spec = spec_of(order, (whole, where, pos[a3]))
            at = (cls, spec[0], spec[1], spec[2], slice(None), pl.ds(0, n))
            first, then = (whole, where) if a1 < a2 else (where, whole)
            tmp = (cls, first, then, slice(None), pl.ds(0, n))
            total = mix[at].astype(F32) + ul1[tmp].astype(F32) + ur1[tmp].astype(F32)
            mix[at] = total.astype(BF16)
            if d:
                dst = t2.at[cls, d - 1, :, :, pl.ds(0, n)]
                remote(mix.at[at], dst, sum_s.at[cls, 1, d], sum_r.at[cls, 1, d], along(a2, d))
    for cls, order in enumerate(ORDERS):
        a1, a2, a3 = order
        n = WIDTHS[cls]
        for d in (1, 3, 2):
            landed(t2.at[cls, d - 1, :, :, pl.ds(0, n)], sum_r.at[cls, 1, d])
        for d in (2, 1, 3, 0):
            where = (pos[a1] + d) % 4
            coords = list(pos)
            coords[a1] = where
            at = (cls, coords[0], coords[1], coords[2], slice(None), pl.ds(0, n))
            total = mix[at].astype(F32)
            for k in range(3):
                total = total + t2[cls, k, where, :, 0:n].astype(F32)
            mix[at] = total.astype(BF16)
            if d:
                dst = last.at[cls, d - 1, :, pl.ds(0, n)]
                remote(mix.at[at], dst, sum_s.at[cls, 2, d], sum_r.at[cls, 2, d], along(a1, d))
    settle(first_axis)
    for cls in range(3):
        n = WIDTHS[cls]
        total = mix[cls, pos[0], pos[1], pos[2], :, 0:n].astype(F32)
        for d in (1, 2, 3):
            landed(last.at[cls, d - 1, :, pl.ds(0, n)], sum_r.at[cls, 2, d])
            total = total + last[cls, d - 1, :, 0:n].astype(F32)
        total = total + hidden[:, cls * PART : cls * PART + n]
        fin_out[0, :, cls * PART : cls * PART + n] = total[0:8]
        fin_out[1, :, cls * PART : cls * PART + n] = total[8:16]
    remote(fin_out.at[other], fin_in, pair_s.at[3], pair_r.at[3], sibling)
    for s in range(2):
        out_ref[s, :, half_cols] = fin_out[core, s * 4 : s * 4 + 4]
    settle()
    landed(fin_in, pair_r.at[3])
    for s in range(2):
        cols = pl.ds(pl.multiple_of(other * HALF, 128), HALF)
        out_ref[s, :, cols] = fin_in[s * 4 : s * 4 + 4]


def layer(attended, residual, routes, gain, router, w_uv, w_out, w_gate, w_up, w_down):
    vmem = pl.BlockSpec(memory_space=pltpu.VMEM)
    hbm = pl.BlockSpec(memory_space=pl.ANY)
    dma = pltpu.SemaphoreType.DMA
    grid = (3, 4, 4, 4, 16, PART)
    return pl.pallas_call(
        layer_kernel,
        out_shape=jax.ShapeDtypeStruct((2, 4, 2 * HALF), F32),
        in_specs=[hbm] * 10,
        out_specs=vmem,
        scratch_shapes=[
            pltpu.VMEM(residual.shape, BF16),
            pltpu.VMEM(routes.shape, jnp.int32),
            pltpu.VMEM(gain.shape, F32),
            pltpu.VMEM(router.shape, F32),
            pltpu.VMEM((2, 8, HALF), F32),
            pltpu.VMEM((8, 128), F32),
            pltpu.VMEM((8, 64, LATENT), BF16),
            pltpu.VMEM((512, 1024), BF16),
            pltpu.VMEM((2, 4, 16, HALF), BF16),
            pltpu.VMEM((4, 16, HALF), BF16),
            pltpu.VMEM((3, 16, HALF), BF16),
            pltpu.VMEM((16, HALF), F32),
            pltpu.VMEM((16, 128), F32),
            pltpu.VMEM((2, 16, 128), F32),
            pltpu.VMEM((2, 16, 128), F32),
            pltpu.VMEM((16, HALF), F32),
            pltpu.VMEM((2,) + grid, BF16),
            pltpu.VMEM(w_uv.shape, BF16),
            pltpu.VMEM(w_out.shape, BF16),
            pltpu.VMEM(w_gate.shape, BF16),
            pltpu.VMEM(w_up.shape, BF16),
            pltpu.VMEM(w_down.shape, BF16),
            pltpu.VMEM((2, 4, 4, 4, 16, 256), F32),
            pltpu.VMEM((4, 4, 4, 16, 256), BF16),
            pltpu.VMEM(grid, BF16),
            pltpu.VMEM(grid, BF16),
            pltpu.VMEM(grid, BF16),
            pltpu.VMEM((3, 4, 4, 16, PART), BF16),
            pltpu.VMEM((3, 4, 4, 16, PART), BF16),
            pltpu.VMEM((3, 4, 4, 16, PART), BF16),
            pltpu.VMEM((3, 3, 4, 16, PART), BF16),
            pltpu.VMEM((3, 3, 16, PART), BF16),
            pltpu.VMEM((2, 8, HALF), F32),
            pltpu.VMEM((8, HALF), F32),
            dma((5,)), dma((5,)), dma((8,)), dma((8,)), dma((4,)), dma((4,)), dma((4,)), dma((4,)),
            dma((3, 4)), dma((3, 4)), dma((3, 4, 4)), dma((3, 4)), dma((3, 4, 4)), dma((3, 4, 4)),
            dma((3, 4)), dma((3, 4)), dma((3, 4)), dma((3, 4)),
            dma((3, 3, 6)), dma((3, 3, 6)),
        ],
        compiler_params=pltpu.CompilerParams(
            collective_id=1, has_side_effects=True, vmem_limit_bytes=56 * 2**20
        ),
        name="layer",
    )(attended, residual, routes, gain, router, w_uv, w_out, w_gate, w_up, w_down)


def shards(
    cache_pool,
    page_table,
    page_counts,
    queries,
    new_latent,
    residual,
    w_uv,
    w_out,
    norm_gain,
    w_router,
    w_gate,
    w_up,
    w_down,
    routes,
):
    table = page_table.T
    incoming = exchange(table, jnp.transpose(cache_pool, (1, 2, 0))).reshape(-1, 3, 96, 128)
    attended = attend(table, page_counts, queries, new_latent, incoming)
    out = layer(
        attended, residual, routes, norm_gain, w_router.T, w_uv, w_out, w_gate, w_up, w_down
    )
    return out.astype(BF16)


def solution(mesh):
    return jax.shard_map(
        shards,
        mesh=mesh,
        in_specs=(
            P(("dp", "ep"), None, None),
            P(),
            P(("dp", "ep"), None),
            P(None, ("dp", "ep"), None, None),
            P(None, ("dp", "ep"), None),
            P(None, ("dp", "ep"), None),
            P("ep", None, None),
            P("ep", None),
            P(),
            P(),
            P("dp", None, "ep"),
            P("dp", None, "ep"),
            P("dp", "ep", None),
            P(None, ("dp", "ep"), None),
        ),
        out_specs=P(None, ("dp", "ep"), None),
        check_vma=False,
    )
```

```python
import functools

import jax
import jax.numpy as jnp
from jax import lax
from jax.experimental import pallas as pl
from jax.experimental.pallas import tpu as pltpu
from jax.sharding import PartitionSpec as P

MESH = pl.DeviceIdType.MESH
F32 = jnp.float32
BF16 = jnp.bfloat16

LATENT = 512
ROPE = 64
PAGE = 64
TILE = 16
score_scale = 192.0 ** (-0.5)
route_scale = 2.5
norm_eps = 1e-06

HALF = 1792
PART = 640
ORDERS = ((0, 1, 2), (1, 2, 0), (2, 0, 1))
WIDTHS = (640, 640, 512)


def exchange_kernel(
    table, pool, out,
    table_v, pool_v, slots, held1, held2, stage,
    psem, lsem, send1, recv1, send2, recv2, send3, recv3,
):
    dp = lax.axis_index("dp")
    ep = lax.axis_index("ep")
    pos = (dp // 4, dp % 4, ep // 2)
    core = ep % 2
    other = 1 - core
    whole = pl.ds(0, 4)

    loads = [
        pltpu.make_async_copy(
            pool.at[pl.ds(i * 16, 16)], pool_v.at[pl.ds(i * 16, 16)], psem.at[i]
        )
        for i in range(4)
    ]
    table_load = pltpu.make_async_copy(table, table_v, psem.at[4])
    table_load.start()
    for load in loads:
        load.start()

    def along(axis, delta, c):
        coords = list(pos)
        coords[axis] = (coords[axis] + delta) % 4
        return (coords[0] * 4 + coords[1], coords[2] * 2 + c)

    def spec_of(order, values):
        spec = [None, None, None]
        for axis, value in zip(order, values):
            spec[axis] = value
        return tuple(spec)

    barrier = pltpu.get_barrier_semaphore()
    peers = [along(a, d, c) for a in range(3) for d in (1, 2, 3) for c in (core, other)]
    peers.append(along(0, 0, other))
    for peer in peers:
        pl.semaphore_signal(barrier, inc=1, device_id=peer, device_id_type=MESH)

    table_load.wait()
    pages = table_v[...]
    wanted = jnp.where(pages // 128 == dp * 8 + ep, pages % 128, 0)
    wanted = jnp.sum(wanted, axis=0, keepdims=True)
    page = lax.broadcasted_iota(jnp.int32, (128, 128), 0)
    onehot = jnp.transpose(jnp.where(wanted == page, 1.0, 0.0)).astype(BF16)

    def put(cls, row, pieces):
        for j in range(0, 16, 4):
            x = jnp.concatenate(pieces(j), axis=0)
            y = lax.dot_general(onehot, x, (((1,), (1,)), ((), ())), preferred_element_type=F32)
            for i in range(4):
                stage[:, j + i, :] = y[:, i * 128 : (i + 1) * 128]
        block = stage[...].astype(BF16).reshape(4, 4, 4, 2, 16, 128)
        slots[cls, :, :, :, :, row : row + 16, :] = block

    def latent_rows(cls, chunk, unit, row):
        def pieces(j):
            t = unit * 16 + j
            return [pool_v[pl.ds(t, 4), chunk * 128 : (chunk + 1) * 128, :].reshape(512, 128)]

        put(cls, row, pieces)

    def rope_rows(cls, unit, row):
        def pieces(j):
            found = []
            for i in range(4):
                found.append(pool_v[unit * 16 + j + i, 512:576, :])
                found.append(pool_v[32 + unit * 16 + j + i, 512:576, :])
            return found

        put(cls, row, pieces)

    def remote(src, dst, ssem, rsem, peer):
        pltpu.make_async_remote_copy(
            src_ref=src, dst_ref=dst, send_sem=ssem, recv_sem=rsem,
            device_id=peer, device_id_type=MESH,
        ).start()

    def landed(ref, sem):
        pltpu.make_async_copy(ref, ref, sem).wait()

    for part in range(6):
        rows = pl.ds(part * 16, 16)
        if part < 4:
            loads[part].wait()
        for cls, order in enumerate(ORDERS):
            a1, a2, a3 = order
            if part < 4:
                latent_rows(cls, cls, part, 16 * part)
            elif cls < 2:
                latent_rows(cls, 3, 2 * cls + part - 4, 16 * part)
            else:
                rope_rows(cls, part - 4, 16 * part)
            if part == 0 and cls == 0:
                pl.semaphore_wait(barrier, len(peers))
            for d in (2, 1, 3):
                src = spec_of(order, ((pos[a1] + d) % 4, whole, whole))
                dst = spec_of(order, (pos[a1], whole, whole))
                remote(
                    slots.at[(cls,) + src + (pl.ds(0, 2), rows)],
                    held1.at[(cls,) + dst + (pl.ds(0, 2), rows)],
                    send1.at[cls], recv1.at[cls, d], along(a1, d, core),
                )
            if part == 5:
                own = (cls,) + spec_of(order, (pos[a1], whole, whole))
                pltpu.make_async_copy(slots.at[own], held1.at[own], lsem.at[cls]).start()

    def second(cls, buf, e):
        a1, a2, a3 = order = ORDERS[cls]
        src1 = (pos[a1] + 4 - e) % 4
        for d in (2, 1, 3):
            src = spec_of(order, (src1, (pos[a2] + d) % 4, whole))
            dst = spec_of(order, (src1, pos[a2], whole))
            remote(
                buf.at[(cls,) + src], held2.at[(cls,) + dst],
                send2.at[cls], recv2.at[cls, d], along(a2, d, core),
            )

    def third(cls, buf, f):
        a1, a2, a3 = order = ORDERS[cls]
        src2 = (pos[a2] + 4 - f) % 4
        for d in (2, 1, 3, 0):
            for k, c in ((0, core), (1, other)):
                src = spec_of(order, (whole, src2, (pos[a3] + d) % 4))
                dst = spec_of(order, (whole, src2, pos[a3]))
                a = buf.at[(cls,) + src + (c,)]
                b = out.at[dst + (core, cls)]
                if d == 0 and k == 0:
                    pltpu.make_async_copy(a, b, recv3.at[cls]).start()
                else:
                    remote(a, b, send3.at[cls, d], recv3.at[cls], along(a3, d, c))

    for cls in range(3):
        second(cls, slots, 0)
    for e in (1, 3, 2):
        for cls, order in enumerate(ORDERS):
            src1 = (pos[order[0]] + 4 - e) % 4
            landed(held1.at[(cls,) + spec_of(order, (src1, whole, whole))], recv1.at[cls, e])
            second(cls, held1, e)
    for cls, order in enumerate(ORDERS):
        own = spec_of(order, (pos[order[0]], whole, whole))
        landed(held1.at[(cls,) + own], lsem.at[cls])
        third(cls, held1, 0)
    for f in (1, 3, 2):
        for cls, order in enumerate(ORDERS):
            a1, a2, a3 = order
            at = spec_of(order, (whole, (pos[a2] + 4 - f) % 4, whole))
            landed(held2.at[(cls,) + at], recv2.at[cls, f])
            third(cls, held2, f)
    for cls in range(3):
        most = held1.at[cls, pl.ds(0, 3)]
        landed(most, send1.at[cls])
        landed(most, send2.at[cls])
    for cls in range(3):
        landed(held1.at[cls, 0, pl.ds(0, 2)], send3.at[cls, 0])
        for d in (1, 2, 3):
            landed(held1.at[cls, 0], send3.at[cls, d])
    for cls in range(3):
        landed(out.at[:, :, :, :, cls], recv3.at[cls])


def exchange(table, pool):
    hbm = pl.BlockSpec(memory_space=pl.ANY)
    dma = pltpu.SemaphoreType.DMA
    held = (3, 4, 4, 4, 2, 96, 128)
    return pl.pallas_call(
        exchange_kernel,
        out_shape=jax.ShapeDtypeStruct((4, 4, 4, 2, 3, 96, 128), BF16),
        in_specs=[hbm, hbm],
        out_specs=hbm,
        scratch_shapes=[
            pltpu.VMEM(table.shape, jnp.int32),
            pltpu.VMEM(pool.shape, BF16),
            pltpu.VMEM(held, BF16),
            pltpu.VMEM(held, BF16),
            pltpu.VMEM(held, BF16),
            pltpu.VMEM((128, 16, 128), F32),
            dma((5,)), dma((3,)), dma((3,)), dma((3, 4)), dma((3,)), dma((3, 4)), dma((3, 4)), dma((3,)),
        ],
        compiler_params=pltpu.CompilerParams(
            collective_id=2, has_side_effects=True, vmem_limit_bytes=56 * 2**20
        ),
        name="exchange",
    )(table, pool)


def attend_kernel(
    table, counts, queries, new, slots, out_ref, q_ref, new_ref, own_ref, keys, scores, sem, in_sem
):
    pages = 64
    me = lax.axis_index("dp") * 8 + lax.axis_index("ep")

    loads = [
        pltpu.make_async_copy(queries, q_ref, in_sem.at[0]),
        pltpu.make_async_copy(new, new_ref, in_sem.at[1]),
    ]
    for load in loads:
        load.start()

    def page_copy(j):
        return pltpu.make_async_copy(slots.at[table[j, me] // 128], keys.at[j], sem.at[j])

    def fetch(j, _):
        page_copy(j).start()
        return 0

    lax.fori_loop(0, pages, fetch, 0)

    def clear(j, _):
        keys[pages + j] = jnp.zeros((3, 96, 128), BF16)
        return 0

    lax.fori_loop(0, TILE, clear, 0)
    own_ref[...] = jnp.zeros_like(own_ref)
    loads[1].wait()
    for step in range(2):
        fresh = new_ref[step].astype(F32)
        for r in range(4):
            own_ref[r, step : step + 1, :] = fresh[r : r + 1]
    loads[0].wait()
    width = TILE * PAGE
    step_of = lax.broadcasted_iota(jnp.int32, (16, 128), 1) // 64
    token = lax.broadcasted_iota(jnp.int32, (16, 128), 0)
    low = lax.broadcasted_iota(jnp.int32, (TILE, 32, 128), 2) < ROPE

    def values_of(page):
        parts = [keys[pl.ds(page, TILE), k, 0:64, :].reshape(width, 128) for k in range(3)]
        parts.append(keys[pl.ds(page, TILE), 0:2, 64:96, :].reshape(width, 128))
        return jnp.concatenate(parts, axis=1)

    def arrive(j, _):
        pltpu.make_async_copy(keys.at[j], keys.at[j], sem.at[j]).wait()
        return 0

    def request(r, carry):
        start, seen = carry
        q = jnp.concatenate([q_ref[0, r], q_ref[1, r]], axis=0)
        own = own_ref[r].astype(BF16)
        s_own = lax.dot_general(own, q, (((1,), (1,)), ((), ())), preferred_element_type=F32)
        s_own = jnp.where(token <= step_of, s_own * score_scale, -jnp.inf)
        q_rope = q[:, LATENT:]
        q_wide = jnp.concatenate([q[:, :LATENT], q_rope, q_rope], axis=1)
        q_turned = jnp.transpose(q_wide)
        length = counts[0, r] * PAGE
        tiles = (length + width - 1) // width
        needed = jnp.minimum(start + tiles * TILE, pages)
        lax.fori_loop(seen, needed, arrive, 0)

        def score(t, top):
            page = start + t * TILE
            rope = keys[pl.ds(page, TILE), 2, 64:96, :]
            zero = jnp.zeros_like(rope)
            pair = jnp.concatenate([jnp.where(low, rope, zero), jnp.where(low, zero, rope)], axis=1)
            key = jnp.concatenate([values_of(page), pair.reshape(width, 128)], axis=1)
            s = jnp.dot(key, q_turned, preferred_element_type=F32)
            place = t * width + lax.broadcasted_iota(jnp.int32, (width, 128), 0)
            s = jnp.where(place < length, s * score_scale, -jnp.inf)
            scores[t] = s
            return jnp.maximum(top, jnp.max(s, axis=0, keepdims=True))

        top = lax.fori_loop(0, tiles, score, jnp.max(s_own, axis=0, keepdims=True))
        p_own = jnp.exp(s_own - top)
        total = jnp.sum(p_own, axis=0, keepdims=True)

        def weigh(p, values):
            turned = jnp.transpose(p).astype(BF16)
            return jnp.dot(turned, values, preferred_element_type=F32)

        acc = weigh(p_own, own[:, :LATENT])

        def mix(t, carry):
            total, acc = carry
            p = jnp.exp(scores[t] - top)
            total = total + jnp.sum(p, axis=0, keepdims=True)
            acc = acc + weigh(p, values_of(start + t * TILE))
            return total, acc

        total, acc = lax.fori_loop(0, tiles, mix, (total, acc))
        scale = jnp.transpose(jnp.broadcast_to(1.0 / total, (128, 128)))[:, 0:1]
        res = (acc * scale).reshape(2, 8, 8, LATENT)
        at = pl.multiple_of(r * 16, 16)
        for g in range(8):
            block = jnp.concatenate([res[0, g], res[1, g]], axis=0)
            out_ref[g, pl.ds(at, 16), :] = block.astype(BF16)
        return start + counts[0, r], jnp.maximum(seen, needed)

    lax.fori_loop(0, 4, request, (jnp.int32(0), jnp.int32(0)), unroll=True)


def attend(table, counts, queries, new_latent, slots):
    smem = pl.BlockSpec(memory_space=pltpu.SMEM)
    vmem = pl.BlockSpec(memory_space=pltpu.VMEM)
    return pl.pallas_call(
        attend_kernel,
        out_shape=jax.ShapeDtypeStruct((8, 64, LATENT), BF16),
        in_specs=[smem, smem] + [pl.BlockSpec(memory_space=pl.ANY)] * 3,
        out_specs=vmem,
        scratch_shapes=[
            pltpu.VMEM(queries.shape, BF16),
            pltpu.VMEM(new_latent.shape, BF16),
            pltpu.VMEM((4, 16, LATENT + ROPE), F32),
            pltpu.VMEM((64 + TILE, 3, 96, 128), BF16),
            pltpu.VMEM((32 // TILE, TILE * PAGE, 128), F32),
            pltpu.SemaphoreType.DMA((64,)),
            pltpu.SemaphoreType.DMA((2,)),
        ],
        compiler_params=pltpu.CompilerParams(vmem_limit_bytes=60 * 2**20),
        name="attend",
    )(table, counts, queries, new_latent, slots)


def layer_kernel(
    attended, residual_in, routes_in, gain_in, router_in, w_uv, w_out, w_gate, w_up, w_down,
    out_ref,
    residual, routes, gain, router, resid, member, heads_in, masked, part_out, part_pair, part_in, res_all, mem_all, stat_out, stat_in, hidden,
    gath, v_uv, v_out, v_gate, v_up, v_down, acc, inner,
    mix, sib_out, sib_in, t1, ul1, ur1, t2, last, fin_out, fin_in,
    wsem, lsem, head_s, head_r, part_s, part_r, pair_s, pair_r,
    ag1_s, ag1_r, ag2_s, ag2_r, ag3_s, ag3_r, sib_s, sib_r, red_s, red_r, sum_s, sum_r,
):
    dp = lax.axis_index("dp")
    ep = lax.axis_index("ep")
    pos = (dp // 4, dp % 4, ep // 2)
    core = ep % 2
    other = 1 - core

    def device(coords, c):
        return (coords[0] * 4 + coords[1], coords[2] * 2 + c)

    def along(axis, delta):
        coords = [pos[0], pos[1], pos[2]]
        coords[axis] = (coords[axis] + delta) % 4
        return device(coords, core)

    sibling = device(pos, other)
    ep_peers = [(dp, (ep + o) % 8) for o in range(1, 8)]
    ring_peers = [along(a, d) for a in (0, 1) for d in (1, 2, 3)]

    def remote(src, dst, ssem, rsem, peer):
        copy = pltpu.make_async_remote_copy(
            src_ref=src, dst_ref=dst, send_sem=ssem, recv_sem=rsem,
            device_id=peer, device_id_type=MESH,
        )
        copy.start()
        sent.append((src, ssem))

    def landed(ref, rsem):
        pltpu.make_async_copy(ref, ref, rsem).wait()

    sent = []

    def settle(count=None):
        for src, ssem in sent[:count]:
            pltpu.make_async_copy(src, src, ssem).wait()
        del sent[:count]

    barrier = pltpu.get_barrier_semaphore()
    for peer in ep_peers + ring_peers:
        pl.semaphore_signal(barrier, inc=1, device_id=peer, device_id_type=MESH)

    loads = [(residual_in, residual), (routes_in, routes), (gain_in, gain), (router_in, router)]
    small = [pltpu.make_async_copy(a, b, lsem.at[1 + i]) for i, (a, b) in enumerate(loads)]
    loads = [(w_uv, v_uv), (w_out, v_out), (w_gate, v_gate), (w_up, v_up), (w_down, v_down)]
    copies = [pltpu.make_async_copy(a, b, wsem.at[i]) for i, (a, b) in enumerate(loads)]
    for copy in small + copies:
        copy.start()
    pl.semaphore_wait(barrier, len(ep_peers) + len(ring_peers))

    for o in (4, 3, 5, 2, 6, 7, 1):
        to = (ep + o) % 8
        remote(attended.at[to], heads_in.at[ep], head_s.at[o], head_r.at[o], (dp, to))
    own_heads = pltpu.make_async_copy(attended.at[ep], heads_in.at[ep], lsem.at[0])
    own_heads.start()

    for copy in small:
        copy.wait()
    for h in range(2):
        cols = slice(h * HALF, (h + 1) * HALF)
        both = [residual[s, :, cols].astype(F32) for s in range(2)]
        resid[h] = jnp.concatenate(both, axis=0)
    route = jnp.concatenate([routes[0], routes[1]], axis=0)
    lanes = lax.broadcasted_iota(jnp.int32, (8, 128), 1)
    named = jnp.zeros((8, 128), F32)
    for k in range(8):
        named = jnp.where(route[:, k : k + 1] == lanes, 1.0, named)
    member[...] = named
    own_rows = pl.ds(pl.multiple_of(core * 8, 8), 8)
    other_rows = pl.ds(pl.multiple_of(other * 8, 8), 8)
    remote(resid.at[other], res_all.at[own_rows], pair_s.at[0], pair_r.at[0], sibling)
    remote(member, mem_all.at[own_rows], pair_s.at[1], pair_r.at[1], sibling)
    res_all[own_rows, :] = resid[core]
    mem_all[own_rows, :] = member[...]

    def clear(i, _):
        acc[0, i] = jnp.zeros((4, 4, 16, 256), F32)
        acc[1, i] = jnp.zeros((4, 4, 16, 256), F32)
        return 0

    lax.fori_loop(0, 4, clear, 0)
    own_heads.wait()
    for o in range(1, 8):
        landed(heads_in.at[(ep + 8 - o) % 8], head_r.at[o])

    copies[0].wait()
    x = heads_in[...].reshape(512, LATENT)
    row_head = lax.broadcasted_iota(jnp.int32, (512, 128), 0) % 8
    for h in range(8):
        y = jnp.dot(x, v_uv[h], preferred_element_type=F32)
        masked[:, h * 128 : (h + 1) * 128] = jnp.where(row_head == h, y, 0.0).astype(BF16)
    to_row = lax.broadcasted_iota(jnp.int32, (64, 512), 0)
    from_row = lax.broadcasted_iota(jnp.int32, (64, 512), 1) // 8
    wanted = (to_row // 8) * 8 + (to_row % 4) * 2 + (to_row % 8) // 4
    pick = jnp.where(from_row == wanted, 1.0, 0.0).astype(BF16)
    flat = jnp.dot(pick, masked[...], preferred_element_type=F32).astype(BF16)

    copies[1].wait()
    for k, h in ((0, other), (1, core)):
        for t in range(HALF // 256):
            cols = pl.ds(pl.multiple_of(h * HALF + t * 256, 256), 256)
            y = jnp.dot(flat, v_out[:, cols], preferred_element_type=F32)
            part_out[k, :, :, t * 256 : (t + 1) * 256] = y.astype(BF16).reshape(4, 16, 256)
        if k == 0:
            remote(part_out.at[0], part_pair, part_s.at[0], part_r.at[0], sibling)
    landed(part_pair, part_r.at[0])
    for d in (2, 1, 3, 0):
        to = (pos[2] + d) % 4
        both = part_out[1, to].astype(F32) + part_pair[to].astype(F32)
        part_out[1, to] = both.astype(BF16)
        if d:
            remote(
                part_out.at[1, to], part_in.at[d - 1], part_s.at[d], part_r.at[d], along(2, d)
            )
    landed(res_all.at[other_rows], pair_r.at[0])
    landed(mem_all.at[other_rows], pair_r.at[1])
    hid = part_out[1, pos[2]].astype(F32)
    settle()
    for d in (1, 3, 2):
        landed(part_in.at[d - 1], part_r.at[d])
        hid = hid + part_in[d - 1].astype(F32)
    hid = hid + res_all[...]
    hidden[...] = hid

    half_cols = pl.ds(pl.multiple_of(core * HALF, 128), HALF)
    scaled = hid * gain[half_cols].reshape(1, HALF)
    stat_out[0] = jnp.zeros((16, 128), F32)
    stat_out[0, :, 0:16] = lax.dot_general(
        scaled, router[:, half_cols], (((1,), (1,)), ((), ())),
        preferred_element_type=F32, precision=lax.Precision.HIGHEST,
    )
    stat_out[1] = jnp.broadcast_to(jnp.sum(hid * hid, axis=1, keepdims=True), (16, 128))
    remote(stat_out, stat_in, pair_s.at[2], pair_r.at[2], sibling)
    landed(stat_in, pair_r.at[2])
    square = stat_out[1] + stat_in[1]
    inv = lax.rsqrt(square / (2 * HALF) + norm_eps)
    affinity = jax.nn.sigmoid((stat_out[0] + stat_in[0]) * inv) * mem_all[...]
    gates = route_scale * affinity / jnp.sum(affinity, axis=1, keepdims=True)
    coarse = gates.astype(BF16)
    fine = (gates - coarse.astype(F32)).astype(BF16)
    normed = (scaled * inv[:, 0:1]).astype(BF16)
    z, xx, yy = pos
    gath[core, 0, z, xx, yy] = normed[:, 0:640]
    gath[core, 1, z, xx, yy] = normed[:, 640:1280]
    gath[core, 2, z, xx, yy, :, 0:512] = normed[:, 1280:1792]
    gath[core, 2, z, xx, yy, :, 512:640] = jnp.where(core == 0, coarse, fine)

    whole = pl.ds(0, 4)
    halves = (pl.ds(0, 2), pl.ds(2, 2))

    def g_at(cls, spec):
        return gath.at[core, cls, spec[0], spec[1], spec[2]]

    def spec_of(order, values):
        spec = [None, None, None]
        for axis, value in zip(order, values):
            spec[axis] = value
        return spec

    def line(cls, e, f):
        a1, a2, a3 = ORDERS[cls]
        where = spec_of((a1, a2, a3), ((pos[a1] + 4 - e) % 4, (pos[a2] + 4 - f) % 4, pos[a3]))
        return g_at(cls, where)

    def quarter(cls, f, shift, half=whole):
        a1, a2, a3 = ORDERS[cls]
        at = (half, (pos[a2] + 4 - f) % 4, (pos[a3] + shift) % 4)
        return g_at(cls, spec_of((a1, a2, a3), at))

    def plane_at(cls, shift):
        a1, a2, a3 = ORDERS[cls]
        return tuple(spec_of((a1, a2, a3), (whole, whole, (pos[a3] + shift) % 4)))

    def to_pair(cls, k, shift):
        plane = gath.at[(core, cls) + plane_at(cls, shift)]
        remote(plane, plane, sib_s.at[cls, k], sib_r.at[cls, k], sibling)

    def second(cls, e):
        b = line(cls, e, 0)
        for d in (1, 3, 2):
            remote(b, b, ag2_s.at[cls, d, e], ag2_r.at[cls, d], along(ORDERS[cls][1], d))

    def third(cls, f):
        b = quarter(cls, f, 0)
        for k, d in ((0, 1), (1, 3)):
            remote(b, b, ag3_s.at[cls, f, k], ag3_r.at[cls, f, k], along(ORDERS[cls][2], d))

    for cls, order in enumerate(ORDERS):
        own = g_at(cls, pos)
        for d in (1, 3, 2):
            remote(own, own, ag1_s.at[cls, d], ag1_r.at[cls, d], along(order[0], d))
    for cls in range(3):
        second(cls, 0)
    for e in (1, 3, 2):
        for cls in range(3):
            landed(line(cls, e, 0), ag1_r.at[cls, e])
            second(cls, e)
    for cls in range(3):
        third(cls, 0)
    for f in (1, 3, 2):
        for cls in range(3):
            landed(quarter(cls, f, 0), ag2_r.at[cls, f])
            third(cls, f)
    for cls in range(3):
        to_pair(cls, 0, 0)
    for copy in copies[2:]:
        copy.wait()

    def expert_in(h, cls, shift):
        at = plane_at(cls, shift)
        n = WIDTHS[cls]
        x = gath[(h, cls) + at].reshape(256, PART)[:, :n]
        rows = pl.ds(pl.multiple_of(h * HALF + cls * PART, 128), n)
        for k, w in enumerate((v_gate, v_up)):
            y = jnp.dot(x, w[0, rows, :], preferred_element_type=F32).reshape(4, 4, 16, 256)
            acc[(k,) + at] = acc[(k,) + at] + y

    def from_pair(cls, k, shift):
        landed(gath.at[(other, cls) + plane_at(cls, shift)], sib_r.at[cls, k])

    for f in (0, 1, 3, 2):
        for cls, order in enumerate(ORDERS):
            landed(quarter(cls, f, 3), ag3_r.at[cls, f, 0])
            b = quarter(cls, f, 3, halves[0])
            remote(b, b, ag3_s.at[cls, f, 2], ag3_r.at[cls, f, 2], along(order[2], 1))
            landed(quarter(cls, f, 1), ag3_r.at[cls, f, 1])
            b = quarter(cls, f, 1, halves[1])
            remote(b, b, ag3_s.at[cls, f, 3], ag3_r.at[cls, f, 3], along(order[2], 3))
        if f == 1:
            for cls in range(3):
                expert_in(core, cls, 0)
        if f == 3:
            for cls in range(3):
                from_pair(cls, 0, 0)
                expert_in(other, cls, 0)
    for k, shift in ((1, 3), (2, 1)):
        for cls in range(3):
            to_pair(cls, k, shift)

    for k, shift in ((1, 3), (2, 1)):
        for cls in range(3):
            expert_in(core, cls, shift)
    for k, shift in ((1, 3), (2, 1)):
        for cls in range(3):
            from_pair(cls, k, shift)
            expert_in(other, cls, shift)
    for cls in range(3):
        for f in range(4):
            landed(quarter(cls, f, 2, halves[0]), ag3_r.at[cls, f, 2])
            landed(quarter(cls, f, 2, halves[1]), ag3_r.at[cls, f, 3])
        to_pair(cls, 3, 2)
    for cls in range(3):
        expert_in(core, cls, 2)
    for cls in range(3):
        from_pair(cls, 3, 2)
        expert_in(other, cls, 2)

    lane = lax.broadcasted_iota(jnp.int32, (256, 128), 1)

    def activate(i, _):
        both = gath[0, 2, i, :, :, :, 512:640].astype(F32) + gath[1, 2, i, :, :, :, 512:640].astype(F32)
        weight = jnp.sum(jnp.where(lane == dp, both.reshape(256, 128), 0.0), axis=1, keepdims=True)
        gate = acc[0, i].reshape(256, 256)
        act = gate / (1.0 + jnp.exp(-gate)) * acc[1, i].reshape(256, 256) * weight
        inner[i] = act.astype(BF16).reshape(4, 4, 16, 256)
        return 0

    lax.fori_loop(0, 4, activate, 0)

    def expert_out(half, cls, at):
        cols = pl.ds(pl.multiple_of(half * HALF + cls * PART, 128), WIDTHS[cls])
        act = inner[at].reshape(256, 256)
        y = jnp.dot(act, v_down[0, :, cols], preferred_element_type=F32)
        return y.reshape(4, 4, 16, WIDTHS[cls])

    def for_pair(shift):
        for cls in range(3):
            at = plane_at(cls, shift)
            b = (cls,) + at + (slice(None), pl.ds(0, WIDTHS[cls]))
            sib_out[b] = expert_out(other, cls, at).astype(BF16)
            remote(sib_out.at[b], sib_in.at[b], red_s.at[cls, shift], red_r.at[cls, shift], sibling)

    def for_self(shift):
        for cls in range(3):
            at = plane_at(cls, shift)
            b = (cls,) + at + (slice(None), pl.ds(0, WIDTHS[cls]))
            y = expert_out(core, cls, at)
            landed(sib_in.at[b], red_r.at[cls, shift])
            mix[b] = (y + sib_in[b].astype(F32)).astype(BF16)

    def block(cls, shift, half):
        a1, a2, a3 = ORDERS[cls]
        spec = spec_of((a1, a2, a3), (half, whole, (pos[a3] + shift) % 4))
        return (cls, spec[0], spec[1], spec[2], slice(None), pl.ds(0, WIDTHS[cls]))

    def temp(cls, half):
        a1, a2, a3 = ORDERS[cls]
        first, then = (half, whole) if a1 < a2 else (whole, half)
        return (cls, first, then, slice(None), pl.ds(0, WIDTHS[cls]))

    def send(cls, shift, half, buf, k, delta):
        remote(
            mix.at[block(cls, shift, halves[half])], buf.at[temp(cls, halves[half])],
            sum_s.at[cls, 0, k], sum_r.at[cls, 0, k], along(ORDERS[cls][2], delta),
        )

    gathered = len(sent)
    for_pair(2)
    for_pair(1)
    for_self(2)
    for cls in range(3):
        send(cls, 2, 0, t1, 0, 1)
        send(cls, 2, 1, t1, 1, 3)
    for_pair(3)
    for_self(1)
    for cls in range(3):
        send(cls, 1, 1, ul1, 2, 1)
    for_self(3)
    for cls in range(3):
        send(cls, 3, 0, ur1, 3, 3)
    settle(gathered)
    for cls in range(3):
        for half, shift, buf, k, delta in ((0, 1, ul1, 0, 1), (1, 3, ur1, 1, 3)):
            at, tmp = block(cls, shift, halves[half]), temp(cls, halves[half])
            landed(t1.at[tmp], sum_r.at[cls, 0, k])
            mix[at] = (mix[at].astype(F32) + t1[tmp].astype(F32)).astype(BF16)
            send(cls, shift, half, buf, k + 4, delta)
    for_pair(0)
    for_self(0)
    first_axis = len(sent)
    for cls, order in enumerate(ORDERS):
        a1, a2, a3 = order
        n = WIDTHS[cls]
        for half, ks in ((0, (4, 3)), (1, (2, 5))):
            tmp = temp(cls, halves[half])
            landed(ul1.at[tmp], sum_r.at[cls, 0, ks[0]])
            landed(ur1.at[tmp], sum_r.at[cls, 0, ks[1]])
        for d in (2, 1, 3, 0):
            where = (pos[a2] + d) % 4
            spec = spec_of(order, (whole, where, pos[a3]))
            at = (cls, spec[0], spec[1], spec[2], slice(None), pl.ds(0, n))
            first, then = (whole, where) if a1 < a2 else (where, whole)
            tmp = (cls, first, then, slice(None), pl.ds(0, n))
            total = mix[at].astype(F32) + ul1[tmp].astype(F32) + ur1[tmp].astype(F32)
            mix[at] = total.astype(BF16)
            if d:
                dst = t2.at[cls, d - 1, :, :, pl.ds(0, n)]
                remote(mix.at[at], dst, sum_s.at[cls, 1, d], sum_r.at[cls, 1, d], along(a2, d))
    for cls, order in enumerate(ORDERS):
        a1, a2, a3 = order
        n = WIDTHS[cls]
        for d in (1, 3, 2):
            landed(t2.at[cls, d - 1, :, :, pl.ds(0, n)], sum_r.at[cls, 1, d])
        for d in (2, 1, 3, 0):
            where = (pos[a1] + d) % 4
            coords = list(pos)
            coords[a1] = where
            at = (cls, coords[0], coords[1], coords[2], slice(None), pl.ds(0, n))
            total = mix[at].astype(F32)
            for k in range(3):
                total = total + t2[cls, k, where, :, 0:n].astype(F32)
            mix[at] = total.astype(BF16)
            if d:
                dst = last.at[cls, d - 1, :, pl.ds(0, n)]
                remote(mix.at[at], dst, sum_s.at[cls, 2, d], sum_r.at[cls, 2, d], along(a1, d))
    settle(first_axis)
    for cls in range(3):
        n = WIDTHS[cls]
        total = mix[cls, pos[0], pos[1], pos[2], :, 0:n].astype(F32)
        for d in (1, 2, 3):
            landed(last.at[cls, d - 1, :, pl.ds(0, n)], sum_r.at[cls, 2, d])
            total = total + last[cls, d - 1, :, 0:n].astype(F32)
        total = total + hidden[:, cls * PART : cls * PART + n]
        fin_out[0, :, cls * PART : cls * PART + n] = total[0:8]
        fin_out[1, :, cls * PART : cls * PART + n] = total[8:16]
    remote(fin_out.at[other], fin_in, pair_s.at[3], pair_r.at[3], sibling)
    for s in range(2):
        out_ref[s, :, half_cols] = fin_out[core, s * 4 : s * 4 + 4]
    settle()
    landed(fin_in, pair_r.at[3])
    for s in range(2):
        cols = pl.ds(pl.multiple_of(other * HALF, 128), HALF)
        out_ref[s, :, cols] = fin_in[s * 4 : s * 4 + 4]


def layer(attended, residual, routes, gain, router, w_uv, w_out, w_gate, w_up, w_down):
    vmem = pl.BlockSpec(memory_space=pltpu.VMEM)
    hbm = pl.BlockSpec(memory_space=pl.ANY)
    dma = pltpu.SemaphoreType.DMA
    grid = (3, 4, 4, 4, 16, PART)
    return pl.pallas_call(
        layer_kernel,
        out_shape=jax.ShapeDtypeStruct((2, 4, 2 * HALF), F32),
        in_specs=[hbm] * 10,
        out_specs=vmem,
        scratch_shapes=[
            pltpu.VMEM(residual.shape, BF16),
            pltpu.VMEM(routes.shape, jnp.int32),
            pltpu.VMEM(gain.shape, F32),
            pltpu.VMEM(router.shape, F32),
            pltpu.VMEM((2, 8, HALF), F32),
            pltpu.VMEM((8, 128), F32),
            pltpu.VMEM((8, 64, LATENT), BF16),
            pltpu.VMEM((512, 1024), BF16),
            pltpu.VMEM((2, 4, 16, HALF), BF16),
            pltpu.VMEM((4, 16, HALF), BF16),
            pltpu.VMEM((3, 16, HALF), BF16),
            pltpu.VMEM((16, HALF), F32),
            pltpu.VMEM((16, 128), F32),
            pltpu.VMEM((2, 16, 128), F32),
            pltpu.VMEM((2, 16, 128), F32),
            pltpu.VMEM((16, HALF), F32),
            pltpu.VMEM((2,) + grid, BF16),
            pltpu.VMEM(w_uv.shape, BF16),
            pltpu.VMEM(w_out.shape, BF16),
            pltpu.VMEM(w_gate.shape, BF16),
            pltpu.VMEM(w_up.shape, BF16),
            pltpu.VMEM(w_down.shape, BF16),
            pltpu.VMEM((2, 4, 4, 4, 16, 256), F32),
            pltpu.VMEM((4, 4, 4, 16, 256), BF16),
            pltpu.VMEM(grid, BF16),
            pltpu.VMEM(grid, BF16),
            pltpu.VMEM(grid, BF16),
            pltpu.VMEM((3, 4, 4, 16, PART), BF16),
            pltpu.VMEM((3, 4, 4, 16, PART), BF16),
            pltpu.VMEM((3, 4, 4, 16, PART), BF16),
            pltpu.VMEM((3, 3, 4, 16, PART), BF16),
            pltpu.VMEM((3, 3, 16, PART), BF16),
            pltpu.VMEM((2, 8, HALF), F32),
            pltpu.VMEM((8, HALF), F32),
            dma((5,)), dma((5,)), dma((8,)), dma((8,)), dma((4,)), dma((4,)), dma((4,)), dma((4,)),
            dma((3, 4)), dma((3, 4)), dma((3, 4, 4)), dma((3, 4)), dma((3, 4, 4)), dma((3, 4, 4)),
            dma((3, 4)), dma((3, 4)), dma((3, 4)), dma((3, 4)),
            dma((3, 3, 6)), dma((3, 3, 6)),
        ],
        compiler_params=pltpu.CompilerParams(
            collective_id=1, has_side_effects=True, vmem_limit_bytes=56 * 2**20
        ),
        name="layer",
    )(attended, residual, routes, gain, router, w_uv, w_out, w_gate, w_up, w_down)


def shards(
    cache_pool,
    page_table,
    page_counts,
    queries,
    new_latent,
    residual,
    w_uv,
    w_out,
    norm_gain,
    w_router,
    w_gate,
    w_up,
    w_down,
    routes,
):
    table = page_table.T
    incoming = exchange(table, jnp.transpose(cache_pool, (1, 2, 0))).reshape(-1, 3, 96, 128)
    attended = attend(table, page_counts, queries, new_latent, incoming)
    out = layer(
        attended, residual, routes, norm_gain, w_router.T, w_uv, w_out, w_gate, w_up, w_down
    )
    return out.astype(BF16)


def solution(mesh):
    return jax.shard_map(
        shards,
        mesh=mesh,
        in_specs=(
            P(("dp", "ep"), None, None),
            P(),
            P(("dp", "ep"), None),
            P(None, ("dp", "ep"), None, None),
            P(None, ("dp", "ep"), None),
            P(None, ("dp", "ep"), None),
            P("ep", None, None),
            P("ep", None),
            P(),
            P(),
            P("dp", None, "ep"),
            P("dp", None, "ep"),
            P("dp", "ep", None),
            P(None, ("dp", "ep"), None),
        ),
        out_specs=P(None, ("dp", "ep"), None),
        check_vma=False,
    )
```
